32 devices in a mesh: dp: 8 (over z, x), seq: 4 (over y, core).
Axes of the slice: x: 2, y: 2, z: 4, core: 2. Of those that a mesh axis runs over, the one named last changes fastest.
Arguments:
- latents: float32 [2, 16, 320, 16], P(None, 'dp', 'seq'), may hold values from -6 to 6
- noise_draw: float32 [2, 16, 320, 16], P(None, 'dp', 'seq'), may hold values from -6 to 6
- heights: int32 [2, 16], P(None, 'dp'), may hold values from 8 to 16, as said below
- widths: int32 [2, 16], P(None, 'dp'), may hold values from 1 to 20, as said below
- labels: int32 [2, 16], P(None, 'dp'), may hold values from 0 to 1000
- timesteps: int32 [2, 16], P(None, 'dp'), may hold values from 0 to 999
- bias_tiles: bfloat16 [2, 16, 16, 320, 320], P(None, 'dp', 'seq'), may hold values from -4 to 4
- param_embed: float32 [272, 1152], P(None, ('dp', 'seq')), may hold values from -0.75 to 0.75
- param_square: float32 [2, 1152, 1152], P(None, None, ('dp', 'seq')), may hold values from -0.375 to 0.375
- param_table: float32 [1001, 1152], P(None, ('dp', 'seq')), may hold values from -0.1875 to 0.1875
- param_shift: float32 [1152, 9216], P(None, ('dp', 'seq')), may hold values from -0.1875 to 0.1875
- param_attend: float32 [1152, 3456], P(None, ('dp', 'seq')), may hold values from -0.1875 to 0.1875
- param_expand: float32 [1152, 4608], P(None, ('dp', 'seq')), may hold values from -0.1875 to 0.1875
- param_reduce: float32 [4608, 1152], P(('dp', 'seq')), may hold values from -0.09375 to 0.09375
- param_final: float32 [1152, 16], P(('dp', 'seq')), may hold values from -0.1875 to 0.1875
- param_biases: float32 [21888], P(('dp', 'seq')), may hold values from -0.3125 to 0.3125
- first_embed: float32 [272, 1152], P(None, ('dp', 'seq')), may hold values from -0.00012207031 to 0.00012207031
- first_square: float32 [2, 1152, 1152], P(None, None, ('dp', 'seq')), may hold values from -0.00012207031 to 0.00012207031
- first_table: float32 [1001, 1152], P(None, ('dp', 'seq')), may hold values from -1.1444092e-05 to 1.1444092e-05
- first_shift: float32 [1152, 9216], P(None, ('dp', 'seq')), may hold values from -0.00012207031 to 0.00012207031
- first_attend: float32 [1152, 3456], P(None, ('dp', 'seq')), may hold values from -0.00012207031 to 0.00012207031
- first_expand: float32 [1152, 4608], P(None, ('dp', 'seq')), may hold values from -0.00012207031 to 0.00012207031
- first_reduce: float32 [4608, 1152], P(('dp', 'seq')), may hold values from -0.00012207031 to 0.00012207031
- first_final: float32 [1152, 16], P(('dp', 'seq')), may hold values from -0.00012207031 to 0.00012207031
- first_biases: float32 [21888], P(('dp', 'seq')), may hold values from -0.00036621094 to 0.00036621094
- second_embed: float32 [272, 1152], P(None, ('dp', 'seq')), may hold values from 8.8507623e-10 to 1.42973855e-08
- second_square: float32 [2, 1152, 1152], P(None, None, ('dp', 'seq')), may hold values from 8.8507623e-10 to 1.42973855e-08
- second_table: float32 [1001, 1152], P(None, ('dp', 'seq')), may hold values from 8.850762e-12 to 1.4297385e-10
- second_shift: float32 [1152, 9216], P(None, ('dp', 'seq')), may hold values from 8.8507623e-10 to 1.42973855e-08
- second_attend: float32 [1152, 3456], P(None, ('dp', 'seq')), may hold values from 8.8507623e-10 to 1.42973855e-08
- second_expand: float32 [1152, 4608], P(None, ('dp', 'seq')), may hold values from 8.8507623e-10 to 1.42973855e-08
- second_reduce: float32 [4608, 1152], P(('dp', 'seq')), may hold values from 8.8507623e-10 to 1.42973855e-08
- second_final: float32 [1152, 16], P(('dp', 'seq')), may hold values from 8.8507623e-10 to 1.42973855e-08
- second_biases: float32 [21888], P(('dp', 'seq')), may hold values from 8.169935e-09 to 1.293573e-07
Outputs:
- loss_total: float32 [], replicated
- value_count: float32 [], replicated
- grad_norm: float32 [], replicated
- new_param_embed: float32 [272, 1152], P(None, ('dp', 'seq'))
- new_param_square: float32 [2, 1152, 1152], P(None, None, ('dp', 'seq'))
- new_param_table: float32 [1001, 1152], P(None, ('dp', 'seq'))
- new_param_shift: float32 [1152, 9216], P(None, ('dp', 'seq'))
- new_param_attend: float32 [1152, 3456], P(None, ('dp', 'seq'))
- new_param_expand: float32 [1152, 4608], P(None, ('dp', 'seq'))
- new_param_reduce: float32 [4608, 1152], P(('dp', 'seq'))
- new_param_final: float32 [1152, 16], P(('dp', 'seq'))
- new_param_biases: float32 [21888], P(('dp', 'seq'))
- new_first_embed: float32 [272, 1152], P(None, ('dp', 'seq'))
- new_first_square: float32 [2, 1152, 1152], P(None, None, ('dp', 'seq'))
- new_first_table: float32 [1001, 1152], P(None, ('dp', 'seq'))
- new_first_shift: float32 [1152, 9216], P(None, ('dp', 'seq'))
- new_first_attend: float32 [1152, 3456], P(None, ('dp', 'seq'))
- new_first_expand: float32 [1152, 4608], P(None, ('dp', 'seq'))
- new_first_reduce: float32 [4608, 1152], P(('dp', 'seq'))
- new_first_final: float32 [1152, 16], P(('dp', 'seq'))
- new_first_biases: float32 [21888], P(('dp', 'seq'))
- new_second_embed: float32 [272, 1152], P(None, ('dp', 'seq'))
- new_second_square: float32 [2, 1152, 1152], P(None, None, ('dp', 'seq'))
- new_second_table: float32 [1001, 1152], P(None, ('dp', 'seq'))
- new_second_shift: float32 [1152, 9216], P(None, ('dp', 'seq'))
- new_second_attend: float32 [1152, 3456], P(None, ('dp', 'seq'))
- new_second_expand: float32 [1152, 4608], P(None, ('dp', 'seq'))
- new_second_reduce: float32 [4608, 1152], P(('dp', 'seq'))
- new_second_final: float32 [1152, 16], P(('dp', 'seq'))
- new_second_biases: float32 [21888], P(('dp', 'seq'))
The draws below stay inside these ranges and needn't reach their ends.
Inputs may be any that keep to these rules, and one draw needn't show every extreme that they name: `heights`: in every micro-batch, one image of each aligned block of 2 images is 16 patches high and 20 wide. `widths`: height times width is at most 320.
All inputs are finite; a program needn't handle non-finite values.
Results may differ from the reference program's by a relative error of at most 0.011.
The reference program's roundings to bfloat16 on the way count: a program that leaves them out, or rounds other values in their place, can miss the bound.
Values may be sent and summed in bfloat16 or wider, within the bound.
No kernel may reach another device: no remote copies, remote signals or barrier semaphores. Data moves between devices by JAX's collectives and lax.ppermute only.
A program may use at most 384 MiB of HBM per device.

```python
import math
import jax
import jax.numpy as jnp
from jax import lax

D = 1152
HEADS = 16
HEAD = 72
FF = 4608
FREQ = 256
CLASSES = 1001
PIN = 16
GRID_H = 16
GRID_W = 20
SLOT = 320
MICRO = 2
IMG_DEV = 2
IMAGES = 16
TSTEPS = 1000
STEP = 10
PARAMS = 29376000


def grid_pair(key):
    clusters = IMAGES // IMG_DEV
    key_high, key_wide, key_full = jax.random.split(key, 3)
    column = jnp.arange(IMAGES, dtype=jnp.int32)
    cluster = column // IMG_DEV
    target = SLOT // 6 + (SLOT - SLOT // 6) * (cluster + 1) // clusters
    height = jax.random.randint(key_high, (MICRO, IMAGES), GRID_H // 2, GRID_H + 1)
    across = jnp.clip(target[None, :] // height + jax.random.randint(key_wide, (MICRO, IMAGES), -1, 2), 1, GRID_W)
    chosen = jax.random.randint(key_full, (MICRO, clusters), 0, IMG_DEV)
    spanning = (column % IMG_DEV)[None, :] == jnp.take(chosen, cluster, axis=1)
    height = jnp.where(spanning, GRID_H, height)
    across = jnp.where(spanning, GRID_W, across)
    return (height.astype(jnp.int32), across.astype(jnp.int32))


def draw_heights(key, part):
    return grid_pair(key)[0]


def draw_widths(key, part):
    return grid_pair(key)[1]


def touch_ends(values, stream_key, low, high):
    dims = values.shape
    spot = [jax.random.randint(jax.random.fold_in(stream_key, axis), (), 0, dims[axis]) for axis in range(len(dims))]
    values = values.at[tuple(spot)].set(low)
    longest = dims.index(max(dims))
    spot[longest] = (spot[longest] + 1) % dims[longest]
    return values.at[tuple(spot)].set(high)


def levels(key, dims, cuts, low, high):
    factor_of = 1.0
    for axis_at, blocks in cuts:
        steps = jax.random.uniform(jax.random.fold_in(jax.random.fold_in(key, 6), axis_at), (blocks,), jnp.float32, low / len(cuts), high / len(cuts))
        factor_of = factor_of * jnp.repeat(jnp.exp(steps), dims[axis_at] // blocks).reshape((-1,) + (1,) * (len(dims) - 1 - axis_at))
    return factor_of


def scatter_about(own_key, shape, scale, reach, shards=(), held_as=jnp.bfloat16):
    entries = jax.random.normal(own_key, shape, jnp.float32) * scale
    if len(shards) > 0:
        entries = levels(own_key, shape, shards, -0.22, 0.18) * entries
    return jnp.clip(entries, min=-reach, max=reach).astype(held_as)


def setup_inputs(seed: int = 0) -> dict:
    seeds = jax.random.split(jax.random.key(seed), 35)
    latents = scatter_about(seeds[0], (MICRO, IMAGES, SLOT, PIN), 1.0, 6.0, ((1, 8), (2, 4)), jnp.float32)
    noise_draw = scatter_about(seeds[1], (MICRO, IMAGES, SLOT, PIN), 1.0, 6.0, ((1, 8), (2, 4)), jnp.float32)
    heights = draw_heights(jax.random.fold_in(seeds[34], 71), 0)
    widths = draw_widths(jax.random.fold_in(seeds[34], 71), 0)
    labels = touch_ends(jax.random.randint(seeds[4], (MICRO, IMAGES), 0, CLASSES), jax.random.fold_in(seeds[4], 1), 0, CLASSES - 1).astype(jnp.int32)
    timesteps = touch_ends(jax.random.randint(seeds[5], (MICRO, IMAGES), 0, TSTEPS), jax.random.fold_in(seeds[5], 1), 0, TSTEPS - 1).astype(jnp.int32)
    bias_tiles = scatter_about(seeds[6], (MICRO, IMAGES, HEADS, SLOT, SLOT), 1.0, 4.0, ((1, 8), (2, 4)))
    param_embed = scatter_about(seeds[7], (PIN + FREQ, D), (4 * PIN) ** -0.5, 0.75, ((1, 32),), jnp.float32)
    param_square = scatter_about(seeds[8], (2, D, D), (D // 4) ** -0.5, 0.375, ((2, 32),), jnp.float32)
    param_table = scatter_about(seeds[9], (CLASSES, D), D ** -0.5, 0.1875, ((1, 32),), jnp.float32)
    param_shift = scatter_about(seeds[10], (D, 8 * D), D ** -0.5, 0.1875, ((1, 32),), jnp.float32)
    param_attend = scatter_about(seeds[11], (D, 3 * D), D ** -0.5, 0.1875, ((1, 32),), jnp.float32)
    param_expand = scatter_about(seeds[12], (D, FF), D ** -0.5, 0.1875, ((1, 32),), jnp.float32)
    param_reduce = scatter_about(seeds[13], (FF, D), FF ** -0.5, 0.09375, ((0, 32),), jnp.float32)
    param_final = scatter_about(seeds[14], (D, PIN), D ** -0.5, 0.1875, ((0, 32),), jnp.float32)
    param_biases = scatter_about(seeds[15], (15 * D + FF,), 0.05, 0.3125, ((0, 32),), jnp.float32)
    first_embed = scatter_about(seeds[16], (PIN + FREQ, D), (0.11 * PARAMS ** -0.5), 0.00012207031, ((1, 32),), jnp.float32)
    first_square = scatter_about(seeds[17], (2, D, D), (0.11 * PARAMS ** -0.5), 0.00012207031, ((2, 32),), jnp.float32)
    first_table = scatter_about(seeds[18], (CLASSES, D), (0.011 * PARAMS ** -0.5), 1.1444091796875e-05, ((1, 32),), jnp.float32)
    first_shift = scatter_about(seeds[19], (D, 8 * D), (0.11 * PARAMS ** -0.5), 0.00012207031, ((1, 32),), jnp.float32)
    first_attend = scatter_about(seeds[20], (D, 3 * D), (0.11 * PARAMS ** -0.5), 0.00012207031, ((1, 32),), jnp.float32)
    first_expand = scatter_about(seeds[21], (D, FF), (0.11 * PARAMS ** -0.5), 0.00012207031, ((1, 32),), jnp.float32)
    first_reduce = scatter_about(seeds[22], (FF, D), (0.11 * PARAMS ** -0.5), 0.00012207031, ((0, 32),), jnp.float32)
    first_final = scatter_about(seeds[23], (D, PIN), (0.11 * PARAMS ** -0.5), 0.00012207031, ((0, 32),), jnp.float32)
    first_biases = scatter_about(seeds[24], (15 * D + FF,), (0.33 * PARAMS ** -0.5), 0.00036621094, ((0, 32),), jnp.float32)
    second_embed = jnp.clip(jnp.exp(math.log(1.4297385497741288e-08) - 2.7821582 * jax.random.uniform(seeds[25], (PIN + FREQ, D), jnp.float32) ** levels(seeds[25], (PIN + FREQ, D), ((1, 32),), -0.2, 0.2)), 8.850762345247176e-10, 1.4297385497741288e-08)
    second_square = jnp.clip(jnp.exp(math.log(1.4297385497741288e-08) - 2.7821582 * jax.random.uniform(seeds[26], (2, D, D), jnp.float32) ** levels(seeds[26], (2, D, D), ((2, 32),), -0.2, 0.2)), 8.850762345247176e-10, 1.4297385497741288e-08)
    second_table = jnp.clip(jnp.exp(math.log(1.4297385497741288e-10) - 2.7821582 * jax.random.uniform(seeds[27], (CLASSES, D), jnp.float32) ** levels(seeds[27], (CLASSES, D), ((1, 32),), -0.2, 0.2)), 8.850762137080359e-12, 1.4297385497741288e-10)
    second_shift = jnp.clip(jnp.exp(math.log(1.4297385497741288e-08) - 2.7821582 * jax.random.uniform(seeds[28], (D, 8 * D), jnp.float32) ** levels(seeds[28], (D, 8 * D), ((1, 32),), -0.2, 0.2)), 8.850762345247176e-10, 1.4297385497741288e-08)
    second_attend = jnp.clip(jnp.exp(math.log(1.4297385497741288e-08) - 2.7821582 * jax.random.uniform(seeds[29], (D, 3 * D), jnp.float32) ** levels(seeds[29], (D, 3 * D), ((1, 32),), -0.2, 0.2)), 8.850762345247176e-10, 1.4297385497741288e-08)
    second_expand = jnp.clip(jnp.exp(math.log(1.4297385497741288e-08) - 2.7821582 * jax.random.uniform(seeds[30], (D, FF), jnp.float32) ** levels(seeds[30], (D, FF), ((1, 32),), -0.2, 0.2)), 8.850762345247176e-10, 1.4297385497741288e-08)
    second_reduce = jnp.clip(jnp.exp(math.log(1.4297385497741288e-08) - 2.7821582 * jax.random.uniform(seeds[31], (FF, D), jnp.float32) ** levels(seeds[31], (FF, D), ((0, 32),), -0.2, 0.2)), 8.850762345247176e-10, 1.4297385497741288e-08)
    second_final = jnp.clip(jnp.exp(math.log(1.4297385497741288e-08) - 2.7821582 * jax.random.uniform(seeds[32], (D, PIN), jnp.float32) ** levels(seeds[32], (D, PIN), ((0, 32),), -0.2, 0.2)), 8.850762345247176e-10, 1.4297385497741288e-08)
    second_biases = jnp.clip(jnp.exp(math.log(1.2935730353547115e-07) - 2.7621174 * jax.random.uniform(seeds[33], (15 * D + FF,), jnp.float32) ** levels(seeds[33], (15 * D + FF,), ((0, 32),), -0.2, 0.2)), 8.169934950785773e-09, 1.2935730353547115e-07)
    return {"latents": latents, "noise_draw": noise_draw, "heights": heights, "widths": widths, "labels": labels, "timesteps": timesteps, "bias_tiles": bias_tiles, "param_embed": param_embed, "param_square": param_square, "param_table": param_table, "param_shift": param_shift, "param_attend": param_attend, "param_expand": param_expand, "param_reduce": param_reduce, "param_final": param_final, "param_biases": param_biases, "first_embed": first_embed, "first_square": first_square, "first_table": first_table, "first_shift": first_shift, "first_attend": first_attend, "first_expand": first_expand, "first_reduce": first_reduce, "first_final": first_final, "first_biases": first_biases, "second_embed": second_embed, "second_square": second_square, "second_table": second_table, "second_shift": second_shift, "second_attend": second_attend, "second_expand": second_expand, "second_reduce": second_reduce, "second_final": second_final, "second_biases": second_biases}


@jax.custom_vjp
def low(v):
    return lax.optimization_barrier(v.astype(jnp.bfloat16)).astype(jnp.float32)

@jax.custom_vjp
def low_back(v):
    return v

def low_keep(v):
    return (low(v), None)

def low_pass(kept, grad):
    return (grad,)

def back_keep(v):
    return (v, None)

def back_low(kept, grad):
    return (low(grad),)
low.defvjp(low_keep, low_pass)
low_back.defvjp(back_keep, back_low)
HIGHEST = lax.Precision.HIGHEST
BETA_ONE = 0.9
BETA_TWO = 0.95
EPSILON = 1e-08
DECAY = 0.1
RATE = 0.03
LIMIT = 1.0

def smooth_gate(values_in):
    return values_in * jax.nn.sigmoid(values_in)

def gaussian_unit(values_in):
    return 0.5 * values_in * (1.0 + jnp.tanh(0.7978845608028654 * (values_in + 0.044715 * values_in * values_in * values_in)))

def modnorm(stream, offset, stretch):
    centred = stream - lax.optimization_barrier(jnp.mean(stream, -1, keepdims=True))
    spread = lax.optimization_barrier(jnp.mean(centred * centred, -1, keepdims=True))
    return centred * lax.rsqrt(spread + 1e-06) * (1.0 + stretch[:, None, :]) + offset[:, None, :]

def time_freq(steps_in):
    half_freq = FREQ // 2
    rate_table = jnp.exp(-math.log(10000.0) * jnp.arange(half_freq).astype(jnp.float32) / half_freq)
    angles = steps_in.astype(jnp.float32)[:, None] * rate_table[None, :]
    return jnp.concatenate([jnp.cos(angles), jnp.sin(angles)], -1)

def signal_level(steps_in):
    angles = (steps_in.astype(jnp.float32) / TSTEPS + 0.008) / 1.008 * (math.pi / 2)
    return jnp.cos(angles) * jnp.cos(angles)

def place_embed(across, first_slot, slots):
    slot_ids = first_slot + jnp.arange(slots, dtype=jnp.int32)
    row_pos = (slot_ids[None, :] // across[:, None]).astype(jnp.float32)
    col_pos = (slot_ids[None, :] % across[:, None]).astype(jnp.float32)
    quarter = D // 4
    rate_table = jnp.exp(-math.log(10000.0) * jnp.arange(quarter).astype(jnp.float32) / quarter)
    rows_angle = row_pos[..., None] * rate_table
    cols_angle = col_pos[..., None] * rate_table
    return jnp.concatenate([jnp.sin(rows_angle), jnp.cos(rows_angle), jnp.sin(cols_angle), jnp.cos(cols_angle)], -1)

def bias_parts(bias_vector):
    marks = [0, D, 2 * D, 3 * D, 11 * D, 12 * D, 13 * D, 14 * D, 14 * D + FF, 15 * D + FF]
    return [bias_vector[marks[number]:marks[number + 1]] for number in range(9)]

def block_loss(params, block_data):
    embed_weight, square_weight, class_table, shift_weight, attend_weight, expand_weight, reduce_weight, final_weight, bias_vector = params
    latent, noise_in, height, across, labels_in, steps_in, bias_tile = block_data
    biases = bias_parts(bias_vector)
    freq_in = low(time_freq(steps_in))
    pre_time = low_back(jnp.matmul(freq_in, embed_weight[PIN:], precision=HIGHEST) + biases[1])
    hid_time = low(smooth_gate(pre_time))
    onehot = (labels_in[:, None] == jnp.arange(CLASSES)[None, :]).astype(jnp.float32)
    condition = low_back(jnp.matmul(hid_time, square_weight[0], precision=HIGHEST) + biases[2] + jnp.matmul(onehot, class_table, precision=HIGHEST))
    cond_act = low(smooth_gate(condition))
    modulation = low_back(jnp.matmul(cond_act, shift_weight, precision=HIGHEST) + biases[3])
    pieces = [modulation[:, number * D:(number + 1) * D] for number in range(8)]
    signal = signal_level(steps_in)[:, None, None]
    noisy_input = low(jnp.sqrt(signal) * latent + jnp.sqrt(1.0 - signal) * noise_in)
    stream_in = low_back(jnp.matmul(noisy_input, embed_weight[:PIN], precision=HIGHEST) + biases[0] + place_embed(across, 0, SLOT))
    normed_one = low(modnorm(stream_in, pieces[0], pieces[1]))
    triple = jnp.matmul(normed_one, attend_weight, precision=HIGHEST) + jnp.concatenate([biases[4], jnp.zeros_like(biases[4]), biases[5]])
    triple = low(low_back(triple)).reshape(-1, SLOT, 3, HEADS, HEAD)
    queries, key_rows, values = (triple[:, :, 0], triple[:, :, 1], triple[:, :, 2])
    usable = jnp.arange(SLOT)[None, :] < (height * across)[:, None]
    raw_scores = jnp.einsum('iqhd,ikhd->ihqk', queries, key_rows, precision=HIGHEST) * HEAD ** (-0.5) + bias_tile.astype(jnp.float32)
    scores = low_back(jnp.where(usable[:, None, None, :], raw_scores, -1e+30))
    row_max = lax.optimization_barrier(jnp.max(scores, -1, keepdims=True))
    log_total = row_max + jnp.log(lax.optimization_barrier(jnp.sum(jnp.exp(scores - row_max), -1, keepdims=True)))
    attention = low(jnp.exp(scores - log_total))
    context = jnp.einsum('ihqk,ikhd->iqhd', attention, values, precision=HIGHEST).reshape(-1, SLOT, D)
    context = low(low_back(context))
    attended = low_back(jnp.matmul(context, square_weight[1], precision=HIGHEST) + biases[6])
    stream_mid = stream_in + pieces[2][:, None, :] * attended
    normed_two = low(modnorm(stream_mid, pieces[3], pieces[4]))
    upward = low_back(jnp.matmul(normed_two, expand_weight, precision=HIGHEST) + biases[7])
    active = low(gaussian_unit(upward))
    downward = low_back(jnp.matmul(active, reduce_weight, precision=HIGHEST) + biases[8])
    stream_out = stream_mid + pieces[5][:, None, :] * downward
    normed_end = low(modnorm(stream_out, pieces[6], pieces[7]))
    predicted = low_back(jnp.matmul(normed_end, final_weight, precision=HIGHEST))
    errors = predicted - noise_in
    kept_rows = usable[:, :, None].astype(jnp.float32)
    return jnp.sum(kept_rows * errors * errors)

def total_loss(params, blocks):

    def advance(carry, block_data):
        return (carry + jax.checkpoint(block_loss)(params, block_data), None)
    result, _ = lax.scan(advance, jnp.zeros((), jnp.float32), blocks)
    return result

def adam_step(weight, moment, second, gradient, factor):
    clipped = gradient * factor
    moment = BETA_ONE * moment + (1.0 - BETA_ONE) * clipped
    second = BETA_TWO * second + (1.0 - BETA_TWO) * clipped * clipped
    fixed_one = moment / (1.0 - BETA_ONE ** STEP)
    fixed_two = second / (1.0 - BETA_TWO ** STEP)
    weight = weight - RATE * (fixed_one / (jnp.sqrt(fixed_two) + EPSILON) + DECAY * weight)
    return (weight, moment, second)

def reference(latents, noise_draw, heights, widths, labels, timesteps, bias_tiles, param_embed, param_square, param_table, param_shift, param_attend, param_expand, param_reduce, param_final, param_biases, first_embed, first_square, first_table, first_shift, first_attend, first_expand, first_reduce, first_final, first_biases, second_embed, second_square, second_table, second_shift, second_attend, second_expand, second_reduce, second_final, second_biases):
    params_in = [param_embed, param_square, param_table, param_shift, param_attend, param_expand, param_reduce, param_final, param_biases]
    firsts = [first_embed, first_square, first_table, first_shift, first_attend, first_expand, first_reduce, first_final, first_biases]
    seconds = [second_embed, second_square, second_table, second_shift, second_attend, second_expand, second_reduce, second_final, second_biases]
    count_blocks = MICRO * IMAGES // IMG_DEV

    def blocked(array):
        return array.reshape((count_blocks, IMG_DEV) + array.shape[2:])
    blocks = (blocked(latents), blocked(noise_draw), blocked(heights), blocked(widths), blocked(labels), blocked(timesteps), blocked(bias_tiles))

    def objective(*weights):
        return total_loss([low(weight) for weight in weights], blocks)
    loss_total, pull = jax.vjp(objective, *params_in)
    grads = pull(jnp.ones_like(loss_total))
    value_count = jnp.sum(heights * widths).astype(jnp.float32) * PIN
    squared = sum((jnp.sum(gradient * gradient) for gradient in grads))
    grad_norm = jnp.sqrt(squared)
    factor = LIMIT / jnp.maximum(grad_norm, LIMIT)
    results = [adam_step(params_in[number], firsts[number], seconds[number], grads[number], factor) for number in range(9)]
    fresh = [results[number][0] for number in range(9)] + [results[number][1] for number in range(9)] + [results[number][2] for number in range(9)]
    return (loss_total, value_count, grad_norm, fresh[0], fresh[1], fresh[2], fresh[3], fresh[4], fresh[5], fresh[6], fresh[7], fresh[8], fresh[9], fresh[10], fresh[11], fresh[12], fresh[13], fresh[14], fresh[15], fresh[16], fresh[17], fresh[18], fresh[19], fresh[20], fresh[21], fresh[22], fresh[23], fresh[24], fresh[25], fresh[26])
```

```python
import functools
import math

import jax
import jax.numpy as jnp
import numpy as np
from jax import lax
from jax.experimental import pallas as pl
from jax.experimental.pallas import tpu as pltpu
from jax.sharding import PartitionSpec as P

D = 1152
HEADS = 16
HEAD = 72
FF = 4608
FREQ = 256
PIN = 16
MICRO = 2
TSTEPS = 1000
STEP = 10
LANES = 128
AXES = ("dp", "seq")

BETA_ONE = 0.9
BETA_TWO = 0.95
EPSILON = 1e-08
DECAY = 0.1
RATE = 0.03
LIMIT = 1.0


def to_low(values_in):
    return values_in.astype(jnp.bfloat16)


def wide(values_in):
    return values_in.astype(jnp.float32)


def smooth_gate(values_in):
    return values_in * jax.nn.sigmoid(values_in)


def smooth_gate_slope(values_in):
    gate = jax.nn.sigmoid(values_in)
    return gate * (1.0 + values_in * (1.0 - gate))


def contract(left, right, left_dim, right_dim):
    return lax.dot_general(
        left,
        right,
        (((left_dim,), (right_dim,)), ((), ())),
        preferred_element_type=jnp.float32,
    )


def time_freq(steps_in):
    half_freq = FREQ // 2
    rate_table = jnp.exp(-math.log(10000.0) * jnp.arange(half_freq).astype(jnp.float32) / half_freq)
    angles = steps_in.astype(jnp.float32)[:, None] * rate_table[None, :]
    return jnp.concatenate([jnp.cos(angles), jnp.sin(angles)], -1)


def signal_level(steps_in):
    angles = (steps_in.astype(jnp.float32) / TSTEPS + 0.008) / 1.008 * (math.pi / 2)
    return jnp.cos(angles) * jnp.cos(angles)


def place_tables(slots, widest):
    quarter = D // 4
    lane = jnp.arange(D)
    rate = jnp.exp(-math.log(10000.0) * (lane % quarter).astype(jnp.float32) / quarter)
    fine = 16
    coarse = -(-slots // fine)
    steps = jnp.concatenate(
        [jnp.arange(coarse, dtype=jnp.float32) * fine, jnp.arange(fine, dtype=jnp.float32)]
    )
    angles = steps[:, None] * rate[None, :]
    sines, cosines = (jnp.sin(angles), jnp.cos(angles))
    sine_high, sine_low = (sines[:coarse, None], sines[None, coarse:])
    cosine_high, cosine_low = (cosines[:coarse, None], cosines[None, coarse:])
    table = jnp.where(
        lane // quarter % 2 == 0,
        sine_high * cosine_low + cosine_high * sine_low,
        cosine_high * cosine_low - sine_high * sine_low,
    ).reshape(coarse * fine, D)
    by_row = lane < 2 * quarter
    table = jnp.concatenate(
        [jnp.where(by_row, table[:slots], 0.0), jnp.where(by_row, 0.0, table[:widest])], 0
    )
    part_one = to_low(table)
    rest = table - wide(part_one)
    part_two = to_low(rest)
    part_three = to_low(rest - wide(part_two))
    return [part_one, part_two, part_three]


def place_picks(slot_ids, across, slots, widest):
    row_pos = (slot_ids // across)[:, None]
    col_pos = (slot_ids % across)[:, None] + slots
    spots = jnp.arange(slots + widest)[None, :]
    return to_low(((row_pos == spots) | (col_pos == spots)).astype(jnp.float32))


def after(values_in, earlier):
    return lax.optimization_barrier((values_in, earlier))[0]


def standardize(stream):
    centred = stream - jnp.mean(stream, -1, keepdims=True)
    scale = lax.rsqrt(jnp.mean(centred * centred, -1, keepdims=True) + 1e-06)
    return (centred * scale, scale)


def stretch_shift(unit, offset, stretch):
    return unit * (1.0 + stretch[:, None, :]) + offset[:, None, :]


def stretch_back(grad, unit, scale, stretch):
    grad_offset = jnp.sum(grad, 1)
    grad_stretch = jnp.sum(grad * unit, 1)
    grad_unit = grad * (1.0 + stretch[:, None, :])
    grad_stream = scale * (
        grad_unit
        - jnp.mean(grad_unit, -1, keepdims=True)
        - unit * jnp.mean(grad_unit * unit, -1, keepdims=True)
    )
    return (grad_stream, grad_offset, grad_stretch)


CUBE = 0.044715
ROOT = 0.7978845608028654


def gaussian_unit(values_in):
    inner = ROOT * (values_in + CUBE * values_in * values_in * values_in)
    return 0.5 * values_in * (1.0 + jnp.tanh(inner))


def gaussian_slope(values_in):
    inner = ROOT * (values_in + CUBE * values_in * values_in * values_in)
    bend = jnp.tanh(inner)
    return 0.5 * (1.0 + bend) + 0.5 * values_in * (1.0 - bend * bend) * ROOT * (
        1.0 + 3.0 * CUBE * values_in * values_in
    )


def attend_probs(nat_ref, bias_ref, head, own, keep):
    width = own * HEAD
    queries = nat_ref[:, head * HEAD : (head + 1) * HEAD]
    keys = nat_ref[:, width + head * HEAD : width + (head + 1) * HEAD]
    values = nat_ref[:, 2 * width + head * HEAD : 2 * width + (head + 1) * HEAD]
    scores = contract(queries, keys, 1, 1) * HEAD ** (-0.5) + wide(bias_ref[0, head])
    scores = jnp.where(keep, scores, -1e30)
    powers = jnp.exp(scores - jnp.max(scores, -1, keepdims=True))
    probs = powers * (1.0 / jnp.sum(powers, -1, keepdims=True))
    return (queries, keys, values, probs)


def attend_enter(meta_ref, triple_ref, nat_ref, masks):
    block = triple_ref.shape[2]
    for number, mask in enumerate(masks):
        first = pl.multiple_of((meta_ref[0] ^ mask) * block, 16)
        nat_ref[pl.ds(first, block), :] = triple_ref[number, 0]
    slots = nat_ref.shape[0]
    local = lax.broadcasted_iota(jnp.int32, (slots, slots), 1)
    return local < meta_ref[1 + pl.program_id(0)]


def attend_kernel(masks, meta_ref, triple_ref, bias_ref, context_ref, nat_ref):
    keep = attend_enter(meta_ref, triple_ref, nat_ref, masks)
    own, block = (bias_ref.shape[1], triple_ref.shape[2])
    mixed = []
    for head in range(own):
        _, _, values, probs = attend_probs(nat_ref, bias_ref, head, own, keep)
        mixed.append(to_low(contract(to_low(probs), values, 1, 0)))
    context = jnp.concatenate(mixed, 1)
    for number in range(len(masks)):
        context_ref[number, 0] = context[number * block : (number + 1) * block]


def attend_back_kernel(
    masks, meta_ref, triple_ref, bias_ref, grad_ref, out_ref, sums_ref, nat_ref, back_ref
):
    keep = attend_enter(meta_ref, triple_ref, nat_ref, masks)
    own, block = (bias_ref.shape[1], triple_ref.shape[2])
    width = own * HEAD
    grads = jnp.concatenate([grad_ref[number, 0] for number in range(len(masks))], 0)
    for head in range(own):
        queries, keys, values, probs = attend_probs(nat_ref, bias_ref, head, own, keep)
        grad_context = grads[:, head * HEAD : (head + 1) * HEAD]
        grad_probs = contract(grad_context, values, 1, 1)
        weighted = probs * grad_probs
        grad_scores = to_low(weighted - probs * jnp.sum(weighted, -1, keepdims=True))
        pieces = (
            contract(grad_scores, keys, 1, 0) * HEAD ** (-0.5),
            contract(grad_scores, queries, 0, 0) * HEAD ** (-0.5),
            contract(to_low(probs), grad_context, 0, 0),
        )
        for kind in range(3):
            begin = kind * width + head * HEAD
            back_ref[:, begin : begin + HEAD] = to_low(pieces[kind])
    sums_ref[0] = jnp.sum(wide(back_ref[...]), 0, keepdims=True)
    for number, mask in enumerate(masks):
        first = pl.multiple_of((meta_ref[0] ^ mask) * block, 16)
        out_ref[number, 0] = back_ref[pl.ds(first, block), :]


def attend_call(masks, meta, triple, bias_tiles, grads):
    images, own, slots, _ = bias_tiles.shape
    count, _, block, full = triple.shape
    width = own * HEAD
    backward = len(grads) > 0
    row = lambda image, meta_ref: (0, image, 0, 0)
    tri_spec = pl.BlockSpec((count, 1, block, full), row)
    slim_spec = pl.BlockSpec((count, 1, block, width), row)
    in_specs = [
        tri_spec,
        pl.BlockSpec((1, own, slots, slots), lambda image, meta_ref: (image, 0, 0, 0)),
    ] + [slim_spec] * len(grads)
    nat = pltpu.VMEM((slots, full), jnp.bfloat16)
    if backward:
        kernel, products = (attend_back_kernel, 6)
        out_shape = (
            jax.ShapeDtypeStruct(triple.shape, jnp.bfloat16),
            jax.ShapeDtypeStruct((images, 1, full), jnp.float32),
        )
        out_specs = (tri_spec, pl.BlockSpec((1, 1, full), lambda image, meta_ref: (image, 0, 0)))
        scratch = [nat, nat]
    else:
        kernel, products = (attend_kernel, 2)
        out_shape = jax.ShapeDtypeStruct((count, images, block, width), jnp.bfloat16)
        out_specs = slim_spec
        scratch = [nat]
    return pl.pallas_call(
        functools.partial(kernel, masks),
        out_shape=out_shape,
        grid_spec=pltpu.PrefetchScalarGridSpec(
            num_scalar_prefetch=1,
            grid=(images,),
            in_specs=in_specs,
            out_specs=out_specs,
            scratch_shapes=scratch,
        ),
        compiler_params=pltpu.CompilerParams(vmem_limit_bytes=40 * 2**20),
        cost_estimate=pl.CostEstimate(flops=1000, bytes_accessed=1000, transcendentals=0),
    )(meta, triple, bias_tiles, *grads)


def weight_copies(pick_ref, weight_ref, kind, held_ref, sem_ref):
    rows = weight_ref.shape[2]
    count = held_ref.shape[1] // rows
    copies = []
    for number in range(4 * count):
        target = held_ref.at[number // count, pl.ds(number % count * rows, rows)]
        copies.append(
            (
                number // count,
                pltpu.make_async_copy(
                    weight_ref.at[pick_ref[number], kind], target, sem_ref.at[kind, number]
                ),
            )
        )
    return copies


def start_copies(groups):
    @pl.when(pl.program_id(0) == 0)
    def _():
        for copies in groups:
            for _, copy in copies:
                copy.start()


def wait_copies(copies):
    for quarter in range(4):

        @pl.when(pl.program_id(0) == quarter)
        def _():
            for number, copy in copies:
                if number == quarter:
                    copy.wait()


def put_pair(total, own_ref, sent_ref):
    rows = own_ref.shape[0]

    @pl.when(pl.program_id(0) == pl.num_programs(0) - 1)
    def _():
        own_ref[...] = total[:rows]
        sent_ref[...] = to_low(total[rows:])


def add_up(total_ref, product):
    @pl.when(pl.program_id(0) == 0)
    def _():
        total_ref[...] = product

    @pl.when(pl.program_id(0) > 0)
    def _():
        total_ref[...] += product


def forward_kernel(
    pick_ref,
    normed_ref,
    bias_ref,
    weight_ref,
    up_ref,
    active_ref,
    own_ref,
    sent_ref,
    expand_held,
    reduce_held,
    total_ref,
    sem_ref,
):
    quarter = pl.program_id(0)
    expand_copies = weight_copies(pick_ref, weight_ref, 0, expand_held, sem_ref)
    reduce_copies = weight_copies(pick_ref, weight_ref, 1, reduce_held, sem_ref)
    start_copies([expand_copies, reduce_copies])
    wait_copies(expand_copies)
    upward = contract(normed_ref[...], expand_held[quarter], 1, 1) + bias_ref[0]
    up_ref[0] = upward
    active = to_low(gaussian_unit(upward))
    active_ref[0] = active
    wait_copies(reduce_copies)
    add_up(total_ref, contract(active, reduce_held[quarter], 1, 0))
    put_pair(total_ref, own_ref, sent_ref)


def backward_kernel(
    pick_ref,
    grad_ref,
    up_ref,
    weight_ref,
    out_ref,
    sums_ref,
    own_ref,
    sent_ref,
    expand_held,
    reduce_held,
    total_ref,
    sem_ref,
):
    quarter = pl.program_id(0)
    expand_copies = weight_copies(pick_ref, weight_ref, 0, expand_held, sem_ref)
    reduce_copies = weight_copies(pick_ref, weight_ref, 1, reduce_held, sem_ref)
    start_copies([reduce_copies, expand_copies])
    wait_copies(reduce_copies)
    grad_active = contract(grad_ref[...], reduce_held[quarter], 1, 1)
    grad_up = to_low(gaussian_slope(up_ref[0]) * grad_active)
    out_ref[0] = grad_up
    sums_ref[0] = jnp.sum(wide(grad_up), 0, keepdims=True)
    wait_copies(expand_copies)
    add_up(total_ref, contract(grad_up, expand_held[quarter], 1, 0))
    put_pair(total_ref, own_ref, sent_ref)


def hidden_call(kernel, pick, left, second, weights):
    rows = left.shape[0]
    size = second.shape[2]
    whole = pl.BlockSpec((rows, D), lambda quarter, pick_ref: (0, 0))
    slab = pl.BlockSpec((1, rows, size), lambda quarter, pick_ref: (quarter, 0, 0))
    line = pl.BlockSpec((1, 1, size), lambda quarter, pick_ref: (quarter, 0, 0))
    half = pl.BlockSpec((rows // 2, D), lambda quarter, pick_ref: (0, 0))
    if kernel is forward_kernel:
        second_spec, out_specs = (line, (slab, slab, half, half))
        kinds = (((4, rows, size), jnp.float32), ((4, rows, size), jnp.bfloat16))
    else:
        second_spec, out_specs = (slab, (slab, line, half, half))
        kinds = (((4, rows, size), jnp.bfloat16), ((4, 1, size), jnp.float32))
    kinds = kinds + (((rows // 2, D), jnp.float32), ((rows // 2, D), jnp.bfloat16))
    return pl.pallas_call(
        kernel,
        out_shape=tuple(jax.ShapeDtypeStruct(shape, kind) for shape, kind in kinds),
        grid_spec=pltpu.PrefetchScalarGridSpec(
            num_scalar_prefetch=1,
            grid=(4,),
            in_specs=[whole, second_spec, pl.BlockSpec(memory_space=pl.ANY)],
            out_specs=out_specs,
            scratch_shapes=[
                pltpu.VMEM((4, size, D), jnp.bfloat16),
                pltpu.VMEM((4, size, D), jnp.bfloat16),
                pltpu.VMEM((rows, D), jnp.float32),
                pltpu.SemaphoreType.DMA((2, 4 * size // weights.shape[2])),
            ],
        ),
        compiler_params=pltpu.CompilerParams(vmem_limit_bytes=56 * 2**20),
        cost_estimate=pl.CostEstimate(flops=1000, bytes_accessed=1000, transcendentals=0),
    )(pick, left, second, weights)


def outer_kernel(grad_up_ref, active_ref, normed_ref, grad_ref, *refs):
    outs, held, sem_ref = (refs[:7], refs[7:14], refs[14])
    step = pl.program_id(0)
    half = held[0].shape[1]
    products = (
        contract(grad_up_ref[0], normed_ref[...], 0, 0),
        contract(active_ref[0], grad_ref[...], 0, 0),
    )
    copies = [pltpu.make_async_copy(held[at], outs[at], sem_ref.at[at]) for at in range(7)]
    for turn in range(4):

        @pl.when(step == turn)
        def _():
            if turn == 3:
                for kind in range(2):
                    held[6][kind] = products[kind]
                copies[6].start()
            else:
                low_ref, high_ref = (held[2 * turn], held[2 * turn + 1])
                for kind in range(2):
                    low_ref[kind] = products[kind][:half].astype(low_ref.dtype)
                    high_ref[kind] = products[kind][half:].astype(high_ref.dtype)
                copies[2 * turn].start()
                copies[2 * turn + 1].start()

    @pl.when(step == 3)
    def _():
        for copy in copies:
            copy.wait()


def outer_call(grad_up, active, normed, grad_down):
    _, rows, size = grad_up.shape
    low, full = (jnp.bfloat16, jnp.float32)
    kinds = [low, low, full, low, low, full]
    shapes = [((2, size // 2, D), kind) for kind in kinds] + [((2, size, D), full)]
    slab = pl.BlockSpec(
        (1, rows, size),
        lambda step: (jnp.where(step == 0, 3, jnp.where(step == 3, 0, step)), 0, 0),
    )
    whole = pl.BlockSpec((rows, D), lambda step: (0, 0))
    return pl.pallas_call(
        outer_kernel,
        out_shape=tuple(jax.ShapeDtypeStruct(shape, kind) for shape, kind in shapes),
        grid=(4,),
        in_specs=[slab, slab, whole, whole],
        out_specs=tuple([pl.BlockSpec(memory_space=pl.ANY)] * 7),
        scratch_shapes=[pltpu.VMEM(shape, kind) for shape, kind in shapes]
        + [pltpu.SemaphoreType.DMA((7,))],
        compiler_params=pltpu.CompilerParams(vmem_limit_bytes=56 * 2**20),
        cost_estimate=pl.CostEstimate(flops=1000, bytes_accessed=1000, transcendentals=0),
    )(grad_up, active, normed, grad_down)


def unit_plan(devices, seq):
    share = 3 * D // devices
    unit = math.gcd(math.gcd(share, D // seq), HEAD)
    per = share // unit
    span = D // seq

    def group_of(number):
        return (number * unit % D) // span

    left = [{local: group_of(owner * per + local) for local in range(per)} for owner in range(devices)]
    send = np.zeros((per, devices), np.int32)
    target = np.zeros((per, devices), np.int32)
    held = np.zeros((per, devices), np.int32)
    for turn in range(per):
        match = [-1] * devices

        def seek(owner, seen):
            groups = set(left[owner].values())
            near = sorted(
                (place for place in range(devices) if place % seq in groups),
                key=lambda place: (place != owner, place // seq != owner // seq, place ^ owner),
            )
            for place in near:
                if place in seen:
                    continue
                seen.add(place)
                if match[place] < 0 or seek(match[place], seen):
                    match[place] = owner
                    return True
            return False

        for owner in range(devices):
            assert seek(owner, set())
        for place, owner in enumerate(match):
            local = next(item for item, group in left[owner].items() if group == place % seq)
            del left[owner][local]
            send[turn, owner] = local
            target[turn, owner] = place
            held[turn, place] = owner * per + local
    return (unit, per, send, target, held)


def unit_rows(devices, seq, unit, per, held):
    dp = devices // seq
    span = D // seq
    extra = D // devices
    rows = np.full((devices, dp * (per * unit + extra)), -1, np.int32)
    for place in range(devices):
        at = 0
        for mask in gather_masks(dp):
            for turn in range(per):
                first = int(held[turn, place ^ (mask * seq)]) * unit
                kind, inside = (first // D, first % D)
                begin = kind * span + inside - span * (place % seq)
                rows[place, at : at + unit] = np.arange(begin, begin + unit)
                at += unit
            at += extra
    return rows


def gather_masks(dp):
    masks = [0]
    bit = dp >> 1
    while bit:
        masks = masks + [item ^ bit for item in masks]
        bit >>= 1
    return masks


def make_step(mesh):
    dp, seq = (mesh.shape["dp"], mesh.shape["seq"])
    devices = dp * seq
    top = devices.bit_length() - 1
    seq_bits = seq.bit_length() - 1
    own_heads = HEADS // seq
    span = D // seq
    unit, per, unit_send, unit_target, unit_held = unit_plan(devices, seq)
    row_table = unit_rows(devices, seq, unit, per, unit_held)
    cols = D // devices
    shift_cols = 8 * D // devices
    hidden_share = FF // devices
    bias_share = (15 * D + FF) // devices
    dp_bits = list(range(top - 1, seq_bits - 1, -1))
    far_bits = list(range(top - 1, 2, -1))
    seq_down = list(range(seq_bits - 1, -1, -1))

    def masks_of(bits):
        masks = [0]
        for bit in bits:
            masks = masks + [mask ^ (1 << bit) for mask in masks]
        return masks

    slot_masks = masks_of(seq_down)

    def swap(values_in, bit):
        return lax.ppermute(
            values_in, AXES, [(place, place ^ (1 << bit)) for place in range(devices)]
        )

    def exchange(values_in):
        return lax.all_to_all(values_in, AXES, split_axis=0, concat_axis=0, tiled=True)

    def share_all(block):
        return exchange(jnp.broadcast_to(block[None], (devices,) + block.shape))

    def gather_rows(rows, bits):
        for bit in bits:
            rows = jnp.concatenate([rows, swap(rows, bit)], 0)
        return rows

    def fold_rows(rows, bits):
        for bit in bits:
            half = rows.shape[0] // 2
            rows = rows[:half] + wide(swap(to_low(rows[half:]), bit))
        return rows

    def fold_second(rows, bits):
        for bit in bits:
            half = rows.shape[1] // 2
            rows = rows[:, :half] + wide(swap(to_low(rows[:, half:]), bit))
        return rows

    def on_device(
        latents,
        noise_draw,
        heights,
        widths,
        labels,
        timesteps,
        bias_tiles,
        *states,
    ):
        params_in, firsts, seconds = (states[:9], states[9:18], states[18:])
        seq_index = lax.axis_index("seq")
        me = lax.axis_index("dp") * seq + seq_index
        local_slots = latents.shape[2]
        slots = local_slots * seq
        widest = min(slots, 32)
        images = latents.shape[0] * latents.shape[1]
        classes = params_in[2].shape[0]
        tokens = images * local_slots
        all_tokens = images * slots
        all_images = images * dp
        latent = latents.reshape(images, local_slots, PIN)
        noise_in = noise_draw.reshape(images, local_slots, PIN)
        height, across = (heights.reshape(images), widths.reshape(images))
        label_own, step_own = (labels.reshape(images), timesteps.reshape(images))
        bias_all = bias_tiles.reshape(images, own_heads, slots, slots)
        used = height * across

        embed_t = params_in[0].T
        square_t = jnp.transpose(params_in[1], (2, 0, 1))
        table_t = to_low(params_in[2].T)
        shift_t = to_low(params_in[3].T)
        attend_t = to_low(params_in[4].T)
        expand_t = to_low(params_in[5].T)
        reduce_r = to_low(params_in[6])

        small = jnp.concatenate(
            [to_low(params_in[8]), to_low(embed_t[:, :PIN]).reshape(-1), to_low(params_in[7]).reshape(-1)]
            + [
                to_low(wide(piece))
                for piece in (step_own // 32, step_own % 32, label_own // 32, label_own % 32)
            ]
        )
        length = -(-small.shape[0] // 2048) * 2048
        small = jnp.pad(small, (0, length - small.shape[0])).reshape(-1, LANES)
        embed_own = to_low(embed_t[:, PIN:]).reshape(-1, LANES)
        small = share_all(jnp.concatenate([small, embed_own], 0))
        embed_time = small[:, length // LANES :].reshape(D, FREQ)
        small = small[:, : length // LANES].reshape(devices, length)
        at = bias_share
        biases = wide(small[:, :at].reshape(-1))
        patch_t = small[:, at : at + cols * PIN].reshape(D, PIN)
        at = at + cols * PIN
        final_weight = small[:, at : at + cols * PIN].reshape(D, PIN)
        at = at + cols * PIN
        numbers = wide(small[::seq, at : at + 4 * images]).reshape(dp, 4, images).astype(jnp.int32)
        steps_all = (numbers[:, 0] * 32 + numbers[:, 1]).reshape(-1)
        labels_all = (numbers[:, 2] * 32 + numbers[:, 3]).reshape(-1)
        marks = [0, D, 2 * D, 3 * D, 11 * D, 12 * D, 13 * D, 14 * D, 14 * D + FF, 15 * D + FF]
        b_patch, b_time, b_cond, b_mod, b_query, b_value, b_proj, b_expand, b_reduce = [
            biases[marks[number] : marks[number + 1]] for number in range(9)
        ]

        attend_t = after(attend_t, small)
        received = []
        for turn in range(per):
            local = jnp.asarray(unit_send[turn])[me]
            received.append(
                lax.ppermute(
                    lax.dynamic_slice(attend_t, (local * unit, 0), (unit, D)),
                    AXES,
                    [(owner, int(unit_target[turn, owner])) for owner in range(devices)],
                )
            )
        both = jnp.concatenate(received + [to_low(square_t[:, 1])], 0)
        hidden_masks = [mask ^ far for mask in (0, 4, 2, 6) for far in masks_of(far_bits)]
        hidden_blocks = jnp.asarray(np.array(hidden_masks, np.int32)) ^ me
        hidden_pick = hidden_blocks[:, None] == jnp.arange(devices)[None, :]
        size = len(hidden_masks) * hidden_share // 4

        tables = place_tables(slots, widest)
        freq_in = to_low(time_freq(steps_all))

        def mine(vector, count):
            return lax.dynamic_slice(vector, (me * count,), (count,))[:, None]

        pre_time_all = contract(embed_time, freq_in, 1, 1) + b_time[:, None]
        hid_time = to_low(smooth_gate(pre_time_all))
        onehot = to_low(
            (labels_all[:, None] == jnp.arange(classes)[None, :]).astype(jnp.float32)
        )
        square_zero = to_low(square_t[:, 0])
        condition = (
            contract(square_zero, hid_time, 1, 0)
            + mine(b_cond, cols)
            + contract(table_t, onehot, 1, 1)
        )
        signal = signal_level(step_own)[:, None, None]
        latent = after(latent, hid_time)
        noisy_own = to_low(jnp.sqrt(signal) * latent + jnp.sqrt(1.0 - signal) * noise_in)
        noisy_own = noisy_own.reshape(tokens, PIN)
        noisy_all = gather_rows(noisy_own, seq_down)
        cond_own = to_low(smooth_gate(condition))
        both_first = gather_rows(after(both, hid_time), dp_bits[:1])
        both_second = gather_rows(after(both_first, cond_own), dp_bits[1:2])

        gathered = lax.all_gather(
            after(jnp.stack([expand_t, reduce_r]), both_second), AXES, axis=0
        )

        across_late = after(across, cond_own)
        block_of = jnp.asarray(np.array(slot_masks, np.int32)) ^ seq_index
        slot_ids = jnp.broadcast_to(
            block_of[:, None, None] * local_slots + jnp.arange(local_slots)[None, None, :],
            (seq, images, local_slots),
        ).reshape(-1)
        across_rows = jnp.broadcast_to(
            across_late[None, :, None], (seq, images, local_slots)
        ).reshape(-1)
        picks = place_picks(slot_ids, across_rows, slots, widest)
        stream_all = (
            contract(
                jnp.concatenate([picks] * 3 + [noisy_all], 1),
                jnp.concatenate(tables + [patch_t.T], 0),
                1,
                0,
            )
            + b_patch
        ).reshape(seq, images, local_slots, D)
        cond_act = after(share_all(cond_own), stream_all).reshape(D, all_images)
        mod_cols = contract(cond_act, shift_t, 0, 1) + mine(b_mod, shift_cols)[:, 0][None, :]
        mod_send = jnp.broadcast_to(
            mod_cols.reshape(dp, 1, images, shift_cols), (dp, seq, images, shift_cols)
        ).reshape(devices, images, shift_cols)
        unit_all, scale_all = standardize(after(stream_all, mod_cols))
        modulation = after(exchange(mod_send), scale_all)
        modulation = jnp.transpose(modulation, (1, 0, 2)).reshape(images, 8 * D)
        off_one, str_one, gate_one, off_two, str_two, gate_two, off_end, str_end = [
            modulation[:, number * D : (number + 1) * D] for number in range(8)
        ]

        both = gather_rows(after(both_second, mod_send), dp_bits[2:])
        my_rows = lax.dynamic_index_in_dim(jnp.asarray(row_table), me, 0, keepdims=False)
        place_units = to_low(
            (my_rows[:, None] == jnp.arange(3 * span)[None, :]).astype(jnp.float32)
        )
        attend_n = to_low(contract(both, place_units, 0, 0))
        normed_one = to_low(
            unit_all * (1.0 + str_one[None, :, None, :]) + off_one[None, :, None, :]
        ).reshape(all_tokens, D)
        stream_in = after(stream_all[0], normed_one)
        unit_one, scale_one = standardize(stream_in)

        def head_bias(vector):
            return lax.dynamic_slice(vector, (seq_index * span,), (span,))

        triple_bias = jnp.concatenate(
            [head_bias(b_query), jnp.zeros((span,), jnp.float32), head_bias(b_value)]
        )
        triple = to_low(contract(normed_one, attend_n, 1, 0) + triple_bias).reshape(
            seq, images, local_slots, 3 * span
        )
        proj_x = both.reshape(dp, per * unit + cols, D)[:, per * unit :].reshape(dp * cols, D)
        for bit in seq_down:
            proj_x = after(gather_rows(proj_x, [bit]), triple)
        slot_block = jnp.asarray(np.array(gather_masks(devices), np.int32)) ^ me
        source = slot_block[:, None] * cols + jnp.arange(cols)[None, :]
        place_proj = to_low(
            (source.reshape(-1)[:, None] == jnp.arange(D)[None, :]).astype(jnp.float32)
        )
        proj_n = to_low(contract(place_proj, proj_x, 0, 0))
        meta = jnp.concatenate([seq_index.reshape(1), used]).astype(jnp.int32)
        context = attend_call(slot_masks, meta, triple, bias_all, ())

        def over_seq(values_in):
            return lax.all_to_all(values_in, "seq", split_axis=0, concat_axis=0, tiled=True)

        merged = jnp.transpose(
            after(over_seq(context), (proj_n, stream_in)).reshape(seq, tokens, span), (1, 0, 2)
        ).reshape(tokens, D)
        attended = (contract(merged, proj_n, 1, 1) + b_proj).reshape(images, local_slots, D)
        stream_mid = stream_in + gate_one[:, None, :] * attended
        unit_two, scale_two = standardize(stream_mid)
        normed_own = to_low(stretch_shift(unit_two, off_two, str_two)).reshape(tokens, D)

        def pair_rows(rows):
            return jnp.concatenate([rows, swap(rows, 0)], 0)

        normed_two = pair_rows(normed_own)
        hidden_bias = jnp.sum(
            jnp.where(hidden_pick[:, :, None], b_expand.reshape(1, devices, hidden_share), 0.0), 1
        ).reshape(4, 1, size)
        if hidden_share % 16 == 0:
            hidden_index, weights = (hidden_blocks, gathered)
        else:
            weights = jnp.transpose(
                jnp.take(gathered, hidden_blocks, axis=0).reshape(4, -1, 2, hidden_share, D),
                (0, 2, 1, 3, 4),
            ).reshape(4, 2, size, D)
            hidden_index = jnp.arange(4, dtype=jnp.int32)
        upward, active, down_own, down_sent = hidden_call(
            forward_kernel, hidden_index, normed_two, hidden_bias, weights
        )
        downward = (down_own + wide(swap(down_sent, 0)) + b_reduce).reshape(images, local_slots, D)
        stream_out = stream_mid + gate_two[:, None, :] * downward
        unit_end, scale_end = standardize(stream_out)
        normed_end = to_low(stretch_shift(unit_end, off_end, str_end)).reshape(tokens, D)
        predicted = contract(normed_end, final_weight, 1, 0).reshape(images, local_slots, PIN)
        errors = predicted - noise_in
        kept = (seq_index * local_slots + jnp.arange(local_slots))[None, :] < used[:, None]
        kept = kept[:, :, None].astype(jnp.float32)
        loss_local = jnp.sum(kept * errors * errors)
        count_local = jnp.sum(kept) * PIN

        grad_pred = to_low(2.0 * kept * errors).reshape(tokens, PIN)
        grad_end = contract(grad_pred, final_weight, 1, 1).reshape(images, local_slots, D)
        grad_out, grad_off_end, grad_str_end = stretch_back(grad_end, unit_end, scale_end, str_end)
        grad_down_own = to_low(grad_out * gate_two[:, None, :]).reshape(tokens, D)
        grad_down = pair_rows(grad_down_own)
        grad_up, up_sums, two_own, two_sent = hidden_call(
            backward_kernel, hidden_index, grad_down, upward, weights
        )

        both_low, both_high, x_low, x_high, y_low, y_high, near = outer_call(
            grad_up, active, normed_two, grad_down
        )
        from_both_low, from_both_high = (swap(both_low, 1), swap(both_high, 2))
        from_x_high = swap(x_high, 2)
        grad_two = two_own + wide(after(swap(two_sent, 0), both_low))
        grad_two = grad_two.reshape(images, local_slots, D)
        grad_mid_norm, grad_off_two, grad_str_two = stretch_back(
            grad_two, unit_two, scale_two, str_two
        )
        grad_mid = grad_out + grad_mid_norm
        grad_att = to_low(grad_mid * gate_one[:, None, :]).reshape(tokens, D)
        grad_merged = to_low(contract(grad_att, proj_n, 1, 0))
        grad_merged = jnp.transpose(grad_merged.reshape(tokens, seq, span), (1, 0, 2))
        grad_att_x = to_low(contract(after(grad_att, grad_merged), place_proj, 1, 1))
        proj_parts = contract(grad_att_x, merged, 0, 0)
        x_low = to_low(after(x_low, grad_merged) + wide(from_both_low))
        y_high = to_low(after(y_high, grad_merged) + wide(from_both_high))
        from_x_low = swap(x_low, 2)
        proj_half = proj_parts.shape[0] // 2
        proj_sent = to_low(proj_parts[proj_half:])
        proj_parts = proj_parts[:proj_half] + wide(swap(proj_sent, 0))
        proj_half = proj_parts.shape[0] // 2
        proj_sent = to_low(proj_parts[proj_half:])
        proj_parts = proj_parts[:proj_half]
        from_proj = swap(proj_sent, 1)
        grad_context = after(over_seq(grad_merged), (proj_sent, x_low, y_high))
        grad_context = grad_context.reshape(seq, images, local_slots, span)

        grad_triple, triple_sums = attend_call(slot_masks, meta, triple, bias_all, (grad_context,))
        grad_triple = grad_triple.reshape(all_tokens, 3 * span)
        half = all_tokens // 2
        one_sent = to_low(contract(grad_triple[half:], attend_n, 1, 1))
        one_kept = contract(grad_triple[:half], attend_n, 1, 1)
        one_parts = one_kept + wide(swap(one_sent, 0))
        for bit in range(1, seq_bits):
            half = one_parts.shape[0] // 2
            one_last = to_low(one_parts[half:])
            one_came = swap(one_last, bit)
            if bit == seq_bits - 1:
                place_own = place_units.reshape(dp, -1, 3 * span)[:, : per * unit]
                place_own = place_own.reshape(dp * per * unit, 3 * span)
                grad_units = to_low(contract(after(grad_triple, one_last), place_own, 1, 1))
                middle = dp * per * unit // 2
                attend_sent = to_low(contract(grad_units[:, middle:], normed_one, 0, 0))
                attend_kept = contract(grad_units[:, :middle], normed_one, 0, 0)
                near_high = after(near, one_last)[:, size // 2 :] + wide(from_x_high)
                proj_parts = after(proj_parts, one_last) + wide(from_proj)
                from_y_high = swap(after(y_high, one_last), 1)
                from_y_low = swap(after(y_low, attend_sent), 1)
                one_came = after(one_came, (attend_sent, attend_kept, near_high))
            one_parts = one_parts[:half] + wide(one_came)
        grad_one = one_parts.reshape(images, local_slots, D)

        proj_parts = proj_parts.reshape(2, dp // 2, cols, D)

        def beside(attend_rows, proj_rows):
            attend_rows = attend_rows.reshape(dp // 2, per * unit, D)
            return jnp.concatenate([attend_rows, proj_rows], 1).reshape(-1, D)

        both_sent = beside(attend_sent, to_low(proj_parts[1]))
        both_parts = beside(attend_kept, proj_parts[0])
        both_half = both_parts.shape[0]
        from_both = swap(both_sent, dp_bits[-1])
        triple_sums = jnp.sum(triple_sums, 0).reshape(-1)

        grad_in_norm, grad_off_one, grad_str_one = stretch_back(
            grad_one, unit_one, scale_one, str_one
        )
        grad_in = to_low(grad_mid + grad_in_norm).reshape(tokens, D)

        grad_gate_one = jnp.sum(grad_mid * attended, 1)
        grad_gate_two = jnp.sum(grad_out * downward, 1)
        grad_mod_parts = jnp.concatenate(
            [
                grad_off_one,
                grad_str_one,
                grad_gate_one,
                grad_off_two,
                grad_str_two,
                grad_gate_two,
                grad_off_end,
                grad_str_end,
            ],
            -1,
        )
        grad_mod_sent = jnp.transpose(
            grad_mod_parts.reshape(images, devices, shift_cols), (1, 0, 2)
        )
        near_sent = to_low(after(near_high, grad_mod_sent) + wide(from_y_high))
        from_high = swap(near_sent, far_bits[-1])
        grad_mod = to_low(
            jnp.sum(
                after(exchange(grad_mod_sent), near_sent).reshape(dp, seq, images, shift_cols), 1
            )
        ).reshape(all_images, shift_cols)

        cond_parts = contract(shift_t, grad_mod, 0, 1).reshape(devices, cols, all_images)
        both_parts = after(both_parts, cond_parts) + wide(from_both)
        both_half = both_half // 2
        both_sent = to_low(both_parts[both_half:])
        from_both = swap(both_sent, dp_bits[-2])
        grad_shift = contract(after(grad_mod, cond_parts), cond_act, 0, 1)
        cond_came = after(exchange(cond_parts), (both_sent, grad_shift))
        grad_cond = to_low(smooth_gate_slope(condition) * jnp.sum(cond_came, 0))
        time_parts = contract(square_zero, grad_cond, 0, 0).reshape(devices, cols * all_images)

        grad_patch = contract(grad_in, noisy_own, 0, 0)
        grad_final = contract(normed_end, grad_pred, 0, 0)

        def heads_out(sums):
            return lax.dynamic_update_slice(
                jnp.zeros((D,), jnp.float32), sums, (seq_index * span,)
            )

        def spread_own(sums, length):
            return lax.dynamic_update_slice(
                jnp.zeros((length,), jnp.float32), sums, (me * sums.shape[0],)
            )

        up_nat = jnp.sum(
            jnp.where(hidden_pick[:, :, None], up_sums.reshape(-1, 1, hidden_share), 0.0), 0
        )
        bias_parts = jnp.concatenate(
            [
                jnp.sum(wide(grad_in), 0),
                jnp.zeros((D,), jnp.float32),
                spread_own(jnp.sum(wide(grad_cond), 1), D),
                spread_own(jnp.sum(wide(grad_mod), 0), 8 * D),
                heads_out(triple_sums[:span]),
                heads_out(triple_sums[2 * span :]),
                jnp.sum(wide(grad_att), 0),
                up_nat.reshape(-1),
                jnp.sum(wide(grad_down_own), 0),
            ]
        )
        mixed = jnp.concatenate(
            [
                time_parts,
                bias_parts.reshape(devices, bias_share),
                grad_patch.reshape(devices, cols * PIN),
                grad_final.reshape(devices, cols * PIN),
            ],
            1,
        )
        both_parts = after(both_parts[:both_half], mixed) + wide(from_both)
        both_half = both_half // 2
        both_sent = to_low(both_parts[both_half:])
        both_parts = both_parts[:both_half] + wide(swap(both_sent, dp_bits[-3]))
        near_low = after(near, time_parts)[:, : size // 2] + wide(from_x_low) + wide(from_y_low)
        near = near_low + wide(from_high)
        if len(far_bits) > 1:
            near_half = near.shape[1] // 2
            near_sent = to_low(near[:, near_half:])
            near = near[:, :near_half] + wide(swap(near_sent, far_bits[-2]))
        grad_table = contract(after(grad_cond, mixed), onehot, 1, 0)
        grad_time_two = contract(after(grad_cond, mixed), hid_time, 1, 1)
        mixed = after(exchange(mixed), (both_sent, near_sent, grad_table, grad_time_two))
        mixed = jnp.sum(mixed, 0)
        time_came, mixed = (mixed[: cols * all_images], mixed[cols * all_images :])
        grad_bias = mixed[:bias_share]
        grad_patch = mixed[bias_share : bias_share + cols * PIN].reshape(cols, PIN)
        grad_final = mixed[bias_share + cols * PIN :].reshape(cols, PIN)
        pre_time = lax.dynamic_slice(pre_time_all, (me * cols, 0), (cols, all_images))
        grad_pre = to_low(smooth_gate_slope(pre_time) * time_came.reshape(cols, all_images))
        time_sums = jnp.sum(wide(grad_pre), 1)
        near = fold_second(near, far_bits[:-2][::-1])
        grad_expand, grad_reduce = (near[0], near[1])
        both_parts = fold_rows(both_parts, dp_bits[:-3][::-1])
        grad_proj = both_parts[per * unit :]
        grad_time_one = contract(grad_pre, freq_in, 1, 0)

        grad_attend = jnp.zeros((per, unit, D), jnp.float32)
        for turn in range(per):
            piece = lax.ppermute(
                both_parts[turn * unit : (turn + 1) * unit],
                AXES,
                [(int(unit_target[turn, owner]), owner) for owner in range(devices)],
            )
            local = jnp.asarray(unit_send[turn])[me] == jnp.arange(per)
            grad_attend = jnp.where(local[:, None, None], piece[None], grad_attend)
        grad_attend = grad_attend.reshape(per * unit, D)

        grad_embed = jnp.concatenate([grad_patch, grad_time_one], 1)
        grad_square = jnp.stack([grad_time_two, grad_proj], 1)
        squares = sum(
            jnp.sum(piece * piece)
            for piece in (
                grad_patch,
                grad_time_one,
                grad_time_two,
                grad_proj,
                grad_table,
                grad_shift,
                grad_attend,
                grad_expand,
                grad_reduce,
                grad_final,
                grad_bias,
                time_sums,
            )
        )
        late = lax.dynamic_update_slice(
            jnp.zeros((devices * bias_share,), jnp.float32), time_sums, (D + me * cols,)
        ).reshape(devices, bias_share)
        numbers = jnp.stack([loss_local, count_local, squares])
        late = jnp.concatenate([late, jnp.broadcast_to(numbers[None], (devices, 3))], 1)
        late = jnp.sum(exchange(late), 0)
        loss_total, value_count, squared = [late[bias_share + number] for number in range(3)]
        grad_norm = jnp.sqrt(squared)
        factor = LIMIT / jnp.maximum(grad_norm, LIMIT)
        grad_bias = grad_bias + late[:bias_share]

        shards = (
            grad_embed.T,
            jnp.transpose(grad_square, (1, 2, 0)),
            grad_table.T,
            grad_shift.T,
            grad_attend.T,
            grad_expand.T,
            grad_reduce,
            grad_final,
            grad_bias,
        )
        results = [
            adam_step(params_in[number], firsts[number], seconds[number], shards[number], factor)
            for number in range(9)
        ]
        fresh = [results[number][part] for part in range(3) for number in range(9)]
        return tuple([loss_total, value_count, grad_norm] + fresh)

    return on_device


def adam_step(weight, moment, second, gradient, factor):
    clipped = gradient * factor
    moment = BETA_ONE * moment + (1.0 - BETA_ONE) * clipped
    second = BETA_TWO * second + (1.0 - BETA_TWO) * clipped * clipped
    fixed_one = moment / (1.0 - BETA_ONE**STEP)
    fixed_two = second / (1.0 - BETA_TWO**STEP)
    weight = weight - RATE * (fixed_one / (jnp.sqrt(fixed_two) + EPSILON) + DECAY * weight)
    return (weight, moment, second)


def solution(mesh):
    both = ("dp", "seq")
    state = (
        P(None, both),
        P(None, None, both),
        P(None, both),
        P(None, both),
        P(None, both),
        P(None, both),
        P(both, None),
        P(both, None),
        P(both),
    )
    batch = (
        P(None, "dp", "seq", None),
        P(None, "dp", "seq", None),
        P(None, "dp"),
        P(None, "dp"),
        P(None, "dp"),
        P(None, "dp"),
        P(None, "dp", "seq", None, None),
    )
    return jax.shard_map(
        make_step(mesh),
        mesh=mesh,
        in_specs=batch + state * 3,
        out_specs=(P(), P(), P()) + state * 3,
        check_vma=False,
    )
```

```python
import functools
import math

import jax
import jax.numpy as jnp
import numpy as np
from jax import lax
from jax.experimental import pallas as pl
from jax.experimental.pallas import tpu as pltpu
from jax.sharding import PartitionSpec as P

D = 1152
HEADS = 16
HEAD = 72
FF = 4608
FREQ = 256
PIN = 16
MICRO = 2
TSTEPS = 1000
STEP = 10
LANES = 128
AXES = ("dp", "seq")

BETA_ONE = 0.9
BETA_TWO = 0.95
EPSILON = 1e-08
DECAY = 0.1
RATE = 0.03
LIMIT = 1.0


def to_low(values_in):
    return values_in.astype(jnp.bfloat16)


def wide(values_in):
    return values_in.astype(jnp.float32)


def smooth_gate(values_in):
    return values_in * jax.nn.sigmoid(values_in)


def smooth_gate_slope(values_in):
    gate = jax.nn.sigmoid(values_in)
    return gate * (1.0 + values_in * (1.0 - gate))


def contract(left, right, left_dim, right_dim):
    return lax.dot_general(
        left,
        right,
        (((left_dim,), (right_dim,)), ((), ())),
        preferred_element_type=jnp.float32,
    )


def time_freq(steps_in):
    half_freq = FREQ // 2
    rate_table = jnp.exp(-math.log(10000.0) * jnp.arange(half_freq).astype(jnp.float32) / half_freq)
    angles = steps_in.astype(jnp.float32)[:, None] * rate_table[None, :]
    return jnp.concatenate([jnp.cos(angles), jnp.sin(angles)], -1)


def signal_level(steps_in):
    angles = (steps_in.astype(jnp.float32) / TSTEPS + 0.008) / 1.008 * (math.pi / 2)
    return jnp.cos(angles) * jnp.cos(angles)


def place_tables(slots, widest):
    quarter = D // 4
    lane = jnp.arange(D)
    rate = jnp.exp(-math.log(10000.0) * (lane % quarter).astype(jnp.float32) / quarter)
    fine = 16
    coarse = -(-slots // fine)
    steps = jnp.concatenate(
        [jnp.arange(coarse, dtype=jnp.float32) * fine, jnp.arange(fine, dtype=jnp.float32)]
    )
    angles = steps[:, None] * rate[None, :]
    sines, cosines = (jnp.sin(angles), jnp.cos(angles))
    sine_high, sine_low = (sines[:coarse, None], sines[None, coarse:])
    cosine_high, cosine_low = (cosines[:coarse, None], cosines[None, coarse:])
    table = jnp.where(
        lane // quarter % 2 == 0,
        sine_high * cosine_low + cosine_high * sine_low,
        cosine_high * cosine_low - sine_high * sine_low,
    ).reshape(coarse * fine, D)
    by_row = lane < 2 * quarter
    table = jnp.concatenate(
        [jnp.where(by_row, table[:slots], 0.0), jnp.where(by_row, 0.0, table[:widest])], 0
    )
    part_one = to_low(table)
    rest = table - wide(part_one)
    part_two = to_low(rest)
    part_three = to_low(rest - wide(part_two))
    return [part_one, part_two, part_three]


def place_picks(slot_ids, across, slots, widest):
    row_pos = (slot_ids // across)[:, None]
    col_pos = (slot_ids % across)[:, None] + slots
    spots = jnp.arange(slots + widest)[None, :]
    return to_low(((row_pos == spots) | (col_pos == spots)).astype(jnp.float32))


def after(values_in, earlier):
    return lax.optimization_barrier((values_in, earlier))[0]


def standardize(stream):
    centred = stream - jnp.mean(stream, -1, keepdims=True)
    scale = lax.rsqrt(jnp.mean(centred * centred, -1, keepdims=True) + 1e-06)
    return (centred * scale, scale)


def stretch_shift(unit, offset, stretch):
    return unit * (1.0 + stretch[:, None, :]) + offset[:, None, :]


def stretch_back(grad, unit, scale, stretch):
    grad_offset = jnp.sum(grad, 1)
    grad_stretch = jnp.sum(grad * unit, 1)
    grad_unit = grad * (1.0 + stretch[:, None, :])
    grad_stream = scale * (
        grad_unit
        - jnp.mean(grad_unit, -1, keepdims=True)
        - unit * jnp.mean(grad_unit * unit, -1, keepdims=True)
    )
    return (grad_stream, grad_offset, grad_stretch)


CUBE = 0.044715
ROOT = 0.7978845608028654


def gaussian_unit(values_in):
    inner = ROOT * (values_in + CUBE * values_in * values_in * values_in)
    return 0.5 * values_in * (1.0 + jnp.tanh(inner))


def gaussian_slope(values_in):
    inner = ROOT * (values_in + CUBE * values_in * values_in * values_in)
    bend = jnp.tanh(inner)
    return 0.5 * (1.0 + bend) + 0.5 * values_in * (1.0 - bend * bend) * ROOT * (
        1.0 + 3.0 * CUBE * values_in * values_in
    )


def attend_probs(nat_ref, bias_ref, head, own, keep):
    width = own * HEAD
    queries = nat_ref[:, head * HEAD : (head + 1) * HEAD]
    keys = nat_ref[:, width + head * HEAD : width + (head + 1) * HEAD]
    values = nat_ref[:, 2 * width + head * HEAD : 2 * width + (head + 1) * HEAD]
    scores = contract(queries, keys, 1, 1) * HEAD ** (-0.5) + wide(bias_ref[0, head])
    scores = jnp.where(keep, scores, -1e30)
    powers = jnp.exp(scores - jnp.max(scores, -1, keepdims=True))
    probs = powers * (1.0 / jnp.sum(powers, -1, keepdims=True))
    return (queries, keys, values, probs)


def attend_enter(meta_ref, triple_ref, nat_ref, masks):
    block = triple_ref.shape[2]
    for number, mask in enumerate(masks):
        first = pl.multiple_of((meta_ref[0] ^ mask) * block, 16)
        nat_ref[pl.ds(first, block), :] = triple_ref[number, 0]
    slots = nat_ref.shape[0]
    local = lax.broadcasted_iota(jnp.int32, (slots, slots), 1)
    return local < meta_ref[1 + pl.program_id(0)]


def attend_kernel(masks, meta_ref, triple_ref, bias_ref, context_ref, nat_ref):
    keep = attend_enter(meta_ref, triple_ref, nat_ref, masks)
    own, block = (bias_ref.shape[1], triple_ref.shape[2])
    mixed = []
    for head in range(own):
        _, _, values, probs = attend_probs(nat_ref, bias_ref, head, own, keep)
        mixed.append(to_low(contract(to_low(probs), values, 1, 0)))
    context = jnp.concatenate(mixed, 1)
    for number in range(len(masks)):
        context_ref[number, 0] = context[number * block : (number + 1) * block]


def attend_back_kernel(
    masks, meta_ref, triple_ref, bias_ref, grad_ref, out_ref, sums_ref, nat_ref, back_ref
):
    keep = attend_enter(meta_ref, triple_ref, nat_ref, masks)
    own, block = (bias_ref.shape[1], triple_ref.shape[2])
    width = own * HEAD
    grads = jnp.concatenate([grad_ref[number, 0] for number in range(len(masks))], 0)
    for head in range(own):
        queries, keys, values, probs = attend_probs(nat_ref, bias_ref, head, own, keep)
        grad_context = grads[:, head * HEAD : (head + 1) * HEAD]
        grad_probs = contract(grad_context, values, 1, 1)
        weighted = probs * grad_probs
        grad_scores = to_low(weighted - probs * jnp.sum(weighted, -1, keepdims=True))
        pieces = (
            contract(grad_scores, keys, 1, 0) * HEAD ** (-0.5),
            contract(grad_scores, queries, 0, 0) * HEAD ** (-0.5),
            contract(to_low(probs), grad_context, 0, 0),
        )
        for kind in range(3):
            begin = kind * width + head * HEAD
            back_ref[:, begin : begin + HEAD] = to_low(pieces[kind])
    sums_ref[0] = jnp.sum(wide(back_ref[...]), 0, keepdims=True)
    for number, mask in enumerate(masks):
        first = pl.multiple_of((meta_ref[0] ^ mask) * block, 16)
        out_ref[number, 0] = back_ref[pl.ds(first, block), :]


def attend_call(masks, meta, triple, bias_tiles, grads):
    images, own, slots, _ = bias_tiles.shape
    count, _, block, full = triple.shape
    width = own * HEAD
    backward = len(grads) > 0
    row = lambda image, meta_ref: (0, image, 0, 0)
    tri_spec = pl.BlockSpec((count, 1, block, full), row)
    slim_spec = pl.BlockSpec((count, 1, block, width), row)
    in_specs = [
        tri_spec,
        pl.BlockSpec((1, own, slots, slots), lambda image, meta_ref: (image, 0, 0, 0)),
    ] + [slim_spec] * len(grads)
    nat = pltpu.VMEM((slots, full), jnp.bfloat16)
    if backward:
        kernel, products = (attend_back_kernel, 6)
        out_shape = (
            jax.ShapeDtypeStruct(triple.shape, jnp.bfloat16),
            jax.ShapeDtypeStruct((images, 1, full), jnp.float32),
        )
        out_specs = (tri_spec, pl.BlockSpec((1, 1, full), lambda image, meta_ref: (image, 0, 0)))
        scratch = [nat, nat]
    else:
        kernel, products = (attend_kernel, 2)
        out_shape = jax.ShapeDtypeStruct((count, images, block, width), jnp.bfloat16)
        out_specs = slim_spec
        scratch = [nat]
    return pl.pallas_call(
        functools.partial(kernel, masks),
        out_shape=out_shape,
        grid_spec=pltpu.PrefetchScalarGridSpec(
            num_scalar_prefetch=1,
            grid=(images,),
            in_specs=in_specs,
            out_specs=out_specs,
            scratch_shapes=scratch,
        ),
        compiler_params=pltpu.CompilerParams(vmem_limit_bytes=40 * 2**20),
        cost_estimate=pl.CostEstimate(flops=1000, bytes_accessed=1000, transcendentals=0),
    )(meta, triple, bias_tiles, *grads)


PARTS = 3


def weight_copies(pick_ref, weight_ref, kind, held_ref, sem_ref):
    rows = weight_ref.shape[2]
    part = held_ref.shape[0] // PARTS
    copies = []
    for number in range(held_ref.shape[0] // rows):
        copies.append(
            (
                number * rows // part,
                pltpu.make_async_copy(
                    weight_ref.at[pick_ref[number], kind],
                    held_ref.at[pl.ds(number * rows, rows)],
                    sem_ref.at[kind, number],
                ),
            )
        )
    return copies


def held_part(held_ref):
    part = held_ref.shape[0] // PARTS
    return held_ref[pl.ds(pl.multiple_of(pl.program_id(0) * part, part), part), :]


def start_copies(groups):
    @pl.when(pl.program_id(0) == 0)
    def _():
        for copies in groups:
            for _, copy in copies:
                copy.start()


def wait_copies(copies):
    for quarter in range(PARTS):

        @pl.when(pl.program_id(0) == quarter)
        def _():
            for number, copy in copies:
                if number == quarter:
                    copy.wait()


def put_pair(total, own_ref, sent_ref):
    rows = own_ref.shape[0]

    @pl.when(pl.program_id(0) == pl.num_programs(0) - 1)
    def _():
        own_ref[...] = total[:rows]
        sent_ref[...] = to_low(total[rows:])


def add_up(total_ref, product):
    @pl.when(pl.program_id(0) == 0)
    def _():
        total_ref[...] = product

    @pl.when(pl.program_id(0) > 0)
    def _():
        total_ref[...] += product


def forward_kernel(
    pick_ref,
    normed_ref,
    bias_ref,
    weight_ref,
    up_ref,
    active_ref,
    own_ref,
    sent_ref,
    expand_held,
    reduce_held,
    total_ref,
    sem_ref,
):
    expand_copies = weight_copies(pick_ref, weight_ref, 0, expand_held, sem_ref)
    reduce_copies = weight_copies(pick_ref, weight_ref, 1, reduce_held, sem_ref)
    start_copies([expand_copies, reduce_copies])
    wait_copies(expand_copies)
    upward = contract(normed_ref[...], held_part(expand_held), 1, 1) + bias_ref[0]
    up_ref[0] = upward
    active = to_low(gaussian_unit(upward))
    active_ref[0] = active
    wait_copies(reduce_copies)
    add_up(total_ref, contract(active, held_part(reduce_held), 1, 0))
    put_pair(total_ref, own_ref, sent_ref)


def backward_kernel(
    pick_ref,
    grad_ref,
    up_ref,
    weight_ref,
    out_ref,
    sums_ref,
    own_ref,
    sent_ref,
    expand_held,
    reduce_held,
    total_ref,
    sem_ref,
):
    expand_copies = weight_copies(pick_ref, weight_ref, 0, expand_held, sem_ref)
    reduce_copies = weight_copies(pick_ref, weight_ref, 1, reduce_held, sem_ref)
    start_copies([reduce_copies, expand_copies])
    wait_copies(reduce_copies)
    grad_active = contract(grad_ref[...], held_part(reduce_held), 1, 1)
    grad_up = to_low(gaussian_slope(up_ref[0]) * grad_active)
    out_ref[0] = grad_up
    sums_ref[0] = jnp.sum(wide(grad_up), 0, keepdims=True)
    wait_copies(expand_copies)
    add_up(total_ref, contract(grad_up, held_part(expand_held), 1, 0))
    put_pair(total_ref, own_ref, sent_ref)


def hidden_call(kernel, pick, left, second, weights):
    rows = left.shape[0]
    size = second.shape[2]
    whole = pl.BlockSpec((rows, D), lambda quarter, pick_ref: (0, 0))
    slab = pl.BlockSpec((1, rows, size), lambda quarter, pick_ref: (quarter, 0, 0))
    line = pl.BlockSpec((1, 1, size), lambda quarter, pick_ref: (quarter, 0, 0))
    half = pl.BlockSpec((rows // 2, D), lambda quarter, pick_ref: (0, 0))
    if kernel is forward_kernel:
        second_spec, out_specs = (line, (slab, slab, half, half))
        kinds = (((PARTS, rows, size), jnp.float32), ((PARTS, rows, size), jnp.bfloat16))
    else:
        second_spec, out_specs = (slab, (slab, line, half, half))
        kinds = (((PARTS, rows, size), jnp.bfloat16), ((PARTS, 1, size), jnp.float32))
    kinds = kinds + (((rows // 2, D), jnp.float32), ((rows // 2, D), jnp.bfloat16))
    return pl.pallas_call(
        kernel,
        out_shape=tuple(jax.ShapeDtypeStruct(shape, kind) for shape, kind in kinds),
        grid_spec=pltpu.PrefetchScalarGridSpec(
            num_scalar_prefetch=1,
            grid=(PARTS,),
            in_specs=[whole, second_spec, pl.BlockSpec(memory_space=pl.ANY)],
            out_specs=out_specs,
            scratch_shapes=[
                pltpu.VMEM((PARTS * size, D), jnp.bfloat16),
                pltpu.VMEM((PARTS * size, D), jnp.bfloat16),
                pltpu.VMEM((rows, D), jnp.float32),
                pltpu.SemaphoreType.DMA((2, PARTS * size // weights.shape[2])),
            ],
        ),
        compiler_params=pltpu.CompilerParams(vmem_limit_bytes=56 * 2**20),
        cost_estimate=pl.CostEstimate(flops=1000, bytes_accessed=1000, transcendentals=0),
    )(pick, left, second, weights)


def piece_ranges(total):
    eighth = total // 8
    marks = [(6, 7), (7, 8), (2, 3), (3, 4), (4, 5), (5, 6), (0, 2)]
    return [(first * eighth, last * eighth) for first, last in marks]


def outer_kernel(grad_up_ref, active_ref, normed_ref, grad_ref, *refs):
    outs, held, sem_ref = (refs[:7], refs[7:14], refs[14])
    part = grad_up_ref.shape[2]
    products = (
        contract(grad_up_ref[0], normed_ref[...], 0, 0),
        contract(active_ref[0], grad_ref[...], 0, 0),
    )
    copies = [pltpu.make_async_copy(held[at], outs[at], sem_ref.at[at]) for at in range(7)]
    ranges = piece_ranges(PARTS * part)
    for turn in range(PARTS):
        begin = (PARTS - 1 - turn) * part

        @pl.when(pl.program_id(0) == turn)
        def _():
            for at, (first, last) in enumerate(ranges):
                low, high = (max(first, begin), min(last, begin + part))
                for kind in range(2):
                    if low < high:
                        value = products[kind][low - begin : high - begin]
                        held[at][kind, low - first : high - first] = value.astype(held[at].dtype)
                if begin <= first < begin + part:
                    copies[at].start()

    @pl.when(pl.program_id(0) == PARTS - 1)
    def _():
        for copy in copies:
            copy.wait()


def outer_call(grad_up, active, normed, grad_down):
    _, rows, part = grad_up.shape
    low, full = (jnp.bfloat16, jnp.float32)
    kinds = (low, low, full, low, low, full, full)
    shapes = [
        ((2, last - first, D), kind)
        for (first, last), kind in zip(piece_ranges(PARTS * part), kinds)
    ]
    slab = pl.BlockSpec((1, rows, part), lambda step: (PARTS - 1 - step, 0, 0))
    whole = pl.BlockSpec((rows, D), lambda step: (0, 0))
    return pl.pallas_call(
        outer_kernel,
        out_shape=tuple(jax.ShapeDtypeStruct(shape, kind) for shape, kind in shapes),
        grid=(PARTS,),
        in_specs=[slab, slab, whole, whole],
        out_specs=tuple([pl.BlockSpec(memory_space=pl.ANY)] * 7),
        scratch_shapes=[pltpu.VMEM(shape, kind) for shape, kind in shapes]
        + [pltpu.SemaphoreType.DMA((7,))],
        compiler_params=pltpu.CompilerParams(vmem_limit_bytes=56 * 2**20),
        cost_estimate=pl.CostEstimate(flops=1000, bytes_accessed=1000, transcendentals=0),
    )(grad_up, active, normed, grad_down)


def unit_plan(devices, seq):
    share = 3 * D // devices
    unit = math.gcd(math.gcd(share, D // seq), HEAD)
    per = share // unit
    span = D // seq

    def group_of(number):
        return (number * unit % D) // span

    left = [{local: group_of(owner * per + local) for local in range(per)} for owner in range(devices)]
    send = np.zeros((per, devices), np.int32)
    target = np.zeros((per, devices), np.int32)
    held = np.zeros((per, devices), np.int32)
    for turn in range(per):
        match = [-1] * devices

        def seek(owner, seen):
            groups = set(left[owner].values())
            near = sorted(
                (place for place in range(devices) if place % seq in groups),
                key=lambda place: (place != owner, place // seq != owner // seq, place ^ owner),
            )
            for place in near:
                if place in seen:
                    continue
                seen.add(place)
                if match[place] < 0 or seek(match[place], seen):
                    match[place] = owner
                    return True
            return False

        for owner in range(devices):
            assert seek(owner, set())
        for place, owner in enumerate(match):
            local = next(item for item, group in left[owner].items() if group == place % seq)
            del left[owner][local]
            send[turn, owner] = local
            target[turn, owner] = place
            held[turn, place] = owner * per + local
    return (unit, per, send, target, held)


def unit_rows(devices, seq, unit, per, held):
    dp = devices // seq
    span = D // seq
    extra = D // devices
    rows = np.full((devices, dp * (per * unit + extra)), -1, np.int32)
    for place in range(devices):
        at = 0
        for mask in gather_masks(dp):
            for turn in range(per):
                first = int(held[turn, place ^ (mask * seq)]) * unit
                kind, inside = (first // D, first % D)
                begin = kind * span + inside - span * (place % seq)
                rows[place, at : at + unit] = np.arange(begin, begin + unit)
                at += unit
            at += extra
    return rows


def gather_masks(dp):
    masks = [0]
    bit = dp >> 1
    while bit:
        masks = masks + [item ^ bit for item in masks]
        bit >>= 1
    return masks


def make_step(mesh):
    dp, seq = (mesh.shape["dp"], mesh.shape["seq"])
    devices = dp * seq
    top = devices.bit_length() - 1
    seq_bits = seq.bit_length() - 1
    own_heads = HEADS // seq
    span = D // seq
    unit, per, unit_send, unit_target, unit_held = unit_plan(devices, seq)
    row_table = unit_rows(devices, seq, unit, per, unit_held)
    cols = D // devices
    shift_cols = 8 * D // devices
    hidden_share = FF // devices
    bias_share = (15 * D + FF) // devices
    dp_bits = list(range(top - 1, seq_bits - 1, -1))
    far_bits = list(range(top - 1, 2, -1))
    seq_down = list(range(seq_bits - 1, -1, -1))

    def masks_of(bits):
        masks = [0]
        for bit in bits:
            masks = masks + [mask ^ (1 << bit) for mask in masks]
        return masks

    slot_masks = masks_of(seq_down)

    def swap(values_in, bit):
        return lax.ppermute(
            values_in, AXES, [(place, place ^ (1 << bit)) for place in range(devices)]
        )

    def exchange(values_in):
        return lax.all_to_all(values_in, AXES, split_axis=0, concat_axis=0, tiled=True)

    def share_all(block):
        return exchange(jnp.broadcast_to(block[None], (devices,) + block.shape))

    def gather_rows(rows, bits):
        for bit in bits:
            rows = jnp.concatenate([rows, swap(rows, bit)], 0)
        return rows

    def fold_rows(rows, bits):
        for bit in bits:
            half = rows.shape[0] // 2
            rows = rows[:half] + wide(swap(to_low(rows[half:]), bit))
        return rows

    def fold_second(rows, bits):
        for bit in bits:
            half = rows.shape[1] // 2
            rows = rows[:, :half] + wide(swap(to_low(rows[:, half:]), bit))
        return rows

    def on_device(
        latents,
        noise_draw,
        heights,
        widths,
        labels,
        timesteps,
        bias_tiles,
        *states,
    ):
        params_in, firsts, seconds = (states[:9], states[9:18], states[18:])
        seq_index = lax.axis_index("seq")
        me = lax.axis_index("dp") * seq + seq_index
        local_slots = latents.shape[2]
        slots = local_slots * seq
        widest = min(slots, 32)
        images = latents.shape[0] * latents.shape[1]
        classes = params_in[2].shape[0]
        tokens = images * local_slots
        all_tokens = images * slots
        all_images = images * dp
        latent = latents.reshape(images, local_slots, PIN)
        noise_in = noise_draw.reshape(images, local_slots, PIN)
        height, across = (heights.reshape(images), widths.reshape(images))
        label_own, step_own = (labels.reshape(images), timesteps.reshape(images))
        bias_all = bias_tiles.reshape(images, own_heads, slots, slots)
        used = height * across

        embed_t = params_in[0].T
        square_t = jnp.transpose(params_in[1], (2, 0, 1))
        table_t = to_low(params_in[2].T)
        shift_t = to_low(params_in[3].T)
        attend_t = to_low(params_in[4].T)
        expand_t = to_low(params_in[5].T)
        reduce_r = to_low(params_in[6])

        small = jnp.concatenate(
            [to_low(params_in[8]), to_low(embed_t[:, :PIN]).reshape(-1), to_low(params_in[7]).reshape(-1)]
            + [
                to_low(wide(piece))
                for piece in (step_own // 32, step_own % 32, label_own // 32, label_own % 32)
            ]
        )
        length = -(-small.shape[0] // 2048) * 2048
        small = jnp.pad(small, (0, length - small.shape[0])).reshape(-1, LANES)
        embed_own = to_low(embed_t[:, PIN:]).reshape(-1, LANES)
        small = share_all(jnp.concatenate([small, embed_own], 0))
        embed_time = small[:, length // LANES :].reshape(D, FREQ)
        small = small[:, : length // LANES].reshape(devices, length)
        at = bias_share
        biases = wide(small[:, :at].reshape(-1))
        patch_t = small[:, at : at + cols * PIN].reshape(D, PIN)
        at = at + cols * PIN
        final_weight = small[:, at : at + cols * PIN].reshape(D, PIN)
        at = at + cols * PIN
        numbers = wide(small[::seq, at : at + 4 * images]).reshape(dp, 4, images).astype(jnp.int32)
        steps_all = (numbers[:, 0] * 32 + numbers[:, 1]).reshape(-1)
        labels_all = (numbers[:, 2] * 32 + numbers[:, 3]).reshape(-1)
        marks = [0, D, 2 * D, 3 * D, 11 * D, 12 * D, 13 * D, 14 * D, 14 * D + FF, 15 * D + FF]
        b_patch, b_time, b_cond, b_mod, b_query, b_value, b_proj, b_expand, b_reduce = [
            biases[marks[number] : marks[number + 1]] for number in range(9)
        ]

        attend_t = after(attend_t, small)
        received = []
        for turn in range(per):
            local = jnp.asarray(unit_send[turn])[me]
            received.append(
                lax.ppermute(
                    lax.dynamic_slice(attend_t, (local * unit, 0), (unit, D)),
                    AXES,
                    [(owner, int(unit_target[turn, owner])) for owner in range(devices)],
                )
            )
        both = jnp.concatenate(received + [to_low(square_t[:, 1])], 0)
        hidden_masks = [mask ^ far for mask in (0, 4, 2, 6) for far in masks_of(far_bits)]
        hidden_blocks = jnp.asarray(np.array(hidden_masks, np.int32)) ^ me
        hidden_pick = hidden_blocks[:, None] == jnp.arange(devices)[None, :]
        size = len(hidden_masks) * hidden_share // 4

        tables = place_tables(slots, widest)
        freq_in = to_low(time_freq(steps_all))

        def mine(vector, count):
            return lax.dynamic_slice(vector, (me * count,), (count,))[:, None]

        pre_time_all = contract(embed_time, freq_in, 1, 1) + b_time[:, None]
        hid_time = to_low(smooth_gate(pre_time_all))
        onehot = to_low(
            (labels_all[:, None] == jnp.arange(classes)[None, :]).astype(jnp.float32)
        )
        square_zero = to_low(square_t[:, 0])
        condition = (
            contract(square_zero, hid_time, 1, 0)
            + mine(b_cond, cols)
            + contract(table_t, onehot, 1, 1)
        )
        signal = signal_level(step_own)[:, None, None]
        latent = after(latent, hid_time)
        noisy_own = to_low(jnp.sqrt(signal) * latent + jnp.sqrt(1.0 - signal) * noise_in)
        noisy_own = noisy_own.reshape(tokens, PIN)
        noisy_all = gather_rows(noisy_own, seq_down)
        cond_own = to_low(smooth_gate(condition))
        both_first = gather_rows(after(both, hid_time), dp_bits[:1])
        both_second = gather_rows(after(both_first, cond_own), dp_bits[1:2])

        gathered = lax.all_gather(
            after(jnp.stack([expand_t, reduce_r]), both_second), AXES, axis=0
        )

        across_late = after(across, cond_own)
        block_of = jnp.asarray(np.array(slot_masks, np.int32)) ^ seq_index
        slot_ids = jnp.broadcast_to(
            block_of[:, None, None] * local_slots + jnp.arange(local_slots)[None, None, :],
            (seq, images, local_slots),
        ).reshape(-1)
        across_rows = jnp.broadcast_to(
            across_late[None, :, None], (seq, images, local_slots)
        ).reshape(-1)
        picks = place_picks(slot_ids, across_rows, slots, widest)
        stream_all = (
            contract(
                jnp.concatenate([picks] * 3 + [noisy_all], 1),
                jnp.concatenate(tables + [patch_t.T], 0),
                1,
                0,
            )
            + b_patch
        ).reshape(seq, images, local_slots, D)
        cond_act = after(share_all(cond_own), stream_all).reshape(D, all_images)
        mod_cols = contract(cond_act, shift_t, 0, 1) + mine(b_mod, shift_cols)[:, 0][None, :]
        mod_send = jnp.broadcast_to(
            mod_cols.reshape(dp, 1, images, shift_cols), (dp, seq, images, shift_cols)
        ).reshape(devices, images, shift_cols)
        unit_all, scale_all = standardize(after(stream_all, mod_cols))
        modulation = after(exchange(mod_send), scale_all)
        modulation = jnp.transpose(modulation, (1, 0, 2)).reshape(images, 8 * D)
        off_one, str_one, gate_one, off_two, str_two, gate_two, off_end, str_end = [
            modulation[:, number * D : (number + 1) * D] for number in range(8)
        ]

        both = gather_rows(after(both_second, mod_send), dp_bits[2:])
        my_rows = lax.dynamic_index_in_dim(jnp.asarray(row_table), me, 0, keepdims=False)
        place_units = to_low(
            (my_rows[:, None] == jnp.arange(3 * span)[None, :]).astype(jnp.float32)
        )
        attend_n = to_low(contract(both, place_units, 0, 0))
        normed_one = to_low(
            unit_all * (1.0 + str_one[None, :, None, :]) + off_one[None, :, None, :]
        ).reshape(all_tokens, D)
        stream_in = after(stream_all[0], normed_one)
        unit_one, scale_one = standardize(stream_in)

        def head_bias(vector):
            return lax.dynamic_slice(vector, (seq_index * span,), (span,))

        triple_bias = jnp.concatenate(
            [head_bias(b_query), jnp.zeros((span,), jnp.float32), head_bias(b_value)]
        )
        triple = to_low(contract(normed_one, attend_n, 1, 0) + triple_bias).reshape(
            seq, images, local_slots, 3 * span
        )
        meta = jnp.concatenate([seq_index.reshape(1), used]).astype(jnp.int32)
        context = attend_call(slot_masks, meta, triple, bias_all, ())

        proj_x = both.reshape(dp, per * unit + cols, D)[:, per * unit :].reshape(dp * cols, D)
        for bit in seq_down:
            proj_x = after(gather_rows(proj_x, [bit]), context)
        slot_block = jnp.asarray(np.array(gather_masks(devices), np.int32)) ^ me
        source = slot_block[:, None] * cols + jnp.arange(cols)[None, :]
        place_proj = to_low(
            (source.reshape(-1)[:, None] == jnp.arange(D)[None, :]).astype(jnp.float32)
        )
        proj_n = to_low(contract(place_proj, proj_x, 0, 0))

        def over_seq(values_in):
            return lax.all_to_all(values_in, "seq", split_axis=0, concat_axis=0, tiled=True)

        merged = jnp.transpose(
            after(over_seq(context), (proj_n, stream_in)).reshape(seq, tokens, span), (1, 0, 2)
        ).reshape(tokens, D)
        attended = (contract(merged, proj_n, 1, 1) + b_proj).reshape(images, local_slots, D)
        stream_mid = stream_in + gate_one[:, None, :] * attended
        unit_two, scale_two = standardize(stream_mid)
        normed_own = to_low(stretch_shift(unit_two, off_two, str_two)).reshape(tokens, D)

        def pair_rows(rows):
            return jnp.concatenate([rows, swap(rows, 0)], 0)

        normed_two = pair_rows(normed_own)
        hidden_bias = jnp.sum(
            jnp.where(hidden_pick[:, :, None], b_expand.reshape(1, devices, hidden_share), 0.0), 1
        ).reshape(PARTS, 1, 4 * size // PARTS)
        if hidden_share % 16 == 0:
            hidden_index, weights = (hidden_blocks, gathered)
        else:
            weights = jnp.transpose(
                jnp.take(gathered, hidden_blocks, axis=0).reshape(4, -1, 2, hidden_share, D),
                (0, 2, 1, 3, 4),
            ).reshape(4, 2, size, D)
            hidden_index = jnp.arange(4, dtype=jnp.int32)
        upward, active, down_own, down_sent = hidden_call(
            forward_kernel, hidden_index, normed_two, hidden_bias, weights
        )
        downward = (down_own + wide(swap(down_sent, 0)) + b_reduce).reshape(images, local_slots, D)
        stream_out = stream_mid + gate_two[:, None, :] * downward
        unit_end, scale_end = standardize(stream_out)
        normed_end = to_low(stretch_shift(unit_end, off_end, str_end)).reshape(tokens, D)
        predicted = contract(normed_end, final_weight, 1, 0).reshape(images, local_slots, PIN)
        errors = predicted - noise_in
        kept = (seq_index * local_slots + jnp.arange(local_slots))[None, :] < used[:, None]
        kept = kept[:, :, None].astype(jnp.float32)
        loss_local = jnp.sum(kept * errors * errors)
        count_local = jnp.sum(kept) * PIN

        grad_pred = to_low(2.0 * kept * errors).reshape(tokens, PIN)
        grad_end = contract(grad_pred, final_weight, 1, 1).reshape(images, local_slots, D)
        grad_out, grad_off_end, grad_str_end = stretch_back(grad_end, unit_end, scale_end, str_end)
        grad_down_own = to_low(grad_out * gate_two[:, None, :]).reshape(tokens, D)
        grad_down = pair_rows(grad_down_own)
        grad_up, up_sums, two_own, two_sent = hidden_call(
            backward_kernel, hidden_index, grad_down, upward, weights
        )

        both_low, both_high, x_low, x_high, y_low, y_high, near = outer_call(
            grad_up, active, normed_two, grad_down
        )
        from_both_low, from_both_high = (swap(both_low, 1), swap(both_high, 2))
        from_x_high = swap(x_high, 2)
        grad_two = two_own + wide(after(swap(two_sent, 0), both_low))
        grad_two = grad_two.reshape(images, local_slots, D)
        grad_mid_norm, grad_off_two, grad_str_two = stretch_back(
            grad_two, unit_two, scale_two, str_two
        )
        grad_mid = grad_out + grad_mid_norm
        grad_att = to_low(grad_mid * gate_one[:, None, :]).reshape(tokens, D)
        grad_merged = to_low(contract(grad_att, proj_n, 1, 0))
        grad_merged = jnp.transpose(grad_merged.reshape(tokens, seq, span), (1, 0, 2))
        grad_att_x = to_low(contract(after(grad_att, grad_merged), place_proj, 1, 1))
        proj_parts = contract(grad_att_x, merged, 0, 0)
        x_low = to_low(after(x_low, grad_merged) + wide(from_both_low))
        y_high = to_low(after(y_high, grad_merged) + wide(from_both_high))
        from_x_low, from_y_high = (swap(x_low, 2), swap(y_high, 1))
        proj_half = proj_parts.shape[0] // 2
        proj_sent = to_low(proj_parts[proj_half:])
        proj_parts = proj_parts[:proj_half] + wide(swap(proj_sent, 0))
        proj_half = proj_parts.shape[0] // 2
        proj_sent = to_low(proj_parts[proj_half:])
        proj_parts = proj_parts[:proj_half]
        from_proj = swap(proj_sent, 1)
        grad_context = after(over_seq(grad_merged), (proj_sent, x_low, y_high))
        grad_context = grad_context.reshape(seq, images, local_slots, span)

        grad_triple, triple_sums = attend_call(slot_masks, meta, triple, bias_all, (grad_context,))
        grad_triple = grad_triple.reshape(all_tokens, 3 * span)
        half = all_tokens // 2
        one_sent = to_low(contract(grad_triple[half:], attend_n, 1, 1))
        one_kept = contract(grad_triple[:half], attend_n, 1, 1)
        one_parts = one_kept + wide(swap(one_sent, 0))
        for bit in range(1, seq_bits):
            half = one_parts.shape[0] // 2
            if bit == seq_bits - 1:
                near_high = after(near, one_sent)[:, size // 2 :]
                near_sent = to_low(near_high + wide(from_x_high) + wide(from_y_high))
                from_high = swap(near_sent, far_bits[-1])
                one_parts = after(one_parts, near_sent)
            one_last = to_low(one_parts[half:])
            one_came = swap(one_last, bit)
            if bit == seq_bits - 1:
                place_own = place_units.reshape(dp, -1, 3 * span)[:, : per * unit]
                place_own = place_own.reshape(dp * per * unit, 3 * span)
                grad_units = to_low(contract(after(grad_triple, one_last), place_own, 1, 1))
                middle = dp * per * unit // 2
                attend_sent = to_low(contract(grad_units[:, middle:], normed_one, 0, 0))
                attend_kept = contract(grad_units[:, :middle], normed_one, 0, 0)
                proj_parts = proj_parts + wide(after(from_proj, attend_sent))
                from_y_low = swap(after(y_low, one_last), 1)
                one_came = after(one_came, (attend_sent, attend_kept))
            one_parts = one_parts[:half] + wide(one_came)
        grad_one = one_parts.reshape(images, local_slots, D)

        proj_parts = proj_parts.reshape(2, dp // 2, cols, D)

        def beside(attend_rows, proj_rows):
            attend_rows = attend_rows.reshape(dp // 2, per * unit, D)
            return jnp.concatenate([attend_rows, proj_rows], 1).reshape(-1, D)

        both_sent = beside(attend_sent, to_low(proj_parts[1]))
        both_parts = beside(attend_kept, proj_parts[0])
        both_half = both_parts.shape[0]
        triple_sums = jnp.sum(triple_sums, 0).reshape(-1)

        grad_in_norm, grad_off_one, grad_str_one = stretch_back(
            grad_one, unit_one, scale_one, str_one
        )
        grad_in = to_low(grad_mid + grad_in_norm).reshape(tokens, D)

        grad_gate_one = jnp.sum(grad_mid * attended, 1)
        grad_gate_two = jnp.sum(grad_out * downward, 1)
        grad_mod_parts = jnp.concatenate(
            [
                grad_off_one,
                grad_str_one,
                grad_gate_one,
                grad_off_two,
                grad_str_two,
                grad_gate_two,
                grad_off_end,
                grad_str_end,
            ],
            -1,
        )
        grad_mod_sent = jnp.transpose(
            grad_mod_parts.reshape(images, devices, shift_cols), (1, 0, 2)
        )
        grad_patch = contract(grad_in, noisy_own, 0, 0)
        grad_final = contract(normed_end, grad_pred, 0, 0)

        def heads_out(sums):
            return lax.dynamic_update_slice(
                jnp.zeros((D,), jnp.float32), sums, (seq_index * span,)
            )

        up_nat = jnp.sum(
            jnp.where(hidden_pick[:, :, None], up_sums.reshape(-1, 1, hidden_share), 0.0), 0
        )
        bias_parts = jnp.concatenate(
            [
                jnp.sum(wide(grad_in), 0),
                jnp.zeros((10 * D,), jnp.float32),
                heads_out(triple_sums[:span]),
                heads_out(triple_sums[2 * span :]),
                jnp.sum(wide(grad_att), 0),
                up_nat.reshape(-1),
                jnp.sum(wide(grad_down_own), 0),
            ]
        ).reshape(devices, bias_share)
        from_both = swap(after(both_sent, grad_mod_sent), dp_bits[-1])
        grad_mod = to_low(
            jnp.sum(
                after(exchange(grad_mod_sent), bias_parts).reshape(dp, seq, images, shift_cols), 1
            )
        ).reshape(all_images, shift_cols)

        cond_parts = contract(shift_t, grad_mod, 0, 1).reshape(devices, cols, all_images)
        both_parts = after(both_parts, cond_parts) + wide(from_both)
        both_half = both_half // 2
        both_sent = to_low(both_parts[both_half:])
        from_both = swap(both_sent, dp_bits[-2])
        near_low = after(near, both_sent)[:, : size // 2] + wide(from_x_low) + wide(from_y_low)
        near = near_low + wide(from_high)
        if len(far_bits) > 1:
            near_half = near.shape[1] // 2
            near_sent = to_low(near[:, near_half:])
            near_kept = near[:, :near_half]
        grad_shift = contract(after(grad_mod, cond_parts), cond_act, 0, 1)
        cond_came = after(exchange(cond_parts), (near_sent, grad_shift))
        grad_cond = to_low(smooth_gate_slope(condition) * jnp.sum(cond_came, 0))
        time_parts = contract(square_zero, grad_cond, 0, 0).reshape(devices, cols * all_images)

        mixed = jnp.concatenate(
            [
                time_parts,
                bias_parts,
                grad_patch.reshape(devices, cols * PIN),
                grad_final.reshape(devices, cols * PIN),
            ],
            1,
        )
        both_parts = after(both_parts[:both_half], mixed) + wide(from_both)
        both_half = both_half // 2
        both_sent = to_low(both_parts[both_half:])
        both_parts = both_parts[:both_half] + wide(swap(both_sent, dp_bits[-3]))
        if len(far_bits) > 1:
            near_came = swap(after(near_sent, both_sent), far_bits[-2])
        grad_table = contract(after(grad_cond, mixed), onehot, 1, 0)
        grad_time_two = contract(after(grad_cond, mixed), hid_time, 1, 1)
        mixed = after(exchange(mixed), (both_sent, grad_table, grad_time_two))
        mixed = jnp.sum(mixed, 0)
        time_came, mixed = (mixed[: cols * all_images], mixed[cols * all_images :])
        grad_bias = mixed[:bias_share]
        grad_patch = mixed[bias_share : bias_share + cols * PIN].reshape(cols, PIN)
        grad_final = mixed[bias_share + cols * PIN :].reshape(cols, PIN)
        pre_time = lax.dynamic_slice(pre_time_all, (me * cols, 0), (cols, all_images))
        grad_pre = to_low(smooth_gate_slope(pre_time) * time_came.reshape(cols, all_images))
        time_sums = jnp.sum(wide(grad_pre), 1)
        cond_sums = jnp.sum(wide(after(grad_cond, mixed)), 1)
        mod_sums = jnp.sum(wide(after(grad_mod, mixed)), 0)
        if len(far_bits) > 1:
            near = near_kept + wide(after(near_came, grad_pre))
        near = fold_second(near, far_bits[:-2][::-1])
        grad_expand, grad_reduce = (near[0], near[1])
        both_parts = fold_rows(both_parts, dp_bits[:-3][::-1])
        grad_proj = both_parts[per * unit :]
        grad_time_one = contract(grad_pre, freq_in, 1, 0)

        grad_attend = jnp.zeros((per, unit, D), jnp.float32)
        for turn in range(per):
            piece = lax.ppermute(
                both_parts[turn * unit : (turn + 1) * unit],
                AXES,
                [(int(unit_target[turn, owner]), owner) for owner in range(devices)],
            )
            local = jnp.asarray(unit_send[turn])[me] == jnp.arange(per)
            grad_attend = jnp.where(local[:, None, None], piece[None], grad_attend)
        grad_attend = grad_attend.reshape(per * unit, D)

        grad_embed = jnp.concatenate([grad_patch, grad_time_one], 1)
        grad_square = jnp.stack([grad_time_two, grad_proj], 1)
        squares = sum(
            jnp.sum(piece * piece)
            for piece in (
                grad_patch,
                grad_time_one,
                grad_time_two,
                grad_proj,
                grad_table,
                grad_shift,
                grad_attend,
                grad_expand,
                grad_reduce,
                grad_final,
                grad_bias,
                time_sums,
                cond_sums,
                mod_sums,
            )
        )
        late = jnp.zeros((devices * bias_share,), jnp.float32)
        for sums, first in ((time_sums, D), (cond_sums, 2 * D), (mod_sums, 3 * D)):
            late = lax.dynamic_update_slice(late, sums, (first + me * sums.shape[0],))
        late = late.reshape(devices, bias_share)
        numbers = jnp.stack([loss_local, count_local, squares])
        late = jnp.concatenate([late, jnp.broadcast_to(numbers[None], (devices, 3))], 1)
        late = jnp.sum(exchange(late), 0)
        loss_total, value_count, squared = [late[bias_share + number] for number in range(3)]
        grad_norm = jnp.sqrt(squared)
        factor = LIMIT / jnp.maximum(grad_norm, LIMIT)
        grad_bias = grad_bias + late[:bias_share]

        shards = (
            grad_embed.T,
            jnp.transpose(grad_square, (1, 2, 0)),
            grad_table.T,
            grad_shift.T,
            grad_attend.T,
            grad_expand.T,
            grad_reduce,
            grad_final,
            grad_bias,
        )
        results = [
            adam_step(params_in[number], firsts[number], seconds[number], shards[number], factor)
            for number in range(9)
        ]
        fresh = [results[number][part] for part in range(3) for number in range(9)]
        return tuple([loss_total, value_count, grad_norm] + fresh)

    return on_device


def adam_step(weight, moment, second, gradient, factor):
    clipped = gradient * factor
    moment = BETA_ONE * moment + (1.0 - BETA_ONE) * clipped
    second = BETA_TWO * second + (1.0 - BETA_TWO) * clipped * clipped
    fixed_one = moment / (1.0 - BETA_ONE**STEP)
    fixed_two = second / (1.0 - BETA_TWO**STEP)
    weight = weight - RATE * (fixed_one / (jnp.sqrt(fixed_two) + EPSILON) + DECAY * weight)
    return (weight, moment, second)


def solution(mesh):
    both = ("dp", "seq")
    state = (
        P(None, both),
        P(None, None, both),
        P(None, both),
        P(None, both),
        P(None, both),
        P(None, both),
        P(both, None),
        P(both, None),
        P(both),
    )
    batch = (
        P(None, "dp", "seq", None),
        P(None, "dp", "seq", None),
        P(None, "dp"),
        P(None, "dp"),
        P(None, "dp"),
        P(None, "dp"),
        P(None, "dp", "seq", None, None),
    )
    return jax.shard_map(
        make_step(mesh),
        mesh=mesh,
        in_specs=batch + state * 3,
        out_specs=(P(), P(), P()) + state * 3,
        check_vma=False,
    )
```

```python
import functools
import math

import jax
import jax.numpy as jnp
import numpy as np
from jax import lax
from jax.experimental import pallas as pl
from jax.experimental.pallas import tpu as pltpu
from jax.sharding import PartitionSpec as P

D = 1152
HEADS = 16
HEAD = 72
FF = 4608
FREQ = 256
PIN = 16
MICRO = 2
TSTEPS = 1000
STEP = 10
LANES = 128
AXES = ("dp", "seq")

BETA_ONE = 0.9
BETA_TWO = 0.95
EPSILON = 1e-08
DECAY = 0.1
RATE = 0.03
LIMIT = 1.0


def to_low(values_in):
    return values_in.astype(jnp.bfloat16)


def wide(values_in):
    return values_in.astype(jnp.float32)


def smooth_gate(values_in):
    return values_in * jax.nn.sigmoid(values_in)


def smooth_gate_slope(values_in):
    gate = jax.nn.sigmoid(values_in)
    return gate * (1.0 + values_in * (1.0 - gate))


def contract(left, right, left_dim, right_dim):
    return lax.dot_general(
        left,
        right,
        (((left_dim,), (right_dim,)), ((), ())),
        preferred_element_type=jnp.float32,
    )


def time_freq(steps_in):
    half_freq = FREQ // 2
    rate_table = jnp.exp(-math.log(10000.0) * jnp.arange(half_freq).astype(jnp.float32) / half_freq)
    angles = steps_in.astype(jnp.float32)[:, None] * rate_table[None, :]
    return jnp.concatenate([jnp.cos(angles), jnp.sin(angles)], -1)


def signal_level(steps_in):
    angles = (steps_in.astype(jnp.float32) / TSTEPS + 0.008) / 1.008 * (math.pi / 2)
    return jnp.cos(angles) * jnp.cos(angles)


def place_tables(slots, widest):
    quarter = D // 4
    lane = jnp.arange(D)
    rate = jnp.exp(-math.log(10000.0) * (lane % quarter).astype(jnp.float32) / quarter)
    fine = 16
    coarse = -(-slots // fine)
    steps = jnp.concatenate(
        [jnp.arange(coarse, dtype=jnp.float32) * fine, jnp.arange(fine, dtype=jnp.float32)]
    )
    angles = steps[:, None] * rate[None, :]
    sines, cosines = (jnp.sin(angles), jnp.cos(angles))
    sine_high, sine_low = (sines[:coarse, None], sines[None, coarse:])
    cosine_high, cosine_low = (cosines[:coarse, None], cosines[None, coarse:])
    table = jnp.where(
        lane // quarter % 2 == 0,
        sine_high * cosine_low + cosine_high * sine_low,
        cosine_high * cosine_low - sine_high * sine_low,
    ).reshape(coarse * fine, D)
    by_row = lane < 2 * quarter
    table = jnp.concatenate(
        [jnp.where(by_row, table[:slots], 0.0), jnp.where(by_row, 0.0, table[:widest])], 0
    )
    part_one = to_low(table)
    rest = table - wide(part_one)
    part_two = to_low(rest)
    part_three = to_low(rest - wide(part_two))
    return [part_one, part_two, part_three]


def place_picks(slot_ids, across, slots, widest):
    row_pos = (slot_ids // across)[:, None]
    col_pos = (slot_ids % across)[:, None] + slots
    spots = jnp.arange(slots + widest)[None, :]
    return to_low(((row_pos == spots) | (col_pos == spots)).astype(jnp.float32))


def after(values_in, earlier):
    return lax.optimization_barrier((values_in, earlier))[0]


def standardize(stream):
    centred = stream - jnp.mean(stream, -1, keepdims=True)
    scale = lax.rsqrt(jnp.mean(centred * centred, -1, keepdims=True) + 1e-06)
    return (centred * scale, scale)


def stretch_shift(unit, offset, stretch):
    return unit * (1.0 + stretch[:, None, :]) + offset[:, None, :]


def stretch_back(grad, unit, scale, stretch):
    grad_offset = jnp.sum(grad, 1)
    grad_stretch = jnp.sum(grad * unit, 1)
    grad_unit = grad * (1.0 + stretch[:, None, :])
    grad_stream = scale * (
        grad_unit
        - jnp.mean(grad_unit, -1, keepdims=True)
        - unit * jnp.mean(grad_unit * unit, -1, keepdims=True)
    )
    return (grad_stream, grad_offset, grad_stretch)


CUBE = 0.044715
ROOT = 0.7978845608028654


def gaussian_unit(values_in):
    inner = ROOT * (values_in + CUBE * values_in * values_in * values_in)
    return 0.5 * values_in * (1.0 + jnp.tanh(inner))


def gaussian_slope(values_in):
    inner = ROOT * (values_in + CUBE * values_in * values_in * values_in)
    bend = jnp.tanh(inner)
    return 0.5 * (1.0 + bend) + 0.5 * values_in * (1.0 - bend * bend) * ROOT * (
        1.0 + 3.0 * CUBE * values_in * values_in
    )


def attend_probs(nat_ref, bias_ref, head, own, keep):
    width = own * HEAD
    queries = nat_ref[:, head * HEAD : (head + 1) * HEAD]
    keys = nat_ref[:, width + head * HEAD : width + (head + 1) * HEAD]
    values = nat_ref[:, 2 * width + head * HEAD : 2 * width + (head + 1) * HEAD]
    scores = contract(queries, keys, 1, 1) * HEAD ** (-0.5) + wide(bias_ref[0, head])
    scores = jnp.where(keep, scores, -1e30)
    powers = jnp.exp(scores - jnp.max(scores, -1, keepdims=True))
    probs = powers * (1.0 / jnp.sum(powers, -1, keepdims=True))
    return (queries, keys, values, probs)


def attend_enter(meta_ref, triple_ref, nat_ref, masks):
    block = triple_ref.shape[2]
    for number, mask in enumerate(masks):
        first = pl.multiple_of((meta_ref[0] ^ mask) * block, 16)
        nat_ref[pl.ds(first, block), :] = triple_ref[number, 0]
    slots = nat_ref.shape[0]
    local = lax.broadcasted_iota(jnp.int32, (slots, slots), 1)
    return local < meta_ref[1 + pl.program_id(0)]


def attend_kernel(masks, meta_ref, triple_ref, bias_ref, context_ref, nat_ref):
    keep = attend_enter(meta_ref, triple_ref, nat_ref, masks)
    own, block = (bias_ref.shape[1], triple_ref.shape[2])
    mixed = []
    for head in range(own):
        _, _, values, probs = attend_probs(nat_ref, bias_ref, head, own, keep)
        mixed.append(to_low(contract(to_low(probs), values, 1, 0)))
    context = jnp.concatenate(mixed, 1)
    for number in range(len(masks)):
        context_ref[number, 0] = context[number * block : (number + 1) * block]


def attend_back_kernel(
    masks, meta_ref, triple_ref, bias_ref, grad_ref, out_ref, sums_ref, nat_ref, back_ref
):
    keep = attend_enter(meta_ref, triple_ref, nat_ref, masks)
    own, block = (bias_ref.shape[1], triple_ref.shape[2])
    width = own * HEAD
    grads = jnp.concatenate([grad_ref[number, 0] for number in range(len(masks))], 0)
    for head in range(own):
        queries, keys, values, probs = attend_probs(nat_ref, bias_ref, head, own, keep)
        grad_context = grads[:, head * HEAD : (head + 1) * HEAD]
        grad_probs = contract(grad_context, values, 1, 1)
        weighted = probs * grad_probs
        grad_scores = to_low(weighted - probs * jnp.sum(weighted, -1, keepdims=True))
        pieces = (
            contract(grad_scores, keys, 1, 0) * HEAD ** (-0.5),
            contract(grad_scores, queries, 0, 0) * HEAD ** (-0.5),
            contract(to_low(probs), grad_context, 0, 0),
        )
        for kind in range(3):
            begin = kind * width + head * HEAD
            back_ref[:, begin : begin + HEAD] = to_low(pieces[kind])
    sums_ref[0] = jnp.sum(wide(back_ref[...]), 0, keepdims=True)
    for number, mask in enumerate(masks):
        first = pl.multiple_of((meta_ref[0] ^ mask) * block, 16)
        out_ref[number, 0] = back_ref[pl.ds(first, block), :]


def attend_call(masks, meta, triple, bias_tiles, grads):
    images, own, slots, _ = bias_tiles.shape
    count, _, block, full = triple.shape
    width = own * HEAD
    backward = len(grads) > 0
    row = lambda image, meta_ref: (0, image, 0, 0)
    tri_spec = pl.BlockSpec((count, 1, block, full), row)
    slim_spec = pl.BlockSpec((count, 1, block, width), row)
    in_specs = [
        tri_spec,
        pl.BlockSpec((1, own, slots, slots), lambda image, meta_ref: (image, 0, 0, 0)),
    ] + [slim_spec] * len(grads)
    nat = pltpu.VMEM((slots, full), jnp.bfloat16)
    if backward:
        kernel, products = (attend_back_kernel, 6)
        out_shape = (
            jax.ShapeDtypeStruct(triple.shape, jnp.bfloat16),
            jax.ShapeDtypeStruct((images, 1, full), jnp.float32),
        )
        out_specs = (tri_spec, pl.BlockSpec((1, 1, full), lambda image, meta_ref: (image, 0, 0)))
        scratch = [nat, nat]
    else:
        kernel, products = (attend_kernel, 2)
        out_shape = jax.ShapeDtypeStruct((count, images, block, width), jnp.bfloat16)
        out_specs = slim_spec
        scratch = [nat]
    return pl.pallas_call(
        functools.partial(kernel, masks),
        out_shape=out_shape,
        grid_spec=pltpu.PrefetchScalarGridSpec(
            num_scalar_prefetch=1,
            grid=(images,),
            in_specs=in_specs,
            out_specs=out_specs,
            scratch_shapes=scratch,
        ),
        compiler_params=pltpu.CompilerParams(vmem_limit_bytes=40 * 2**20),
        cost_estimate=pl.CostEstimate(flops=1000, bytes_accessed=1000, transcendentals=0),
    )(meta, triple, bias_tiles, *grads)


PARTS = 3


def weight_copies(pick_ref, weight_ref, kind, held_ref, sem_ref):
    rows = weight_ref.shape[2]
    part = held_ref.shape[0] // PARTS
    copies = []
    for number in range(held_ref.shape[0] // rows):
        copies.append(
            (
                number * rows // part,
                pltpu.make_async_copy(
                    weight_ref.at[pick_ref[number], kind],
                    held_ref.at[pl.ds(number * rows, rows)],
                    sem_ref.at[kind, number],
                ),
            )
        )
    return copies


def held_part(held_ref):
    part = held_ref.shape[0] // PARTS
    return held_ref[pl.ds(pl.multiple_of(pl.program_id(0) * part, part), part), :]


def start_copies(groups):
    @pl.when(pl.program_id(0) == 0)
    def _():
        for copies in groups:
            for _, copy in copies:
                copy.start()


def wait_copies(copies):
    for quarter in range(PARTS):

        @pl.when(pl.program_id(0) == quarter)
        def _():
            for number, copy in copies:
                if number == quarter:
                    copy.wait()


def put_pair(total, own_ref, sent_ref):
    rows = own_ref.shape[0]

    @pl.when(pl.program_id(0) == pl.num_programs(0) - 1)
    def _():
        own_ref[...] = total[:rows]
        sent_ref[...] = to_low(total[rows:])


def add_up(total_ref, product):
    @pl.when(pl.program_id(0) == 0)
    def _():
        total_ref[...] = product

    @pl.when(pl.program_id(0) > 0)
    def _():
        total_ref[...] += product


def forward_kernel(
    pick_ref,
    normed_ref,
    bias_ref,
    weight_ref,
    up_ref,
    active_ref,
    own_ref,
    sent_ref,
    expand_held,
    reduce_held,
    total_ref,
    sem_ref,
):
    expand_copies = weight_copies(pick_ref, weight_ref, 0, expand_held, sem_ref)
    reduce_copies = weight_copies(pick_ref, weight_ref, 1, reduce_held, sem_ref)
    start_copies([expand_copies, reduce_copies])
    wait_copies(expand_copies)
    upward = contract(normed_ref[...], held_part(expand_held), 1, 1) + bias_ref[0]
    up_ref[0] = upward
    active = to_low(gaussian_unit(upward))
    active_ref[0] = active
    wait_copies(reduce_copies)
    add_up(total_ref, contract(active, held_part(reduce_held), 1, 0))
    put_pair(total_ref, own_ref, sent_ref)


def backward_kernel(
    pick_ref,
    grad_ref,
    up_ref,
    weight_ref,
    out_ref,
    sums_ref,
    own_ref,
    sent_ref,
    expand_held,
    reduce_held,
    total_ref,
    sem_ref,
):
    expand_copies = weight_copies(pick_ref, weight_ref, 0, expand_held, sem_ref)
    reduce_copies = weight_copies(pick_ref, weight_ref, 1, reduce_held, sem_ref)
    start_copies([reduce_copies, expand_copies])
    wait_copies(reduce_copies)
    grad_active = contract(grad_ref[...], held_part(reduce_held), 1, 1)
    grad_up = to_low(gaussian_slope(up_ref[0]) * grad_active)
    out_ref[0] = grad_up
    sums_ref[0] = jnp.sum(wide(grad_up), 0, keepdims=True)
    wait_copies(expand_copies)
    add_up(total_ref, contract(grad_up, held_part(expand_held), 1, 0))
    put_pair(total_ref, own_ref, sent_ref)


def hidden_call(kernel, pick, left, second, weights):
    rows = left.shape[0]
    size = second.shape[2]
    whole = pl.BlockSpec((rows, D), lambda quarter, pick_ref: (0, 0))
    slab = pl.BlockSpec((1, rows, size), lambda quarter, pick_ref: (quarter, 0, 0))
    line = pl.BlockSpec((1, 1, size), lambda quarter, pick_ref: (quarter, 0, 0))
    half = pl.BlockSpec((rows // 2, D), lambda quarter, pick_ref: (0, 0))
    if kernel is forward_kernel:
        second_spec, out_specs = (line, (slab, slab, half, half))
        kinds = (((PARTS, rows, size), jnp.float32), ((PARTS, rows, size), jnp.bfloat16))
    else:
        second_spec, out_specs = (slab, (slab, line, half, half))
        kinds = (((PARTS, rows, size), jnp.bfloat16), ((PARTS, 1, size), jnp.float32))
    kinds = kinds + (((rows // 2, D), jnp.float32), ((rows // 2, D), jnp.bfloat16))
    return pl.pallas_call(
        kernel,
        out_shape=tuple(jax.ShapeDtypeStruct(shape, kind) for shape, kind in kinds),
        grid_spec=pltpu.PrefetchScalarGridSpec(
            num_scalar_prefetch=1,
            grid=(PARTS,),
            in_specs=[whole, second_spec, pl.BlockSpec(memory_space=pl.ANY)],
            out_specs=out_specs,
            scratch_shapes=[
                pltpu.VMEM((PARTS * size, D), jnp.bfloat16),
                pltpu.VMEM((PARTS * size, D), jnp.bfloat16),
                pltpu.VMEM((rows, D), jnp.float32),
                pltpu.SemaphoreType.DMA((2, PARTS * size // weights.shape[2])),
            ],
        ),
        compiler_params=pltpu.CompilerParams(vmem_limit_bytes=56 * 2**20),
        cost_estimate=pl.CostEstimate(flops=1000, bytes_accessed=1000, transcendentals=0),
    )(pick, left, second, weights)


def piece_ranges(total):
    eighth = total // 8
    marks = [(6, 7), (7, 8), (2, 3), (3, 4), (4, 5), (5, 6), (0, 2)]
    return [(first * eighth, last * eighth) for first, last in marks]


def outer_kernel(grad_up_ref, active_ref, normed_ref, grad_ref, *refs):
    outs, held, sem_ref = (refs[:7], refs[7:14], refs[14])
    part = grad_up_ref.shape[2]
    products = (
        contract(grad_up_ref[0], normed_ref[...], 0, 0),
        contract(active_ref[0], grad_ref[...], 0, 0),
    )
    copies = [pltpu.make_async_copy(held[at], outs[at], sem_ref.at[at]) for at in range(7)]
    ranges = piece_ranges(PARTS * part)
    for turn in range(PARTS):
        begin = (PARTS - 1 - turn) * part

        @pl.when(pl.program_id(0) == turn)
        def _():
            for at, (first, last) in enumerate(ranges):
                low, high = (max(first, begin), min(last, begin + part))
                for kind in range(2):
                    if low < high:
                        value = products[kind][low - begin : high - begin]
                        held[at][kind, low - first : high - first] = value.astype(held[at].dtype)
                if begin <= first < begin + part:
                    copies[at].start()

    @pl.when(pl.program_id(0) == PARTS - 1)
    def _():
        for copy in copies:
            copy.wait()


def outer_call(grad_up, active, normed, grad_down):
    _, rows, part = grad_up.shape
    low, full = (jnp.bfloat16, jnp.float32)
    kinds = (low, low, full, low, low, full, full)
    shapes = [
        ((2, last - first, D), kind)
        for (first, last), kind in zip(piece_ranges(PARTS * part), kinds)
    ]
    slab = pl.BlockSpec((1, rows, part), lambda step: (PARTS - 1 - step, 0, 0))
    whole = pl.BlockSpec((rows, D), lambda step: (0, 0))
    return pl.pallas_call(
        outer_kernel,
        out_shape=tuple(jax.ShapeDtypeStruct(shape, kind) for shape, kind in shapes),
        grid=(PARTS,),
        in_specs=[slab, slab, whole, whole],
        out_specs=tuple([pl.BlockSpec(memory_space=pl.ANY)] * 7),
        scratch_shapes=[pltpu.VMEM(shape, kind) for shape, kind in shapes]
        + [pltpu.SemaphoreType.DMA((7,))],
        compiler_params=pltpu.CompilerParams(vmem_limit_bytes=56 * 2**20),
        cost_estimate=pl.CostEstimate(flops=1000, bytes_accessed=1000, transcendentals=0),
    )(grad_up, active, normed, grad_down)


def unit_plan(devices, seq):
    share = 3 * D // devices
    unit = math.gcd(math.gcd(share, D // seq), HEAD)
    per = share // unit
    span = D // seq

    def group_of(number):
        return (number * unit % D) // span

    left = [{local: group_of(owner * per + local) for local in range(per)} for owner in range(devices)]
    send = np.zeros((per, devices), np.int32)
    target = np.zeros((per, devices), np.int32)
    held = np.zeros((per, devices), np.int32)
    for turn in range(per):
        match = [-1] * devices

        def seek(owner, seen):
            groups = set(left[owner].values())
            near = sorted(
                (place for place in range(devices) if place % seq in groups),
                key=lambda place: (place != owner, place // seq != owner // seq, place ^ owner),
            )
            for place in near:
                if place in seen:
                    continue
                seen.add(place)
                if match[place] < 0 or seek(match[place], seen):
                    match[place] = owner
                    return True
            return False

        for owner in range(devices):
            assert seek(owner, set())
        for place, owner in enumerate(match):
            local = next(item for item, group in left[owner].items() if group == place % seq)
            del left[owner][local]
            send[turn, owner] = local
            target[turn, owner] = place
            held[turn, place] = owner * per + local
    return (unit, per, send, target, held)


def unit_rows(devices, seq, unit, per, held):
    dp = devices // seq
    span = D // seq
    extra = D // devices
    rows = np.full((devices, dp * (per * unit + extra)), -1, np.int32)
    for place in range(devices):
        at = 0
        for mask in gather_masks(dp):
            for turn in range(per):
                first = int(held[turn, place ^ (mask * seq)]) * unit
                kind, inside = (first // D, first % D)
                begin = kind * span + inside - span * (place % seq)
                rows[place, at : at + unit] = np.arange(begin, begin + unit)
                at += unit
            at += extra
    return rows


def gather_masks(dp):
    masks = [0]
    bit = dp >> 1
    while bit:
        masks = masks + [item ^ bit for item in masks]
        bit >>= 1
    return masks


def make_step(mesh):
    dp, seq = (mesh.shape["dp"], mesh.shape["seq"])
    devices = dp * seq
    top = devices.bit_length() - 1
    seq_bits = seq.bit_length() - 1
    own_heads = HEADS // seq
    span = D // seq
    unit, per, unit_send, unit_target, unit_held = unit_plan(devices, seq)
    row_table = unit_rows(devices, seq, unit, per, unit_held)
    cols = D // devices
    shift_cols = 8 * D // devices
    hidden_share = FF // devices
    bias_share = (15 * D + FF) // devices
    dp_bits = list(range(top - 1, seq_bits - 1, -1))
    far_bits = list(range(top - 1, 2, -1))
    seq_down = list(range(seq_bits - 1, -1, -1))

    def masks_of(bits):
        masks = [0]
        for bit in bits:
            masks = masks + [mask ^ (1 << bit) for mask in masks]
        return masks

    slot_masks = masks_of(seq_down)

    def swap(values_in, bit):
        return lax.ppermute(
            values_in, AXES, [(place, place ^ (1 << bit)) for place in range(devices)]
        )

    def exchange(values_in):
        return lax.all_to_all(values_in, AXES, split_axis=0, concat_axis=0, tiled=True)

    def share_all(block):
        return exchange(jnp.broadcast_to(block[None], (devices,) + block.shape))

    def gather_rows(rows, bits):
        for bit in bits:
            rows = jnp.concatenate([rows, swap(rows, bit)], 0)
        return rows

    def fold_rows(rows, bits):
        for bit in bits:
            half = rows.shape[0] // 2
            rows = rows[:half] + wide(swap(to_low(rows[half:]), bit))
        return rows

    def fold_second(rows, bits):
        for bit in bits:
            half = rows.shape[1] // 2
            rows = rows[:, :half] + wide(swap(to_low(rows[:, half:]), bit))
        return rows

    def on_device(
        latents,
        noise_draw,
        heights,
        widths,
        labels,
        timesteps,
        bias_tiles,
        *states,
    ):
        params_in, firsts, seconds = (states[:9], states[9:18], states[18:])
        seq_index = lax.axis_index("seq")
        me = lax.axis_index("dp") * seq + seq_index
        local_slots = latents.shape[2]
        slots = local_slots * seq
        widest = min(slots, 32)
        images = latents.shape[0] * latents.shape[1]
        classes = params_in[2].shape[0]
        tokens = images * local_slots
        all_tokens = images * slots
        all_images = images * dp
        latent = latents.reshape(images, local_slots, PIN)
        noise_in = noise_draw.reshape(images, local_slots, PIN)
        height, across = (heights.reshape(images), widths.reshape(images))
        label_own, step_own = (labels.reshape(images), timesteps.reshape(images))
        bias_all = bias_tiles.reshape(images, own_heads, slots, slots)
        used = height * across

        embed_t = params_in[0].T
        square_t = jnp.transpose(params_in[1], (2, 0, 1))
        table_t = to_low(params_in[2].T)
        shift_t = to_low(params_in[3].T)
        attend_t = to_low(params_in[4].T)
        expand_t = to_low(params_in[5].T)
        reduce_r = to_low(params_in[6])

        small = jnp.concatenate(
            [to_low(params_in[8]), to_low(embed_t[:, :PIN]).reshape(-1), to_low(params_in[7]).reshape(-1)]
            + [
                to_low(wide(piece))
                for piece in (step_own // 32, step_own % 32, label_own // 32, label_own % 32)
            ]
        )
        length = -(-small.shape[0] // 2048) * 2048
        small = jnp.pad(small, (0, length - small.shape[0])).reshape(-1, LANES)
        embed_own = to_low(embed_t[:, PIN:]).reshape(-1, LANES)
        small = share_all(jnp.concatenate([small, embed_own], 0))
        embed_time = small[:, length // LANES :].reshape(D, FREQ)
        small = small[:, : length // LANES].reshape(devices, length)
        at = bias_share
        biases = wide(small[:, :at].reshape(-1))
        patch_t = small[:, at : at + cols * PIN].reshape(D, PIN)
        at = at + cols * PIN
        final_weight = small[:, at : at + cols * PIN].reshape(D, PIN)
        at = at + cols * PIN
        numbers = wide(small[::seq, at : at + 4 * images]).reshape(dp, 4, images).astype(jnp.int32)
        steps_all = (numbers[:, 0] * 32 + numbers[:, 1]).reshape(-1)
        labels_all = (numbers[:, 2] * 32 + numbers[:, 3]).reshape(-1)
        marks = [0, D, 2 * D, 3 * D, 11 * D, 12 * D, 13 * D, 14 * D, 14 * D + FF, 15 * D + FF]
        b_patch, b_time, b_cond, b_mod, b_query, b_value, b_proj, b_expand, b_reduce = [
            biases[marks[number] : marks[number + 1]] for number in range(9)
        ]

        attend_t = after(attend_t, small)
        received = []
        for turn in range(per):
            local = jnp.asarray(unit_send[turn])[me]
            received.append(
                lax.ppermute(
                    lax.dynamic_slice(attend_t, (local * unit, 0), (unit, D)),
                    AXES,
                    [(owner, int(unit_target[turn, owner])) for owner in range(devices)],
                )
            )
        both = jnp.concatenate(received + [to_low(square_t[:, 1])], 0)
        hidden_masks = [mask ^ far for mask in (0, 4, 2, 6) for far in masks_of(far_bits)]
        hidden_blocks = jnp.asarray(np.array(hidden_masks, np.int32)) ^ me
        hidden_pick = hidden_blocks[:, None] == jnp.arange(devices)[None, :]
        size = len(hidden_masks) * hidden_share // 4

        tables = place_tables(slots, widest)
        freq_in = to_low(time_freq(steps_all))

        def mine(vector, count):
            return lax.dynamic_slice(vector, (me * count,), (count,))[:, None]

        pre_time_all = contract(embed_time, freq_in, 1, 1) + b_time[:, None]
        hid_time = to_low(smooth_gate(pre_time_all))
        onehot = to_low(
            (labels_all[:, None] == jnp.arange(classes)[None, :]).astype(jnp.float32)
        )
        square_zero = to_low(square_t[:, 0])
        condition = (
            contract(square_zero, hid_time, 1, 0)
            + mine(b_cond, cols)
            + contract(table_t, onehot, 1, 1)
        )
        signal = signal_level(step_own)[:, None, None]
        latent = after(latent, hid_time)
        noisy_own = to_low(jnp.sqrt(signal) * latent + jnp.sqrt(1.0 - signal) * noise_in)
        noisy_own = noisy_own.reshape(tokens, PIN)
        noisy_all = gather_rows(noisy_own, seq_down)
        cond_own = to_low(smooth_gate(condition))

        across_late = after(across, cond_own)
        block_of = jnp.asarray(np.array(slot_masks, np.int32)) ^ seq_index
        slot_ids = jnp.broadcast_to(
            block_of[:, None, None] * local_slots + jnp.arange(local_slots)[None, None, :],
            (seq, images, local_slots),
        ).reshape(-1)
        across_rows = jnp.broadcast_to(
            across_late[None, :, None], (seq, images, local_slots)
        ).reshape(-1)
        picks = place_picks(slot_ids, across_rows, slots, widest)
        stream_all = (
            contract(
                jnp.concatenate([picks] * 3 + [noisy_all], 1),
                jnp.concatenate(tables + [patch_t.T], 0),
                1,
                0,
            )
            + b_patch
        ).reshape(seq, images, local_slots, D)
        cond_came = share_all(cond_own)
        cond_act = cond_came.reshape(D, all_images)
        both_first = gather_rows(after(both, hid_time), dp_bits[:1])
        both_second = gather_rows(both_first, dp_bits[1:2])

        gathered = lax.all_gather(
            after(jnp.stack([expand_t, reduce_r]), (both_second, cond_came)), AXES, axis=0
        )
        mod_cols = contract(cond_act, shift_t, 0, 1) + mine(b_mod, shift_cols)[:, 0][None, :]
        mod_send = jnp.broadcast_to(
            mod_cols.reshape(dp, 1, images, shift_cols), (dp, seq, images, shift_cols)
        ).reshape(devices, images, shift_cols)
        unit_all, scale_all = standardize(after(stream_all, mod_cols))
        modulation = after(exchange(mod_send), scale_all)
        modulation = jnp.transpose(modulation, (1, 0, 2)).reshape(images, 8 * D)
        off_one, str_one, gate_one, off_two, str_two, gate_two, off_end, str_end = [
            modulation[:, number * D : (number + 1) * D] for number in range(8)
        ]

        both = gather_rows(after(both_second, mod_send), dp_bits[2:])
        my_rows = lax.dynamic_index_in_dim(jnp.asarray(row_table), me, 0, keepdims=False)
        place_units = to_low(
            (my_rows[:, None] == jnp.arange(3 * span)[None, :]).astype(jnp.float32)
        )
        attend_n = to_low(contract(both, place_units, 0, 0))
        normed_one = to_low(
            unit_all * (1.0 + str_one[None, :, None, :]) + off_one[None, :, None, :]
        ).reshape(all_tokens, D)
        stream_in = after(stream_all[0], normed_one)
        unit_one, scale_one = standardize(stream_in)

        def head_bias(vector):
            return lax.dynamic_slice(vector, (seq_index * span,), (span,))

        triple_bias = jnp.concatenate(
            [head_bias(b_query), jnp.zeros((span,), jnp.float32), head_bias(b_value)]
        )
        triple = to_low(contract(normed_one, attend_n, 1, 0) + triple_bias).reshape(
            seq, images, local_slots, 3 * span
        )
        meta = jnp.concatenate([seq_index.reshape(1), used]).astype(jnp.int32)
        context = attend_call(slot_masks, meta, triple, bias_all, ())

        proj_x = both.reshape(dp, per * unit + cols, D)[:, per * unit :].reshape(dp * cols, D)
        for bit in seq_down:
            proj_x = after(gather_rows(proj_x, [bit]), context)
        slot_block = jnp.asarray(np.array(gather_masks(devices), np.int32)) ^ me
        source = slot_block[:, None] * cols + jnp.arange(cols)[None, :]
        place_proj = to_low(
            (source.reshape(-1)[:, None] == jnp.arange(D)[None, :]).astype(jnp.float32)
        )
        proj_n = to_low(contract(place_proj, proj_x, 0, 0))

        def over_seq(values_in):
            return lax.all_to_all(values_in, "seq", split_axis=0, concat_axis=0, tiled=True)

        merged = jnp.transpose(
            after(over_seq(context), (proj_n, stream_in)).reshape(seq, tokens, span), (1, 0, 2)
        ).reshape(tokens, D)
        attended = (contract(merged, proj_n, 1, 1) + b_proj).reshape(images, local_slots, D)
        stream_mid = stream_in + gate_one[:, None, :] * attended
        unit_two, scale_two = standardize(stream_mid)
        normed_own = to_low(stretch_shift(unit_two, off_two, str_two)).reshape(tokens, D)

        def pair_rows(rows):
            return jnp.concatenate([rows, swap(rows, 0)], 0)

        normed_two = pair_rows(normed_own)
        hidden_bias = jnp.sum(
            jnp.where(hidden_pick[:, :, None], b_expand.reshape(1, devices, hidden_share), 0.0), 1
        ).reshape(PARTS, 1, 4 * size // PARTS)
        if hidden_share % 16 == 0:
            hidden_index, weights = (hidden_blocks, gathered)
        else:
            weights = jnp.transpose(
                jnp.take(gathered, hidden_blocks, axis=0).reshape(4, -1, 2, hidden_share, D),
                (0, 2, 1, 3, 4),
            ).reshape(4, 2, size, D)
            hidden_index = jnp.arange(4, dtype=jnp.int32)
        upward, active, down_own, down_sent = hidden_call(
            forward_kernel, hidden_index, normed_two, hidden_bias, weights
        )
        downward = (down_own + wide(swap(down_sent, 0)) + b_reduce).reshape(images, local_slots, D)
        stream_out = stream_mid + gate_two[:, None, :] * downward
        unit_end, scale_end = standardize(stream_out)
        normed_end = to_low(stretch_shift(unit_end, off_end, str_end)).reshape(tokens, D)
        predicted = contract(normed_end, final_weight, 1, 0).reshape(images, local_slots, PIN)
        errors = predicted - noise_in
        kept = (seq_index * local_slots + jnp.arange(local_slots))[None, :] < used[:, None]
        kept = kept[:, :, None].astype(jnp.float32)
        loss_local = jnp.sum(kept * errors * errors)
        count_local = jnp.sum(kept) * PIN

        grad_pred = to_low(2.0 * kept * errors).reshape(tokens, PIN)
        grad_end = contract(grad_pred, final_weight, 1, 1).reshape(images, local_slots, D)
        grad_out, grad_off_end, grad_str_end = stretch_back(grad_end, unit_end, scale_end, str_end)
        grad_down_own = to_low(grad_out * gate_two[:, None, :]).reshape(tokens, D)
        grad_down = pair_rows(grad_down_own)
        grad_up, up_sums, two_own, two_sent = hidden_call(
            backward_kernel, hidden_index, grad_down, upward, weights
        )

        both_low, both_high, x_low, x_high, y_low, y_high, near = outer_call(
            grad_up, active, normed_two, grad_down
        )
        from_both_low, from_both_high = (swap(both_low, 1), swap(both_high, 2))
        from_x_high = swap(x_high, 2)
        grad_two = two_own + wide(after(swap(two_sent, 0), both_low))
        grad_two = grad_two.reshape(images, local_slots, D)
        grad_mid_norm, grad_off_two, grad_str_two = stretch_back(
            grad_two, unit_two, scale_two, str_two
        )
        grad_mid = grad_out + grad_mid_norm
        grad_att = to_low(grad_mid * gate_one[:, None, :]).reshape(tokens, D)
        grad_merged = to_low(contract(grad_att, proj_n, 1, 0))
        grad_merged = jnp.transpose(grad_merged.reshape(tokens, seq, span), (1, 0, 2))
        grad_att_x = to_low(contract(after(grad_att, grad_merged), place_proj, 1, 1))
        proj_parts = contract(grad_att_x, merged, 0, 0)
        x_low = to_low(after(x_low, grad_merged) + wide(from_both_low))
        y_high = to_low(after(y_high, grad_merged) + wide(from_both_high))
        from_x_low, from_y_high = (swap(x_low, 2), swap(y_high, 1))
        proj_half = proj_parts.shape[0] // 2
        proj_sent = to_low(proj_parts[proj_half:])
        proj_parts = proj_parts[:proj_half] + wide(swap(proj_sent, 0))
        proj_half = proj_parts.shape[0] // 2
        proj_sent = to_low(proj_parts[proj_half:])
        proj_parts = proj_parts[:proj_half]
        from_proj = swap(proj_sent, 1)
        grad_context = after(over_seq(grad_merged), (proj_sent, x_low, y_high))
        grad_context = grad_context.reshape(seq, images, local_slots, span)

        grad_triple, triple_sums = attend_call(slot_masks, meta, triple, bias_all, (grad_context,))
        grad_triple = grad_triple.reshape(all_tokens, 3 * span)
        half = all_tokens // 2
        one_sent = to_low(contract(grad_triple[half:], attend_n, 1, 1))
        one_kept = contract(grad_triple[:half], attend_n, 1, 1)
        one_parts = one_kept + wide(swap(one_sent, 0))
        for bit in range(1, seq_bits):
            half = one_parts.shape[0] // 2
            if bit == seq_bits - 1:
                near_high = after(near, one_sent)[:, size // 2 :]
                near_sent = to_low(near_high + wide(from_x_high) + wide(from_y_high))
                from_high = swap(near_sent, far_bits[-1])
                one_parts = after(one_parts, near_sent)
            one_last = to_low(one_parts[half:])
            one_came = swap(one_last, bit)
            if bit == seq_bits - 1:
                own_rows = after(my_rows, one_last).reshape(dp, -1)[:, : per * unit].reshape(-1)
                place_own = to_low(
                    (own_rows[:, None] == jnp.arange(3 * span)[None, :]).astype(jnp.float32)
                )
                grad_units = to_low(contract(after(grad_triple, one_last), place_own, 1, 1))
                middle = dp * per * unit // 2
                attend_sent = to_low(contract(grad_units[:, middle:], normed_one, 0, 0))
                attend_kept = contract(grad_units[:, :middle], normed_one, 0, 0)
                proj_parts = proj_parts + wide(after(from_proj, attend_sent))
                from_y_low = swap(after(y_low, one_last), 1)
                one_came = after(one_came, (attend_sent, attend_kept))
            one_parts = one_parts[:half] + wide(one_came)
        grad_one = one_parts.reshape(images, local_slots, D)

        proj_parts = proj_parts.reshape(2, dp // 2, cols, D)

        def beside(attend_rows, proj_rows):
            attend_rows = attend_rows.reshape(dp // 2, per * unit, D)
            return jnp.concatenate([attend_rows, proj_rows], 1).reshape(-1, D)

        both_sent = beside(attend_sent, to_low(proj_parts[1]))
        both_parts = beside(attend_kept, proj_parts[0])
        both_half = both_parts.shape[0]
        triple_sums = jnp.sum(triple_sums, 0).reshape(-1)

        grad_in_norm, grad_off_one, grad_str_one = stretch_back(
            grad_one, unit_one, scale_one, str_one
        )
        grad_in = to_low(grad_mid + grad_in_norm).reshape(tokens, D)

        grad_gate_one = jnp.sum(grad_mid * attended, 1)
        grad_gate_two = jnp.sum(grad_out * downward, 1)
        grad_mod_parts = jnp.concatenate(
            [
                grad_off_one,
                grad_str_one,
                grad_gate_one,
                grad_off_two,
                grad_str_two,
                grad_gate_two,
                grad_off_end,
                grad_str_end,
            ],
            -1,
        )
        grad_mod_sent = jnp.transpose(
            grad_mod_parts.reshape(images, devices, shift_cols), (1, 0, 2)
        )
        grad_patch = contract(grad_in, noisy_own, 0, 0)
        grad_final = contract(normed_end, grad_pred, 0, 0)

        def heads_out(sums):
            return lax.dynamic_update_slice(
                jnp.zeros((D,), jnp.float32), sums, (seq_index * span,)
            )

        up_nat = jnp.sum(
            jnp.where(hidden_pick[:, :, None], up_sums.reshape(-1, 1, hidden_share), 0.0), 0
        )
        bias_parts = jnp.concatenate(
            [
                jnp.sum(wide(grad_in), 0),
                jnp.zeros((10 * D,), jnp.float32),
                heads_out(triple_sums[:span]),
                heads_out(triple_sums[2 * span :]),
                jnp.sum(wide(grad_att), 0),
                up_nat.reshape(-1),
                jnp.sum(wide(grad_down_own), 0),
            ]
        ).reshape(devices, bias_share)
        from_both = swap(after(both_sent, grad_mod_sent), dp_bits[-1])
        grad_mod = to_low(
            jnp.sum(
                after(exchange(grad_mod_sent), bias_parts).reshape(dp, seq, images, shift_cols), 1
            )
        ).reshape(all_images, shift_cols)

        cond_parts = contract(shift_t, grad_mod, 0, 1).reshape(devices, cols, all_images)
        both_parts = after(both_parts, cond_parts) + wide(from_both)
        both_half = both_half // 2
        both_sent = to_low(both_parts[both_half:])
        from_both = swap(both_sent, dp_bits[-2])
        near_low = after(near, both_sent)[:, : size // 2] + wide(from_x_low) + wide(from_y_low)
        near = near_low + wide(from_high)
        if len(far_bits) > 1:
            near_half = near.shape[1] // 2
            near_sent = to_low(near[:, near_half:])
            near_kept = near[:, :near_half]
        grad_shift = contract(after(grad_mod, cond_parts), cond_act, 0, 1)
        cond_came = after(exchange(cond_parts), (near_sent, grad_shift))
        grad_cond = to_low(smooth_gate_slope(condition) * jnp.sum(cond_came, 0))
        time_parts = contract(square_zero, grad_cond, 0, 0).reshape(devices, cols * all_images)

        mixed = jnp.concatenate(
            [
                time_parts,
                bias_parts,
                grad_patch.reshape(devices, cols * PIN),
                grad_final.reshape(devices, cols * PIN),
            ],
            1,
        )
        both_parts = after(both_parts[:both_half], mixed) + wide(from_both)
        both_half = both_half // 2
        both_sent = to_low(both_parts[both_half:])
        both_parts = both_parts[:both_half] + wide(swap(both_sent, dp_bits[-3]))
        if len(far_bits) > 1:
            near_came = swap(after(near_sent, both_sent), far_bits[-2])
        grad_table = contract(after(grad_cond, mixed), onehot, 1, 0)
        grad_time_two = contract(after(grad_cond, mixed), hid_time, 1, 1)
        mixed = after(exchange(mixed), (both_sent, grad_table, grad_time_two))
        mixed = jnp.sum(mixed, 0)
        time_came, mixed = (mixed[: cols * all_images], mixed[cols * all_images :])
        grad_bias = mixed[:bias_share]
        grad_patch = mixed[bias_share : bias_share + cols * PIN].reshape(cols, PIN)
        grad_final = mixed[bias_share + cols * PIN :].reshape(cols, PIN)
        pre_time = lax.dynamic_slice(pre_time_all, (me * cols, 0), (cols, all_images))
        grad_pre = to_low(smooth_gate_slope(pre_time) * time_came.reshape(cols, all_images))
        time_sums = jnp.sum(wide(grad_pre), 1)
        cond_sums = jnp.sum(wide(after(grad_cond, mixed)), 1)
        mod_sums = jnp.sum(wide(after(grad_mod, mixed)), 0)
        if len(far_bits) > 1:
            near = near_kept + wide(after(near_came, grad_pre))
        near = fold_second(near, far_bits[:-2][::-1])
        grad_expand, grad_reduce = (near[0], near[1])
        both_parts = fold_rows(both_parts, dp_bits[:-3][::-1])
        grad_proj = both_parts[per * unit :]
        grad_time_one = contract(grad_pre, freq_in, 1, 0)

        grad_attend = jnp.zeros((per, unit, D), jnp.float32)
        for turn in range(per):
            piece = lax.ppermute(
                both_parts[turn * unit : (turn + 1) * unit],
                AXES,
                [(int(unit_target[turn, owner]), owner) for owner in range(devices)],
            )
            local = after(jnp.asarray(unit_send[turn])[me], both_sent) == jnp.arange(per)
            grad_attend = jnp.where(local[:, None, None], piece[None], grad_attend)
        grad_attend = grad_attend.reshape(per * unit, D)

        grad_embed = jnp.concatenate([grad_patch, grad_time_one], 1)
        grad_square = jnp.stack([grad_time_two, grad_proj], 1)
        squares = sum(
            jnp.sum(piece * piece)
            for piece in (
                grad_patch,
                grad_time_one,
                grad_time_two,
                grad_proj,
                grad_table,
                grad_shift,
                grad_attend,
                grad_expand,
                grad_reduce,
                grad_final,
                grad_bias,
                time_sums,
                cond_sums,
                mod_sums,
            )
        )
        late = jnp.zeros((devices * bias_share,), jnp.float32)
        for sums, first in ((time_sums, D), (cond_sums, 2 * D), (mod_sums, 3 * D)):
            late = lax.dynamic_update_slice(late, sums, (first + me * sums.shape[0],))
        late = late.reshape(devices, bias_share)
        numbers = jnp.stack([loss_local, count_local, squares])
        late = jnp.concatenate([late, jnp.broadcast_to(numbers[None], (devices, 3))], 1)
        late = jnp.sum(exchange(late), 0)
        loss_total, value_count, squared = [late[bias_share + number] for number in range(3)]
        grad_norm = jnp.sqrt(squared)
        factor = LIMIT / jnp.maximum(grad_norm, LIMIT)
        grad_bias = grad_bias + late[:bias_share]

        shards = (
            grad_embed.T,
            jnp.transpose(grad_square, (1, 2, 0)),
            grad_table.T,
            grad_shift.T,
            grad_attend.T,
            grad_expand.T,
            grad_reduce,
            grad_final,
            grad_bias,
        )
        results = [
            adam_step(params_in[number], firsts[number], seconds[number], shards[number], factor)
            for number in range(9)
        ]
        fresh = [results[number][part] for part in range(3) for number in range(9)]
        return tuple([loss_total, value_count, grad_norm] + fresh)

    return on_device


def adam_step(weight, moment, second, gradient, factor):
    clipped = gradient * factor
    moment = BETA_ONE * moment + (1.0 - BETA_ONE) * clipped
    second = BETA_TWO * second + (1.0 - BETA_TWO) * clipped * clipped
    fixed_one = moment / (1.0 - BETA_ONE**STEP)
    fixed_two = second / (1.0 - BETA_TWO**STEP)
    weight = weight - RATE * (fixed_one / (jnp.sqrt(fixed_two) + EPSILON) + DECAY * weight)
    return (weight, moment, second)


def solution(mesh):
    both = ("dp", "seq")
    state = (
        P(None, both),
        P(None, None, both),
        P(None, both),
        P(None, both),
        P(None, both),
        P(None, both),
        P(both, None),
        P(both, None),
        P(both),
    )
    batch = (
        P(None, "dp", "seq", None),
        P(None, "dp", "seq", None),
        P(None, "dp"),
        P(None, "dp"),
        P(None, "dp"),
        P(None, "dp"),
        P(None, "dp", "seq", None, None),
    )
    return jax.shard_map(
        make_step(mesh),
        mesh=mesh,
        in_specs=batch + state * 3,
        out_specs=(P(), P(), P()) + state * 3,
        check_vma=False,
    )
```

```python
import functools
import math

import jax
import jax.numpy as jnp
import numpy as np
from jax import lax
from jax.experimental import pallas as pl
from jax.experimental.pallas import tpu as pltpu
from jax.sharding import PartitionSpec as P

D = 1152
HEADS = 16
HEAD = 72
FF = 4608
FREQ = 256
PIN = 16
MICRO = 2
TSTEPS = 1000
STEP = 10
LANES = 128
AXES = ("dp", "seq")

BETA_ONE = 0.9
BETA_TWO = 0.95
EPSILON = 1e-08
DECAY = 0.1
RATE = 0.03
LIMIT = 1.0


def to_low(values_in):
    return values_in.astype(jnp.bfloat16)


def wide(values_in):
    return values_in.astype(jnp.float32)


def smooth_gate(values_in):
    return values_in * jax.nn.sigmoid(values_in)


def smooth_gate_slope(values_in):
    gate = jax.nn.sigmoid(values_in)
    return gate * (1.0 + values_in * (1.0 - gate))


def contract(left, right, left_dim, right_dim):
    return lax.dot_general(
        left,
        right,
        (((left_dim,), (right_dim,)), ((), ())),
        preferred_element_type=jnp.float32,
    )


def time_freq(steps_in):
    half_freq = FREQ // 2
    rate_table = jnp.exp(-math.log(10000.0) * jnp.arange(half_freq).astype(jnp.float32) / half_freq)
    angles = steps_in.astype(jnp.float32)[:, None] * rate_table[None, :]
    return jnp.concatenate([jnp.cos(angles), jnp.sin(angles)], -1)


def signal_level(steps_in):
    angles = (steps_in.astype(jnp.float32) / TSTEPS + 0.008) / 1.008 * (math.pi / 2)
    return jnp.cos(angles) * jnp.cos(angles)


def place_tables(slots, widest):
    quarter = D // 4
    lane = jnp.arange(D)
    rate = jnp.exp(-math.log(10000.0) * (lane % quarter).astype(jnp.float32) / quarter)
    fine = 16
    coarse = -(-slots // fine)
    steps = jnp.concatenate(
        [jnp.arange(coarse, dtype=jnp.float32) * fine, jnp.arange(fine, dtype=jnp.float32)]
    )
    angles = steps[:, None] * rate[None, :]
    sines, cosines = (jnp.sin(angles), jnp.cos(angles))
    sine_high, sine_low = (sines[:coarse, None], sines[None, coarse:])
    cosine_high, cosine_low = (cosines[:coarse, None], cosines[None, coarse:])
    table = jnp.where(
        lane // quarter % 2 == 0,
        sine_high * cosine_low + cosine_high * sine_low,
        cosine_high * cosine_low - sine_high * sine_low,
    ).reshape(coarse * fine, D)
    by_row = lane < 2 * quarter
    table = jnp.concatenate(
        [jnp.where(by_row, table[:slots], 0.0), jnp.where(by_row, 0.0, table[:widest])], 0
    )
    part_one = to_low(table)
    rest = table - wide(part_one)
    part_two = to_low(rest)
    part_three = to_low(rest - wide(part_two))
    return [part_one, part_two, part_three]


def place_picks(slot_ids, across, slots, widest):
    row_pos = (slot_ids // across)[:, None]
    col_pos = (slot_ids % across)[:, None] + slots
    spots = jnp.arange(slots + widest)[None, :]
    return to_low(((row_pos == spots) | (col_pos == spots)).astype(jnp.float32))


def after(values_in, earlier):
    return lax.optimization_barrier((values_in, earlier))[0]


def standardize(stream):
    centred = stream - jnp.mean(stream, -1, keepdims=True)
    scale = lax.rsqrt(jnp.mean(centred * centred, -1, keepdims=True) + 1e-06)
    return (centred * scale, scale)


def stretch_shift(unit, offset, stretch):
    return unit * (1.0 + stretch[:, None, :]) + offset[:, None, :]


def stretch_back(grad, unit, scale, stretch):
    grad_offset = jnp.sum(grad, 1)
    grad_stretch = jnp.sum(grad * unit, 1)
    grad_unit = grad * (1.0 + stretch[:, None, :])
    grad_stream = scale * (
        grad_unit
        - jnp.mean(grad_unit, -1, keepdims=True)
        - unit * jnp.mean(grad_unit * unit, -1, keepdims=True)
    )
    return (grad_stream, grad_offset, grad_stretch)


CUBE = 0.044715
ROOT = 0.7978845608028654


def gaussian_unit(values_in):
    inner = ROOT * (values_in + CUBE * values_in * values_in * values_in)
    return 0.5 * values_in * (1.0 + jnp.tanh(inner))


def gaussian_slope(values_in):
    inner = ROOT * (values_in + CUBE * values_in * values_in * values_in)
    bend = jnp.tanh(inner)
    return 0.5 * (1.0 + bend) + 0.5 * values_in * (1.0 - bend * bend) * ROOT * (
        1.0 + 3.0 * CUBE * values_in * values_in
    )


def attend_probs(nat_ref, bias_ref, head, own, keep):
    width = own * HEAD
    queries = nat_ref[:, head * HEAD : (head + 1) * HEAD]
    keys = nat_ref[:, width + head * HEAD : width + (head + 1) * HEAD]
    values = nat_ref[:, 2 * width + head * HEAD : 2 * width + (head + 1) * HEAD]
    scores = contract(queries, keys, 1, 1) * HEAD ** (-0.5) + wide(bias_ref[0, head])
    scores = jnp.where(keep, scores, -1e30)
    powers = jnp.exp(scores - jnp.max(scores, -1, keepdims=True))
    probs = powers * (1.0 / jnp.sum(powers, -1, keepdims=True))
    return (queries, keys, values, probs)


def attend_enter(meta_ref, triple_ref, nat_ref, masks):
    block = triple_ref.shape[2]
    for number, mask in enumerate(masks):
        first = pl.multiple_of((meta_ref[0] ^ mask) * block, 16)
        nat_ref[pl.ds(first, block), :] = triple_ref[number, 0]
    slots = nat_ref.shape[0]
    local = lax.broadcasted_iota(jnp.int32, (slots, slots), 1)
    return local < meta_ref[1 + pl.program_id(0)]


def attend_kernel(masks, meta_ref, triple_ref, bias_ref, context_ref, nat_ref):
    keep = attend_enter(meta_ref, triple_ref, nat_ref, masks)
    own, block = (bias_ref.shape[1], triple_ref.shape[2])
    mixed = []
    for head in range(own):
        _, _, values, probs = attend_probs(nat_ref, bias_ref, head, own, keep)
        mixed.append(to_low(contract(to_low(probs), values, 1, 0)))
    context = jnp.concatenate(mixed, 1)
    for number in range(len(masks)):
        context_ref[number, 0] = context[number * block : (number + 1) * block]


def attend_back_kernel(
    masks, meta_ref, triple_ref, bias_ref, grad_ref, out_ref, sums_ref, nat_ref, back_ref
):
    keep = attend_enter(meta_ref, triple_ref, nat_ref, masks)
    own, block = (bias_ref.shape[1], triple_ref.shape[2])
    width = own * HEAD
    grads = jnp.concatenate([grad_ref[number, 0] for number in range(len(masks))], 0)
    for head in range(own):
        queries, keys, values, probs = attend_probs(nat_ref, bias_ref, head, own, keep)
        grad_context = grads[:, head * HEAD : (head + 1) * HEAD]
        grad_probs = contract(grad_context, values, 1, 1)
        weighted = probs * grad_probs
        grad_scores = to_low(weighted - probs * jnp.sum(weighted, -1, keepdims=True))
        pieces = (
            contract(grad_scores, keys, 1, 0) * HEAD ** (-0.5),
            contract(grad_scores, queries, 0, 0) * HEAD ** (-0.5),
            contract(to_low(probs), grad_context, 0, 0),
        )
        for kind in range(3):
            begin = kind * width + head * HEAD
            back_ref[:, begin : begin + HEAD] = to_low(pieces[kind])
    sums_ref[0] = jnp.sum(wide(back_ref[...]), 0, keepdims=True)
    for number, mask in enumerate(masks):
        first = pl.multiple_of((meta_ref[0] ^ mask) * block, 16)
        out_ref[number, 0] = back_ref[pl.ds(first, block), :]


def attend_call(masks, meta, triple, bias_tiles, grads):
    images, own, slots, _ = bias_tiles.shape
    count, _, block, full = triple.shape
    width = own * HEAD
    backward = len(grads) > 0
    row = lambda image, meta_ref: (0, image, 0, 0)
    tri_spec = pl.BlockSpec((count, 1, block, full), row)
    slim_spec = pl.BlockSpec((count, 1, block, width), row)
    in_specs = [
        tri_spec,
        pl.BlockSpec((1, own, slots, slots), lambda image, meta_ref: (image, 0, 0, 0)),
    ] + [slim_spec] * len(grads)
    nat = pltpu.VMEM((slots, full), jnp.bfloat16)
    if backward:
        kernel, products = (attend_back_kernel, 6)
        out_shape = (
            jax.ShapeDtypeStruct(triple.shape, jnp.bfloat16),
            jax.ShapeDtypeStruct((images, 1, full), jnp.float32),
        )
        out_specs = (tri_spec, pl.BlockSpec((1, 1, full), lambda image, meta_ref: (image, 0, 0)))
        scratch = [nat, nat]
    else:
        kernel, products = (attend_kernel, 2)
        out_shape = jax.ShapeDtypeStruct((count, images, block, width), jnp.bfloat16)
        out_specs = slim_spec
        scratch = [nat]
    return pl.pallas_call(
        functools.partial(kernel, masks),
        out_shape=out_shape,
        grid_spec=pltpu.PrefetchScalarGridSpec(
            num_scalar_prefetch=1,
            grid=(images,),
            in_specs=in_specs,
            out_specs=out_specs,
            scratch_shapes=scratch,
        ),
        compiler_params=pltpu.CompilerParams(vmem_limit_bytes=40 * 2**20),
        cost_estimate=pl.CostEstimate(flops=1000, bytes_accessed=1000, transcendentals=0),
    )(meta, triple, bias_tiles, *grads)


PARTS = 3


def weight_copies(pick_ref, weight_ref, kind, held_ref, sem_ref):
    rows = weight_ref.shape[2]
    part = held_ref.shape[0] // PARTS
    copies = []
    for number in range(held_ref.shape[0] // rows):
        copies.append(
            (
                number * rows // part,
                pltpu.make_async_copy(
                    weight_ref.at[pick_ref[number], kind],
                    held_ref.at[pl.ds(number * rows, rows)],
                    sem_ref.at[kind, number],
                ),
            )
        )
    return copies


def held_part(held_ref):
    part = held_ref.shape[0] // PARTS
    return held_ref[pl.ds(pl.multiple_of(pl.program_id(0) * part, part), part), :]


def start_copies(groups):
    @pl.when(pl.program_id(0) == 0)
    def _():
        for copies in groups:
            for _, copy in copies:
                copy.start()


def wait_copies(copies):
    for quarter in range(PARTS):

        @pl.when(pl.program_id(0) == quarter)
        def _():
            for number, copy in copies:
                if number == quarter:
                    copy.wait()


def put_pair(total, own_ref, sent_ref):
    rows = own_ref.shape[0]

    @pl.when(pl.program_id(0) == pl.num_programs(0) - 1)
    def _():
        own_ref[...] = total[:rows]
        sent_ref[...] = to_low(total[rows:])


def add_up(total_ref, product):
    @pl.when(pl.program_id(0) == 0)
    def _():
        total_ref[...] = product

    @pl.when(pl.program_id(0) > 0)
    def _():
        total_ref[...] += product


def forward_kernel(
    pick_ref,
    normed_ref,
    bias_ref,
    weight_ref,
    up_ref,
    active_ref,
    own_ref,
    sent_ref,
    expand_held,
    reduce_held,
    total_ref,
    sem_ref,
):
    expand_copies = weight_copies(pick_ref, weight_ref, 0, expand_held, sem_ref)
    reduce_copies = weight_copies(pick_ref, weight_ref, 1, reduce_held, sem_ref)
    start_copies([expand_copies, reduce_copies])
    wait_copies(expand_copies)
    upward = contract(normed_ref[...], held_part(expand_held), 1, 1) + bias_ref[0]
    up_ref[0] = upward
    active = to_low(gaussian_unit(upward))
    active_ref[0] = active
    wait_copies(reduce_copies)
    add_up(total_ref, contract(active, held_part(reduce_held), 1, 0))
    put_pair(total_ref, own_ref, sent_ref)


def backward_kernel(
    pick_ref,
    grad_ref,
    up_ref,
    weight_ref,
    out_ref,
    sums_ref,
    own_ref,
    sent_ref,
    expand_held,
    reduce_held,
    total_ref,
    sem_ref,
):
    expand_copies = weight_copies(pick_ref, weight_ref, 0, expand_held, sem_ref)
    reduce_copies = weight_copies(pick_ref, weight_ref, 1, reduce_held, sem_ref)
    start_copies([reduce_copies, expand_copies])
    wait_copies(reduce_copies)
    grad_active = contract(grad_ref[...], held_part(reduce_held), 1, 1)
    grad_up = to_low(gaussian_slope(up_ref[0]) * grad_active)
    out_ref[0] = grad_up
    sums_ref[0] = jnp.sum(wide(grad_up), 0, keepdims=True)
    wait_copies(expand_copies)
    add_up(total_ref, contract(grad_up, held_part(expand_held), 1, 0))
    put_pair(total_ref, own_ref, sent_ref)


def hidden_call(kernel, pick, left, second, weights):
    rows = left.shape[0]
    size = second.shape[2]
    whole = pl.BlockSpec((rows, D), lambda quarter, pick_ref: (0, 0))
    slab = pl.BlockSpec((1, rows, size), lambda quarter, pick_ref: (quarter, 0, 0))
    line = pl.BlockSpec((1, 1, size), lambda quarter, pick_ref: (quarter, 0, 0))
    half = pl.BlockSpec((rows // 2, D), lambda quarter, pick_ref: (0, 0))
    if kernel is forward_kernel:
        second_spec, out_specs = (line, (slab, slab, half, half))
        kinds = (((PARTS, rows, size), jnp.float32), ((PARTS, rows, size), jnp.bfloat16))
    else:
        second_spec, out_specs = (slab, (slab, line, half, half))
        kinds = (((PARTS, rows, size), jnp.bfloat16), ((PARTS, 1, size), jnp.float32))
    kinds = kinds + (((rows // 2, D), jnp.float32), ((rows // 2, D), jnp.bfloat16))
    return pl.pallas_call(
        kernel,
        out_shape=tuple(jax.ShapeDtypeStruct(shape, kind) for shape, kind in kinds),
        grid_spec=pltpu.PrefetchScalarGridSpec(
            num_scalar_prefetch=1,
            grid=(PARTS,),
            in_specs=[whole, second_spec, pl.BlockSpec(memory_space=pl.ANY)],
            out_specs=out_specs,
            scratch_shapes=[
                pltpu.VMEM((PARTS * size, D), jnp.bfloat16),
                pltpu.VMEM((PARTS * size, D), jnp.bfloat16),
                pltpu.VMEM((rows, D), jnp.float32),
                pltpu.SemaphoreType.DMA((2, PARTS * size // weights.shape[2])),
            ],
        ),
        compiler_params=pltpu.CompilerParams(vmem_limit_bytes=56 * 2**20),
        cost_estimate=pl.CostEstimate(flops=1000, bytes_accessed=1000, transcendentals=0),
    )(pick, left, second, weights)


def piece_ranges(total):
    eighth = total // 8
    marks = [(6, 7), (7, 8), (2, 3), (3, 4), (4, 5), (5, 6), (0, 2)]
    return [(first * eighth, last * eighth) for first, last in marks]


def outer_kernel(grad_up_ref, active_ref, normed_ref, grad_ref, *refs):
    outs, held, sem_ref = (refs[:7], refs[7:14], refs[14])
    part = grad_up_ref.shape[2]
    products = (
        contract(grad_up_ref[0], normed_ref[...], 0, 0),
        contract(active_ref[0], grad_ref[...], 0, 0),
    )
    copies = [pltpu.make_async_copy(held[at], outs[at], sem_ref.at[at]) for at in range(7)]
    ranges = piece_ranges(PARTS * part)
    for turn in range(PARTS):
        begin = (PARTS - 1 - turn) * part

        @pl.when(pl.program_id(0) == turn)
        def _():
            for at, (first, last) in enumerate(ranges):
                low, high = (max(first, begin), min(last, begin + part))
                for kind in range(2):
                    if low < high:
                        value = products[kind][low - begin : high - begin]
                        held[at][kind, low - first : high - first] = value.astype(held[at].dtype)
                if begin <= first < begin + part:
                    copies[at].start()

    @pl.when(pl.program_id(0) == PARTS - 1)
    def _():
        for copy in copies:
            copy.wait()


def outer_call(grad_up, active, normed, grad_down):
    _, rows, part = grad_up.shape
    low, full = (jnp.bfloat16, jnp.float32)
    kinds = (low, low, full, low, low, full, full)
    shapes = [
        ((2, last - first, D), kind)
        for (first, last), kind in zip(piece_ranges(PARTS * part), kinds)
    ]
    slab = pl.BlockSpec((1, rows, part), lambda step: (PARTS - 1 - step, 0, 0))
    whole = pl.BlockSpec((rows, D), lambda step: (0, 0))
    return pl.pallas_call(
        outer_kernel,
        out_shape=tuple(jax.ShapeDtypeStruct(shape, kind) for shape, kind in shapes),
        grid=(PARTS,),
        in_specs=[slab, slab, whole, whole],
        out_specs=tuple([pl.BlockSpec(memory_space=pl.ANY)] * 7),
        scratch_shapes=[pltpu.VMEM(shape, kind) for shape, kind in shapes]
        + [pltpu.SemaphoreType.DMA((7,))],
        compiler_params=pltpu.CompilerParams(vmem_limit_bytes=56 * 2**20),
        cost_estimate=pl.CostEstimate(flops=1000, bytes_accessed=1000, transcendentals=0),
    )(grad_up, active, normed, grad_down)


def unit_plan(devices, seq):
    share = 3 * D // devices
    unit = math.gcd(math.gcd(share, D // seq), HEAD)
    per = share // unit
    span = D // seq

    def group_of(number):
        return (number * unit % D) // span

    left = [{local: group_of(owner * per + local) for local in range(per)} for owner in range(devices)]
    send = np.zeros((per, devices), np.int32)
    target = np.zeros((per, devices), np.int32)
    held = np.zeros((per, devices), np.int32)
    for turn in range(per):
        match = [-1] * devices

        def seek(owner, seen):
            groups = set(left[owner].values())
            near = sorted(
                (place for place in range(devices) if place % seq in groups),
                key=lambda place: (place != owner, place // seq != owner // seq, place ^ owner),
            )
            for place in near:
                if place in seen:
                    continue
                seen.add(place)
                if match[place] < 0 or seek(match[place], seen):
                    match[place] = owner
                    return True
            return False

        for owner in range(devices):
            assert seek(owner, set())
        for place, owner in enumerate(match):
            local = next(item for item, group in left[owner].items() if group == place % seq)
            del left[owner][local]
            send[turn, owner] = local
            target[turn, owner] = place
            held[turn, place] = owner * per + local
    return (unit, per, send, target, held)


def unit_rows(devices, seq, unit, per, held):
    dp = devices // seq
    span = D // seq
    extra = D // devices
    rows = np.full((devices, dp * (per * unit + extra)), -1, np.int32)
    for place in range(devices):
        at = 0
        for mask in gather_masks(dp):
            for turn in range(per):
                first = int(held[turn, place ^ (mask * seq)]) * unit
                kind, inside = (first // D, first % D)
                begin = kind * span + inside - span * (place % seq)
                rows[place, at : at + unit] = np.arange(begin, begin + unit)
                at += unit
            at += extra
    return rows


def gather_masks(dp):
    masks = [0]
    bit = dp >> 1
    while bit:
        masks = masks + [item ^ bit for item in masks]
        bit >>= 1
    return masks


def make_step(mesh):
    dp, seq = (mesh.shape["dp"], mesh.shape["seq"])
    devices = dp * seq
    top = devices.bit_length() - 1
    seq_bits = seq.bit_length() - 1
    own_heads = HEADS // seq
    span = D // seq
    unit, per, unit_send, unit_target, unit_held = unit_plan(devices, seq)
    row_table = unit_rows(devices, seq, unit, per, unit_held)
    cols = D // devices
    shift_cols = 8 * D // devices
    hidden_share = FF // devices
    bias_share = (15 * D + FF) // devices
    dp_bits = list(range(top - 1, seq_bits - 1, -1))
    far_bits = list(range(top - 1, 2, -1))
    seq_down = list(range(seq_bits - 1, -1, -1))

    def masks_of(bits):
        masks = [0]
        for bit in bits:
            masks = masks + [mask ^ (1 << bit) for mask in masks]
        return masks

    slot_masks = masks_of(seq_down)

    def swap(values_in, bit):
        return lax.ppermute(
            values_in, AXES, [(place, place ^ (1 << bit)) for place in range(devices)]
        )

    def exchange(values_in):
        return lax.all_to_all(values_in, AXES, split_axis=0, concat_axis=0, tiled=True)

    def share_all(block):
        return exchange(jnp.broadcast_to(block[None], (devices,) + block.shape))

    def gather_rows(rows, bits):
        for bit in bits:
            rows = jnp.concatenate([rows, swap(rows, bit)], 0)
        return rows

    def fold_rows(rows, bits):
        for bit in bits:
            half = rows.shape[0] // 2
            rows = rows[:half] + wide(swap(to_low(rows[half:]), bit))
        return rows

    def fold_second(rows, bits):
        for bit in bits:
            half = rows.shape[1] // 2
            rows = rows[:, :half] + wide(swap(to_low(rows[:, half:]), bit))
        return rows

    def on_device(
        latents,
        noise_draw,
        heights,
        widths,
        labels,
        timesteps,
        bias_tiles,
        *states,
    ):
        params_in, firsts, seconds = (states[:9], states[9:18], states[18:])
        seq_index = lax.axis_index("seq")
        me = lax.axis_index("dp") * seq + seq_index
        local_slots = latents.shape[2]
        slots = local_slots * seq
        widest = min(slots, 32)
        images = latents.shape[0] * latents.shape[1]
        classes = params_in[2].shape[0]
        tokens = images * local_slots
        all_tokens = images * slots
        all_images = images * dp
        latent = latents.reshape(images, local_slots, PIN)
        noise_in = noise_draw.reshape(images, local_slots, PIN)
        height, across = (heights.reshape(images), widths.reshape(images))
        label_own, step_own = (labels.reshape(images), timesteps.reshape(images))
        bias_all = bias_tiles.reshape(images, own_heads, slots, slots)
        used = height * across

        embed_t = params_in[0].T
        square_t = jnp.transpose(params_in[1], (2, 0, 1))
        table_t = to_low(params_in[2].T)
        shift_t = to_low(params_in[3].T)
        attend_t = to_low(params_in[4].T)
        expand_t = to_low(params_in[5].T)
        reduce_r = to_low(params_in[6])

        small = jnp.concatenate(
            [to_low(params_in[8]), to_low(embed_t[:, :PIN]).reshape(-1), to_low(params_in[7]).reshape(-1)]
            + [
                to_low(wide(piece))
                for piece in (step_own // 32, step_own % 32, label_own // 32, label_own % 32)
            ]
        )
        length = -(-small.shape[0] // 2048) * 2048
        small = jnp.pad(small, (0, length - small.shape[0])).reshape(-1, LANES)
        embed_own = to_low(embed_t[:, PIN:]).reshape(-1, LANES)
        small = share_all(jnp.concatenate([small, embed_own], 0))
        embed_time = small[:, length // LANES :].reshape(D, FREQ)
        small = small[:, : length // LANES].reshape(devices, length)
        at = bias_share
        biases = wide(small[:, :at].reshape(-1))
        patch_t = small[:, at : at + cols * PIN].reshape(D, PIN)
        at = at + cols * PIN
        final_weight = small[:, at : at + cols * PIN].reshape(D, PIN)
        at = at + cols * PIN
        numbers = wide(small[::seq, at : at + 4 * images]).reshape(dp, 4, images).astype(jnp.int32)
        steps_all = (numbers[:, 0] * 32 + numbers[:, 1]).reshape(-1)
        labels_all = (numbers[:, 2] * 32 + numbers[:, 3]).reshape(-1)
        marks = [0, D, 2 * D, 3 * D, 11 * D, 12 * D, 13 * D, 14 * D, 14 * D + FF, 15 * D + FF]
        b_patch, b_time, b_cond, b_mod, b_query, b_value, b_proj, b_expand, b_reduce = [
            biases[marks[number] : marks[number + 1]] for number in range(9)
        ]

        attend_t = after(attend_t, small)
        received = []
        for turn in range(per):
            local = jnp.asarray(unit_send[turn])[me]
            received.append(
                lax.ppermute(
                    lax.dynamic_slice(attend_t, (local * unit, 0), (unit, D)),
                    AXES,
                    [(owner, int(unit_target[turn, owner])) for owner in range(devices)],
                )
            )
        both = jnp.concatenate(received + [to_low(square_t[:, 1])], 0)
        hidden_masks = [mask ^ far for mask in (0, 4, 2, 6) for far in masks_of(far_bits)]
        hidden_blocks = jnp.asarray(np.array(hidden_masks, np.int32)) ^ me
        hidden_pick = hidden_blocks[:, None] == jnp.arange(devices)[None, :]
        size = len(hidden_masks) * hidden_share // 4

        tables = place_tables(slots, widest)
        freq_in = to_low(time_freq(steps_all))

        def mine(vector, count):
            return lax.dynamic_slice(vector, (me * count,), (count,))[:, None]

        pre_time_all = contract(embed_time, freq_in, 1, 1) + b_time[:, None]
        hid_time = to_low(smooth_gate(pre_time_all))
        onehot = to_low(
            (labels_all[:, None] == jnp.arange(classes)[None, :]).astype(jnp.float32)
        )
        square_zero = to_low(square_t[:, 0])
        condition = (
            contract(square_zero, hid_time, 1, 0)
            + mine(b_cond, cols)
            + contract(table_t, onehot, 1, 1)
        )
        signal = signal_level(step_own)[:, None, None]
        latent = after(latent, hid_time)
        noisy_own = to_low(jnp.sqrt(signal) * latent + jnp.sqrt(1.0 - signal) * noise_in)
        noisy_own = noisy_own.reshape(tokens, PIN)
        noisy_all = gather_rows(noisy_own, seq_down)
        cond_own = to_low(smooth_gate(condition))

        across_late = after(across, cond_own)
        block_of = jnp.asarray(np.array(slot_masks, np.int32)) ^ seq_index
        slot_ids = jnp.broadcast_to(
            block_of[:, None, None] * local_slots + jnp.arange(local_slots)[None, None, :],
            (seq, images, local_slots),
        ).reshape(-1)
        across_rows = jnp.broadcast_to(
            across_late[None, :, None], (seq, images, local_slots)
        ).reshape(-1)
        picks = place_picks(slot_ids, across_rows, slots, widest)
        stream_all = (
            contract(
                jnp.concatenate([picks] * 3 + [noisy_all], 1),
                jnp.concatenate(tables + [patch_t.T], 0),
                1,
                0,
            )
            + b_patch
        ).reshape(seq, images, local_slots, D)
        cond_came = share_all(cond_own)
        cond_act = cond_came.reshape(D, all_images)
        both_first = gather_rows(after(both, hid_time), dp_bits[:1])
        both_second = gather_rows(both_first, dp_bits[1:2])

        gathered = lax.all_gather(
            after(jnp.stack([expand_t, reduce_r]), (both_second, cond_came)), AXES, axis=0
        )
        mod_cols = contract(cond_act, shift_t, 0, 1) + mine(b_mod, shift_cols)[:, 0][None, :]
        mod_send = jnp.broadcast_to(
            mod_cols.reshape(dp, 1, images, shift_cols), (dp, seq, images, shift_cols)
        ).reshape(devices, images, shift_cols)
        unit_all, scale_all = standardize(after(stream_all, mod_cols))
        modulation = after(exchange(mod_send), scale_all)
        modulation = jnp.transpose(modulation, (1, 0, 2)).reshape(images, 8 * D)
        off_one, str_one, gate_one, off_two, str_two, gate_two, off_end, str_end = [
            modulation[:, number * D : (number + 1) * D] for number in range(8)
        ]

        both = gather_rows(after(both_second, mod_send), dp_bits[2:])
        my_rows = lax.dynamic_index_in_dim(jnp.asarray(row_table), me, 0, keepdims=False)
        place_units = to_low(
            (my_rows[:, None] == jnp.arange(3 * span)[None, :]).astype(jnp.float32)
        )
        attend_n = to_low(contract(both, place_units, 0, 0))
        normed_one = to_low(
            unit_all * (1.0 + str_one[None, :, None, :]) + off_one[None, :, None, :]
        ).reshape(all_tokens, D)
        stream_in = after(stream_all[0], normed_one)
        unit_one, scale_one = standardize(stream_in)

        def head_bias(vector):
            return lax.dynamic_slice(vector, (seq_index * span,), (span,))

        triple_bias = jnp.concatenate(
            [head_bias(b_query), jnp.zeros((span,), jnp.float32), head_bias(b_value)]
        )
        triple = to_low(contract(normed_one, attend_n, 1, 0) + triple_bias).reshape(
            seq, images, local_slots, 3 * span
        )
        meta = jnp.concatenate([seq_index.reshape(1), used]).astype(jnp.int32)
        context = attend_call(slot_masks, meta, triple, bias_all, ())

        proj_x = both.reshape(dp, per * unit + cols, D)[:, per * unit :].reshape(dp * cols, D)
        for bit in seq_down:
            proj_x = after(gather_rows(proj_x, [bit]), context)
        slot_block = jnp.asarray(np.array(gather_masks(devices), np.int32)) ^ me
        source = slot_block[:, None] * cols + jnp.arange(cols)[None, :]
        place_proj = to_low(
            (source.reshape(-1)[:, None] == jnp.arange(D)[None, :]).astype(jnp.float32)
        )
        proj_n = to_low(contract(place_proj, proj_x, 0, 0))

        def over_seq(values_in):
            return lax.all_to_all(values_in, "seq", split_axis=0, concat_axis=0, tiled=True)

        merged = jnp.transpose(
            after(over_seq(context), (proj_n, stream_in)).reshape(seq, tokens, span), (1, 0, 2)
        ).reshape(tokens, D)
        attended = (contract(merged, proj_n, 1, 1) + b_proj).reshape(images, local_slots, D)
        stream_mid = stream_in + gate_one[:, None, :] * attended
        unit_two, scale_two = standardize(stream_mid)
        normed_own = to_low(stretch_shift(unit_two, off_two, str_two)).reshape(tokens, D)

        def pair_rows(rows):
            return jnp.concatenate([rows, swap(rows, 0)], 0)

        normed_two = pair_rows(normed_own)
        hidden_bias = jnp.sum(
            jnp.where(hidden_pick[:, :, None], b_expand.reshape(1, devices, hidden_share), 0.0), 1
        ).reshape(PARTS, 1, 4 * size // PARTS)
        if hidden_share % 16 == 0:
            hidden_index, weights = (hidden_blocks, gathered)
        else:
            weights = jnp.transpose(
                jnp.take(gathered, hidden_blocks, axis=0).reshape(4, -1, 2, hidden_share, D),
                (0, 2, 1, 3, 4),
            ).reshape(4, 2, size, D)
            hidden_index = jnp.arange(4, dtype=jnp.int32)
        upward, active, down_own, down_sent = hidden_call(
            forward_kernel, hidden_index, normed_two, hidden_bias, weights
        )
        downward = (down_own + wide(swap(down_sent, 0)) + b_reduce).reshape(images, local_slots, D)
        stream_out = stream_mid + gate_two[:, None, :] * downward
        unit_end, scale_end = standardize(stream_out)
        normed_end = to_low(stretch_shift(unit_end, off_end, str_end)).reshape(tokens, D)
        predicted = contract(normed_end, final_weight, 1, 0).reshape(images, local_slots, PIN)
        errors = predicted - noise_in
        kept = (seq_index * local_slots + jnp.arange(local_slots))[None, :] < used[:, None]
        kept = kept[:, :, None].astype(jnp.float32)
        loss_local = jnp.sum(kept * errors * errors)
        count_local = jnp.sum(kept) * PIN

        grad_pred = to_low(2.0 * kept * errors).reshape(tokens, PIN)
        grad_end = contract(grad_pred, final_weight, 1, 1).reshape(images, local_slots, D)
        grad_out, grad_off_end, grad_str_end = stretch_back(grad_end, unit_end, scale_end, str_end)
        grad_down_own = to_low(grad_out * gate_two[:, None, :]).reshape(tokens, D)
        grad_down = pair_rows(grad_down_own)
        grad_up, up_sums, two_own, two_sent = hidden_call(
            backward_kernel, hidden_index, grad_down, upward, weights
        )

        both_low, both_high, x_low, x_high, y_low, y_high, near = outer_call(
            grad_up, active, normed_two, grad_down
        )
        from_both_low, from_both_high = (swap(both_low, 1), swap(both_high, 2))
        from_x_high = swap(x_high, 2)
        grad_two = two_own + wide(after(swap(two_sent, 0), both_low))
        grad_two = grad_two.reshape(images, local_slots, D)
        grad_mid_norm, grad_off_two, grad_str_two = stretch_back(
            grad_two, unit_two, scale_two, str_two
        )
        grad_mid = grad_out + grad_mid_norm
        grad_att = to_low(grad_mid * gate_one[:, None, :]).reshape(tokens, D)
        grad_merged = to_low(contract(grad_att, proj_n, 1, 0))
        grad_merged = jnp.transpose(grad_merged.reshape(tokens, seq, span), (1, 0, 2))
        grad_att_x = to_low(contract(after(grad_att, grad_merged), place_proj, 1, 1))
        proj_parts = contract(grad_att_x, merged, 0, 0)
        x_low = to_low(after(x_low, grad_merged) + wide(from_both_low))
        y_high = to_low(after(y_high, grad_merged) + wide(from_both_high))
        from_x_low, from_y_high = (swap(x_low, 2), swap(y_high, 1))
        proj_half = proj_parts.shape[0] // 2
        proj_sent = to_low(proj_parts[proj_half:])
        proj_parts = proj_parts[:proj_half] + wide(swap(proj_sent, 0))
        proj_half = proj_parts.shape[0] // 2
        proj_sent = to_low(proj_parts[proj_half:])
        proj_parts = proj_parts[:proj_half]
        from_proj = swap(proj_sent, 1)
        grad_context = after(over_seq(grad_merged), (proj_sent, x_low, y_high))
        grad_context = grad_context.reshape(seq, images, local_slots, span)

        grad_triple, triple_sums = attend_call(slot_masks, meta, triple, bias_all, (grad_context,))
        grad_triple = grad_triple.reshape(all_tokens, 3 * span)
        half = all_tokens // 2
        one_sent = to_low(contract(grad_triple[half:], attend_n, 1, 1))
        one_kept = contract(grad_triple[:half], attend_n, 1, 1)
        one_parts = one_kept + wide(swap(one_sent, 0))
        for bit in range(1, seq_bits):
            half = one_parts.shape[0] // 2
            if bit == seq_bits - 1:
                near_high = after(near, one_sent)[:, size // 2 :]
                near_sent = to_low(near_high + wide(from_x_high) + wide(from_y_high))
                from_high = swap(near_sent, far_bits[-1])
                one_parts = after(one_parts, near_sent)
            one_last = to_low(one_parts[half:])
            one_came = swap(one_last, bit)
            if bit == seq_bits - 1:
                own_rows = after(my_rows, one_last).reshape(dp, -1)[:, : per * unit].reshape(-1)
                place_own = to_low(
                    (own_rows[:, None] == jnp.arange(3 * span)[None, :]).astype(jnp.float32)
                )
                grad_units = to_low(contract(after(grad_triple, one_last), place_own, 1, 1))
                middle = dp * per * unit // 2
                attend_sent = to_low(contract(grad_units[:, middle:], normed_one, 0, 0))
                attend_kept = contract(grad_units[:, :middle], normed_one, 0, 0)
                proj_parts = proj_parts + wide(after(from_proj, attend_sent))
                from_y_low = swap(after(y_low, one_last), 1)
                one_came = after(one_came, (attend_sent, attend_kept))
            one_parts = one_parts[:half] + wide(one_came)
        grad_one = one_parts.reshape(images, local_slots, D)

        proj_parts = proj_parts.reshape(2, dp // 2, cols, D)

        def beside(attend_rows, proj_rows):
            attend_rows = attend_rows.reshape(dp // 2, per * unit, D)
            return jnp.concatenate([attend_rows, proj_rows], 1).reshape(-1, D)

        both_sent = beside(attend_sent, to_low(proj_parts[1]))
        both_parts = beside(attend_kept, proj_parts[0])
        both_half = both_parts.shape[0]
        triple_sums = jnp.sum(triple_sums, 0).reshape(-1)

        grad_in_norm, grad_off_one, grad_str_one = stretch_back(
            grad_one, unit_one, scale_one, str_one
        )
        grad_in = to_low(grad_mid + grad_in_norm).reshape(tokens, D)

        grad_gate_one = jnp.sum(grad_mid * attended, 1)
        grad_gate_two = jnp.sum(grad_out * downward, 1)
        grad_mod_parts = jnp.concatenate(
            [
                grad_off_one,
                grad_str_one,
                grad_gate_one,
                grad_off_two,
                grad_str_two,
                grad_gate_two,
                grad_off_end,
                grad_str_end,
            ],
            -1,
        )
        grad_mod_sent = jnp.transpose(
            grad_mod_parts.reshape(images, devices, shift_cols), (1, 0, 2)
        )
        grad_patch = contract(grad_in, noisy_own, 0, 0)
        grad_final = contract(normed_end, grad_pred, 0, 0)

        def heads_out(sums):
            return lax.dynamic_update_slice(
                jnp.zeros((D,), jnp.float32), sums, (seq_index * span,)
            )

        up_nat = jnp.sum(
            jnp.where(hidden_pick[:, :, None], up_sums.reshape(-1, 1, hidden_share), 0.0), 0
        )
        bias_parts = jnp.concatenate(
            [
                jnp.sum(wide(grad_in), 0),
                jnp.zeros((10 * D,), jnp.float32),
                heads_out(triple_sums[:span]),
                heads_out(triple_sums[2 * span :]),
                jnp.sum(wide(grad_att), 0),
                up_nat.reshape(-1),
                jnp.sum(wide(grad_down_own), 0),
            ]
        ).reshape(devices, bias_share)
        from_both = swap(after(both_sent, grad_mod_sent), dp_bits[-1])
        grad_mod = to_low(
            jnp.sum(
                after(exchange(grad_mod_sent), bias_parts).reshape(dp, seq, images, shift_cols), 1
            )
        ).reshape(all_images, shift_cols)

        cond_parts = contract(shift_t, grad_mod, 0, 1).reshape(devices, cols, all_images)
        both_parts = after(both_parts, cond_parts) + wide(from_both)
        both_half = both_half // 2
        both_sent = to_low(both_parts[both_half:])
        from_both = swap(both_sent, dp_bits[-2])
        near_low = after(near, both_sent)[:, : size // 2] + wide(from_x_low) + wide(from_y_low)
        near = near_low + wide(from_high)
        if len(far_bits) > 1:
            near_half = near.shape[1] // 2
            near_sent = to_low(near[:, near_half:])
            near_kept = near[:, :near_half]
        grad_shift = contract(after(grad_mod, cond_parts), cond_act, 0, 1)
        cond_came = after(exchange(cond_parts), (near_sent, grad_shift))
        grad_cond = to_low(smooth_gate_slope(condition) * jnp.sum(cond_came, 0))
        time_parts = contract(square_zero, grad_cond, 0, 0).reshape(devices, cols * all_images)

        mixed = jnp.concatenate(
            [
                time_parts,
                bias_parts,
                grad_patch.reshape(devices, cols * PIN),
                grad_final.reshape(devices, cols * PIN),
            ],
            1,
        )
        both_parts = after(both_parts[:both_half], mixed) + wide(from_both)
        both_half = both_half // 2
        both_sent = to_low(both_parts[both_half:])
        both_parts = both_parts[:both_half] + wide(swap(both_sent, dp_bits[-3]))
        if len(far_bits) > 1:
            near_came = swap(after(near_sent, both_parts), far_bits[-2])
        grad_table = contract(after(grad_cond, mixed), onehot, 1, 0)
        grad_time_two = contract(after(grad_cond, mixed), hid_time, 1, 1)
        mixed = after(exchange(mixed), (both_sent, grad_table, grad_time_two))
        mixed = jnp.sum(mixed, 0)
        time_came, mixed = (mixed[: cols * all_images], mixed[cols * all_images :])
        grad_bias = mixed[:bias_share]
        grad_patch = mixed[bias_share : bias_share + cols * PIN].reshape(cols, PIN)
        grad_final = mixed[bias_share + cols * PIN :].reshape(cols, PIN)
        pre_time = lax.dynamic_slice(pre_time_all, (me * cols, 0), (cols, all_images))
        grad_pre = to_low(smooth_gate_slope(pre_time) * time_came.reshape(cols, all_images))
        time_sums = jnp.sum(wide(grad_pre), 1)
        cond_sums = jnp.sum(wide(after(grad_cond, mixed)), 1)
        mod_sums = jnp.sum(wide(after(grad_mod, mixed)), 0)
        if len(far_bits) > 1:
            near = near_kept + wide(after(near_came, grad_pre))
        near = fold_second(near, far_bits[:-2][::-1])
        grad_expand, grad_reduce = (near[0], near[1])
        both_parts = fold_rows(both_parts, dp_bits[:-3][::-1])
        grad_proj = both_parts[per * unit :]
        grad_time_one = contract(grad_pre, freq_in, 1, 0)

        grad_attend = jnp.zeros((per, unit, D), jnp.float32)
        for turn in range(per):
            piece = lax.ppermute(
                both_parts[turn * unit : (turn + 1) * unit],
                AXES,
                [(int(unit_target[turn, owner]), owner) for owner in range(devices)],
            )
            local = after(jnp.asarray(unit_send[turn])[me], both_sent) == jnp.arange(per)
            grad_attend = jnp.where(local[:, None, None], piece[None], grad_attend)
        grad_attend = grad_attend.reshape(per * unit, D)

        grad_embed = jnp.concatenate([grad_patch, grad_time_one], 1)
        grad_square = jnp.stack([grad_time_two, grad_proj], 1)
        squares = sum(
            jnp.sum(piece * piece)
            for piece in (
                grad_patch,
                grad_time_one,
                grad_time_two,
                grad_proj,
                grad_table,
                grad_shift,
                grad_attend,
                grad_expand,
                grad_reduce,
                grad_final,
                grad_bias,
                time_sums,
                cond_sums,
                mod_sums,
            )
        )
        late = jnp.zeros((devices * bias_share,), jnp.float32)
        for sums, first in ((time_sums, D), (cond_sums, 2 * D), (mod_sums, 3 * D)):
            late = lax.dynamic_update_slice(late, sums, (first + me * sums.shape[0],))
        late = late.reshape(devices, bias_share)
        numbers = jnp.stack([loss_local, count_local, squares])
        late = jnp.concatenate([late, jnp.broadcast_to(numbers[None], (devices, 3))], 1)
        late = jnp.sum(exchange(late), 0)
        loss_total, value_count, squared = [late[bias_share + number] for number in range(3)]
        grad_norm = jnp.sqrt(squared)
        factor = LIMIT / jnp.maximum(grad_norm, LIMIT)
        grad_bias = grad_bias + late[:bias_share]

        shards = (
            grad_embed.T,
            jnp.transpose(grad_square, (1, 2, 0)),
            grad_table.T,
            grad_shift.T,
            grad_attend.T,
            grad_expand.T,
            grad_reduce,
            grad_final,
            grad_bias,
        )
        results = [
            adam_step(params_in[number], firsts[number], seconds[number], shards[number], factor)
            for number in range(9)
        ]
        fresh = [results[number][part] for part in range(3) for number in range(9)]
        return tuple([loss_total, value_count, grad_norm] + fresh)

    return on_device


def adam_step(weight, moment, second, gradient, factor):
    clipped = gradient * factor
    moment = BETA_ONE * moment + (1.0 - BETA_ONE) * clipped
    second = BETA_TWO * second + (1.0 - BETA_TWO) * clipped * clipped
    fixed_one = moment / (1.0 - BETA_ONE**STEP)
    fixed_two = second / (1.0 - BETA_TWO**STEP)
    weight = weight - RATE * (fixed_one / (jnp.sqrt(fixed_two) + EPSILON) + DECAY * weight)
    return (weight, moment, second)


def solution(mesh):
    both = ("dp", "seq")
    state = (
        P(None, both),
        P(None, None, both),
        P(None, both),
        P(None, both),
        P(None, both),
        P(None, both),
        P(both, None),
        P(both, None),
        P(both),
    )
    batch = (
        P(None, "dp", "seq", None),
        P(None, "dp", "seq", None),
        P(None, "dp"),
        P(None, "dp"),
        P(None, "dp"),
        P(None, "dp"),
        P(None, "dp", "seq", None, None),
    )
    return jax.shard_map(
        make_step(mesh),
        mesh=mesh,
        in_specs=batch + state * 3,
        out_specs=(P(), P(), P()) + state * 3,
        check_vma=False,
    )
```
